128 devices in a mesh: grp: 16 (over z_hi, x, core), blk: 8 (over y, z_lo).
Axes of the slice: x: 4, y: 4, z: 4 (z_hi: 2, z_lo: 2; z = z_hi * 2 + z_lo), core: 2. Of those that a mesh axis runs over, the one named last changes fastest.
Arguments:
- queries: bfloat16 [32768, 2048], P(('grp', 'blk')), may hold values from -8 to 8
- keys: bfloat16 [32768, 2048], P(('grp', 'blk')), may hold values from -8 to 8
- values: bfloat16 [32768, 2048], P(('grp', 'blk')), may hold values from -6 to 6
- cluster_ids: int32 [32768], P(('grp', 'blk')), may hold values from 0 to 63, as said below
- positions: int32 [32768], P(('grp', 'blk')), may hold values from 0 to 32767, each once
Outputs:
- attended: bfloat16 [32768, 2048], P(('grp', 'blk'))
The draws below stay inside these ranges and needn't reach their ends.
Inputs may be any that keep to these rules, and one draw needn't show every extreme that they name: `cluster_ids`: group g holds clusters g * 4 to g * 4 + 3. The 256 tokens of one device lie in the clusters of one group at most 32 times; for each index along blk, one group drawn from the seed receives exactly 32 tokens from every device with that index.
All inputs are finite; a program needn't handle non-finite values.
Results may differ from the reference program's by a relative error of at most 0.007.
Values may be sent and summed in bfloat16 or wider, within the bound.
No kernel may reach another device: no remote copies, remote signals or barrier semaphores. Data moves between devices by JAX's collectives and lax.ppermute only.
A program may use at most 192 MiB of HBM per device.

```python
import jax
import jax.numpy as jnp
from jax import lax

HEAD_DIM = 128
D = 2048
TOK_DEV = 256
CL_GRP = 4
CLUSTERS = 64
CAP = 32
TOKENS = 32768
N_GRP = 16
N_BLK = 8


def draw_cluster_ids(key, part):
    key = jax.random.fold_in(key, 11)
    key_full, key_perm, key_rows, key_local = jax.random.split(key, 4)
    device_count = N_GRP * N_BLK
    slot_count = N_GRP * CAP
    full_group = jax.random.randint(key_full, (N_BLK,), 0, N_GRP)

    def one_device(device):
        ranks = jax.random.permutation(jax.random.fold_in(key_perm, device), slot_count)
        owners = jnp.arange(slot_count, dtype=jnp.int32) // CAP
        priority = jnp.where(owners == full_group[device % N_BLK], -1, ranks)
        chosen = jnp.argsort(priority, stable=True)[:TOK_DEV]
        chosen = jax.random.permutation(jax.random.fold_in(key_rows, device), chosen)
        return (chosen // CAP).astype(jnp.int32)
    groups = jax.vmap(one_device)(jnp.arange(device_count, dtype=jnp.int32)).reshape(-1)
    local = jax.random.randint(key_local, (TOKENS,), 0, CL_GRP)
    return (groups * CL_GRP + local).astype(jnp.int32)


def draw_keys(key, part):
    key = jax.random.fold_in(key, 21)
    drawn = jnp.clip(jax.random.normal(key, (TOKENS, D), jnp.float32), -6.0, 6.0)
    return drawn.astype(jnp.bfloat16)


def draw_queries(key, part):
    key = jax.random.fold_in(key, 22)
    drawn = jnp.clip(jax.random.normal(key, (TOKENS, D), jnp.float32), -6.0, 6.0)
    return drawn.astype(jnp.bfloat16)


def levels(stream_key, extent, cuts, smallest, top_value):
    loudness = 1.0
    for dim, shards_of in cuts:
        steps = jax.random.uniform(jax.random.fold_in(jax.random.fold_in(stream_key, 6), dim), (shards_of,), jnp.float32, smallest / len(cuts), top_value / len(cuts))
        loudness = loudness * jnp.repeat(jnp.exp(steps), extent[dim] // shards_of).reshape((-1,) + (1,) * (len(extent) - 1 - dim))
    return loudness


def gaussian(rng, shape, deviation, reach, cuts=(), kind=jnp.bfloat16):
    values = jax.random.normal(rng, shape, jnp.float32) * deviation
    if len(cuts) > 0:
        values = levels(rng, shape, cuts, -0.22, 0.18) * values
    return jnp.clip(values, min=-reach, max=reach).astype(kind)


def setup_inputs(seed: int = 0) -> dict:
    arg_keys = jax.random.split(jax.random.key(seed), 6)
    queries = draw_queries(jax.random.fold_in(arg_keys[5], 71), 0)
    keys = draw_keys(jax.random.fold_in(arg_keys[5], 71), 0)
    values = gaussian(arg_keys[2], (TOKENS, D), 1.0, 6.0, ((0, 128),))
    cluster_ids = draw_cluster_ids(jax.random.fold_in(arg_keys[5], 71), 0)
    positions = jax.random.permutation(arg_keys[4], TOKENS).astype(jnp.int32)
    return dict(queries=queries, keys=keys, values=values, cluster_ids=cluster_ids, positions=positions)


def absorb(state, query_heads, query_cluster, query_place, key_heads, value_heads, key_cluster, key_place):
    row_max, totals, summed = state
    scores = jnp.einsum("qhd,khd->hqk", query_heads.astype(jnp.float32), key_heads.astype(jnp.float32)) * (HEAD_DIM ** -0.5)
    visible = (key_cluster[None, :] == query_cluster[:, None]) & (key_place[None, :] <= query_place[:, None])
    masked = jnp.where(visible[None], scores, -1e30)
    fresh = jnp.maximum(row_max, jnp.max(masked, axis=2))
    weight = jnp.where(visible[None], jnp.exp(scores - fresh[:, :, None]), 0.0)
    rescale = jnp.exp(row_max - fresh)
    totals = totals * rescale + jnp.sum(weight, axis=2)
    rounded = lax.optimization_barrier(weight.astype(jnp.bfloat16)).astype(jnp.float32)
    summed = summed * rescale[:, :, None] + jnp.einsum("hqk,khd->hqd", rounded, value_heads.astype(jnp.float32))
    return (fresh, totals, summed)


def reference(queries, keys, values, cluster_ids, positions):
    token_total = queries.shape[0]
    width = queries.shape[1]
    heads = width // HEAD_DIM
    rows = 512
    block_count = -(-token_total // rows)
    padded = block_count * rows
    extra = padded - token_total
    order = jnp.argsort(cluster_ids * token_total + positions).astype(jnp.int32)
    sorted_cluster = cluster_ids[order]
    counts = jax.ops.segment_sum(jnp.ones_like(cluster_ids), cluster_ids, num_segments=CLUSTERS)
    offsets = (jnp.cumsum(counts) - counts).astype(jnp.int32)
    first_row = offsets[sorted_cluster]

    def extend(array):
        return jnp.concatenate([array[order], jnp.zeros((extra, width), array.dtype)], axis=0).reshape(padded, heads, HEAD_DIM)

    shaped_q = extend(queries)
    shaped_k = extend(keys)
    shaped_v = extend(values)
    cluster_pad = jnp.concatenate([sorted_cluster, jnp.full((extra,), -1, jnp.int32)])
    place_pad = jnp.concatenate([positions[order], jnp.zeros((extra,), jnp.int32)])
    first_pad = jnp.concatenate([first_row, jnp.full((extra,), token_total, jnp.int32)])

    def one_block(number):
        start = number * rows
        query_heads = lax.dynamic_slice_in_dim(shaped_q, start, rows, 0)
        query_cluster = lax.dynamic_slice_in_dim(cluster_pad, start, rows, 0)
        query_place = lax.dynamic_slice_in_dim(place_pad, start, rows, 0)
        begin = (first_pad[start] // rows).astype(jnp.int32)
        initial = (jnp.full((heads, rows), -1e30, jnp.float32), jnp.zeros((heads, rows), jnp.float32), jnp.zeros((heads, rows, HEAD_DIM), jnp.float32))

        def absorb_block(key_block, state):
            offset = key_block * rows
            return absorb(state, query_heads, query_cluster, query_place,
                          lax.dynamic_slice_in_dim(shaped_k, offset, rows, 0),
                          lax.dynamic_slice_in_dim(shaped_v, offset, rows, 0),
                          lax.dynamic_slice_in_dim(cluster_pad, offset, rows, 0),
                          lax.dynamic_slice_in_dim(place_pad, offset, rows, 0))

        row_max, totals, summed = lax.fori_loop(begin, number + 1, absorb_block, initial)
        result = summed / totals[:, :, None]
        return result.transpose(1, 0, 2).reshape(rows, width).astype(jnp.bfloat16)

    blocks = lax.map(one_block, jnp.arange(block_count, dtype=jnp.int32))
    flat = blocks.reshape(padded, width)[:token_total]
    return jnp.zeros_like(queries).at[order].set(flat)
```

```python
import functools

import jax
import jax.numpy as jnp
from jax import lax
from jax.experimental import pallas as pl
from jax.experimental.pallas import tpu as pltpu
from jax.sharding import PartitionSpec as P

HEAD_DIM = 128
CL_GRP = 4
CL_SET = 2 * CL_GRP
RUN = 48
CODES = CL_SET * RUN
BLK = 256
F32 = jnp.float32
BF16 = jnp.bfloat16
HIDDEN = -1e30


def chunk_rows(slots):
    return -(-(3 * slots + 8) // 16) * 16


def iota(shape, dim):
    return lax.broadcasted_iota(jnp.int32, shape, dim).astype(F32)


def column(row):
    return jnp.transpose(jnp.broadcast_to(row, (128, row.shape[1])))


def nt_dot(a, b):
    return lax.dot_general(a, b, (((1,), (1,)), ((), ())), preferred_element_type=F32)


def dot(a, b):
    return jnp.dot(a, b, preferred_element_type=F32)


def pack_kernel(slots, sets, parity_ref, cid_ref, pos_ref, q_ref, k_ref, v_ref, out_ref, slot_ref, place, meta):
    tokens = cid_ref.shape[1]

    @pl.when(pl.program_id(0) == 0)
    def _():
        cid = cid_ref[...]
        pos = pos_ref[...]
        own = jnp.bitwise_and(cid, CL_SET - 1)
        group = (cid - own).astype(F32) * (1.0 / CL_SET)
        key = cid.astype(F32) * tokens + iota((1, tokens), 1)
        keys = column(key)
        keys = jnp.concatenate([keys] * (tokens // 128), axis=1)
        below = keys < key
        rank = jnp.sum(jnp.where(below & (keys >= group * (CL_SET * tokens)), 1.0, 0.0), axis=0, keepdims=True)
        within = jnp.sum(jnp.where(below & (keys >= cid.astype(F32) * tokens), 1.0, 0.0), axis=0, keepdims=True)
        fits = rank < slots
        slot = jnp.where(fits, group * slots + rank, -1.0)
        slot_ref[...] = slot
        place[...] = jnp.where(iota((sets * slots, tokens), 0) == slot, 1.0, 0.0).astype(BF16)
        lane = jnp.where(fits, group * 128 + rank + 64 * parity_ref[0, 0].astype(F32), -1.0)
        spread = jnp.where(iota((sets * 128, tokens), 0) == lane, 1.0, 0.0).astype(BF16)
        low = jnp.bitwise_and(pos, 255)
        high = jnp.right_shift(pos, 8) + 1
        row = lax.broadcasted_iota(jnp.int32, (16, tokens), 0)
        facts = jnp.where(
            row == 0,
            high.astype(F32),
            jnp.where(row == 1, low.astype(F32), jnp.where(row == 2, own.astype(F32) + 1.0, jnp.where(row == 3, within, 0.0))),
        ).astype(BF16)
        meta[...] = nt_dot(facts, spread)

    x = jnp.concatenate([q_ref[...], k_ref[...], v_ref[...]], axis=1)
    y = dot(place[...], x)
    gap = out_ref.shape[2] - 3 * slots - 8
    for s in range(sets):
        part = y[s * slots : (s + 1) * slots]
        pieces = [part[:, :128], part[:, 128:256], part[:, 256:]]
        if gap:
            pieces.append(jnp.zeros((gap, 128), F32))
        pieces.append(meta[0:8, s * 128 : (s + 1) * 128])
        out_ref[s, 0] = jnp.concatenate(pieces, axis=0).astype(BF16)


def attend_kernel(slots, x_ref, o_ref, xs, ps, os, kp, code, high, low, tab_v, tab, sem):
    sources, rows, _ = x_ref.shape
    blocks = sources // 4
    total_rows = xs.shape[0]

    facts = x_ref[:, rows - 16 : rows, :].astype(F32)
    high[...] = facts[:, 8, :]
    low[...] = facts[:, 9, :]
    own = facts[:, 10, :]
    within = facts[:, 11, :]
    lane = iota((sources, 128), 1)
    counts = jnp.zeros((sources, 128), F32)
    for c in range(CL_SET):
        n = jnp.sum(jnp.where(own == c + 1, 1.0, 0.0), axis=1, keepdims=True)
        counts = counts + jnp.where(lane == c, n, 0.0)
    counts16 = counts.astype(BF16)
    r = lax.broadcasted_iota(jnp.int32, (sources, sources), 0)
    s = lax.broadcasted_iota(jnp.int32, (sources, sources), 1)

    def picked(mask):
        return dot(jnp.where(mask, 1.0, 0.0).astype(BF16), counts16)

    first = jnp.bitwise_and(r, -4)
    before = picked(s < r)
    before_block = picked(s < first)
    after_block = picked(s < first + 4)
    total = picked(s >= 0)
    nblk = jnp.floor((total + (BLK - 1)) * (1.0 / BLK))
    start_blk = dot(nblk.astype(BF16), jnp.where((r < s) & (r < CL_SET), 1.0, 0.0).astype(BF16))
    base = start_blk * BLK
    aligned = base + jnp.floor(before_block * (1.0 / 16)) * 16
    shift = base + before - aligned
    passes = jnp.where(lane < CL_SET, jnp.floor((base + after_block - aligned + (RUN - 1)) * (1.0 / RUN)), 0.0)
    passes = jnp.max(passes, axis=1, keepdims=True)
    place = within
    for c in range(CL_SET):
        place = place + jnp.where(own == c + 1, shift[:, c : c + 1], 0.0)
    step = jnp.floor(place * (1.0 / RUN) + (0.5 / RUN))
    code[...] = jnp.where(own > 0.0, step * CODES + (own - 1.0) * RUN + (place - step * RUN) + 1.0, 0.0)
    last = start_blk + nblk
    used = jnp.max(jnp.where(lane < CL_SET, last, 0.0), axis=1, keepdims=True)
    table = jnp.where(lane < CL_SET, aligned, 0.0)
    table = jnp.where(lane == 8, passes, table)
    table = jnp.where(lane == 9, used, table)
    spin = jnp.zeros((sources, 128), F32)
    for c in range(CL_SET):
        spin = spin + jnp.where(lane == 16 + c, start_blk[:, c : c + 1], 0.0) + jnp.where(lane == 24 + c, nblk[:, c : c + 1], 0.0)
    tab_v[...] = (table + spin).astype(jnp.int32)
    copy = pltpu.make_async_copy(tab_v, tab, sem)
    copy.start()
    os[...] = jnp.zeros(os.shape, BF16)
    copy.wait()
    used_blocks = tab[0, 9]

    def clear(i, _):
        at = pl.ds(pl.multiple_of(i * BLK, BLK), BLK)
        xs[at, :] = jnp.zeros((BLK, xs.shape[1]), BF16)
        ps[at, :] = jnp.zeros((BLK, 128), F32)
        return 0

    lax.fori_loop(0, jnp.minimum(used_blocks + 2, total_rows // BLK), clear, 0)

    def joined(ref, b):
        return jnp.concatenate(
            [
                ref[pl.ds(4 * b, 1), :] + ref[pl.ds(4 * b + 1, 1), :],
                ref[pl.ds(4 * b + 2, 1), :] + ref[pl.ds(4 * b + 3, 1), :],
            ],
            axis=1,
        )

    which = lax.broadcasted_iota(jnp.int32, (128, 256), 0)
    code_rows = iota((CODES, 256), 0)

    def compact(b, _):
        x4 = x_ref[pl.ds(4 * b, 4)].astype(F32)
        xcat = jnp.concatenate([x4[:, i * slots : i * slots + 64].reshape(256, 128) for i in range(3)], axis=1).astype(BF16)
        row = joined(code, b)
        where_at = jnp.where(which == 0, joined(high, b), jnp.where(which == 1, joined(low, b), 0.0)).astype(BF16)

        def one(p, _):
            select = jnp.where(code_rows == row - (p * CODES + 1).astype(F32), 1.0, 0.0).astype(BF16)
            y = dot(select, xcat).astype(BF16)
            z = nt_dot(select, where_at)
            for c in range(CL_SET):
                at = pl.ds(pl.multiple_of(tab[4 * b, c] + p * RUN, 16), RUN)
                xs[at, :] = xs[at, :] + y[c * RUN : (c + 1) * RUN]
                ps[at, :] = ps[at, :] + z[c * RUN : (c + 1) * RUN]
            return 0

        lax.fori_loop(0, tab[4 * b, 8], one, 0)
        return 0

    lax.fori_loop(0, blocks, compact, 0)

    def key_places(i, _):
        t = jnp.transpose(ps[pl.ds(pl.multiple_of(i * BLK, BLK), BLK), :])
        k = t[0:1] * 256.0 + t[1:2]
        kp[pl.ds(i, 1), :] = jnp.where(k > 0.0, k, 1e9)
        return 0

    lax.fori_loop(0, used_blocks, key_places, 0)

    def cluster(c, _):
        begin = tab[0, 16 + c]
        count = tab[0, 24 + c]

        def queries(i, _):
            at = pl.ds(pl.multiple_of((begin + i) * BLK, BLK), BLK)
            q = xs[at, 0:128]
            w = ps[at, 0:2]
            qp = w[:, 0:1] * 256.0 + w[:, 1:2]

            def keys(j, carried):
                top, total, summed = carried
                kat = pl.ds(pl.multiple_of((begin + j) * BLK, BLK), BLK)
                scores = nt_dot(q, xs[kat, 128:256]) * HEAD_DIM ** (-0.5)
                scores = jnp.where(kp[pl.ds(begin + j, 1), :] <= qp, scores, HIDDEN)
                fresh = jnp.maximum(top, jnp.max(scores, axis=1, keepdims=True))
                weight = jnp.exp(scores - fresh)
                rescale = jnp.exp(top - fresh)
                total = total * rescale + jnp.sum(weight, axis=1, keepdims=True)
                summed = summed * rescale + dot(weight.astype(BF16), xs[kat, 256:384])
                return fresh, total, summed

            init = (jnp.full((BLK, 1), HIDDEN, F32), jnp.zeros((BLK, 1), F32), jnp.zeros((BLK, 128), F32))
            _, total, summed = lax.fori_loop(0, count, keys, init)
            os[at, :] = (summed / total).astype(BF16)
            return 0

        lax.fori_loop(0, count, queries, 0)
        return 0

    lax.fori_loop(0, CL_SET, cluster, 0)

    code_lanes = iota((256, CODES), 1)

    def spread(b, _):
        col = column(joined(code, b))
        col = jnp.concatenate([col] * (CODES // 128), axis=1)

        def one(p, acc):
            cat = jnp.concatenate(
                [os[pl.ds(pl.multiple_of(tab[4 * b, c] + p * RUN, 16), RUN), :] for c in range(CL_SET)], axis=0
            )
            select = jnp.where(code_lanes == col - (p * CODES + 1).astype(F32), 1.0, 0.0).astype(BF16)
            return acc + dot(select, cat)

        acc = lax.fori_loop(0, tab[4 * b, 8], one, jnp.zeros((256, 128), F32))
        o_ref[pl.ds(4 * b, 4)] = acc.reshape(4, 64, 128)[:, :slots].astype(BF16)
        return 0

    lax.fori_loop(0, blocks, spread, 0)


def unpack_kernel(slots, slot_ref, r_ref, out_ref, select):
    sets, heads = r_ref.shape[0], r_ref.shape[1]

    @pl.when(pl.program_id(0) == 0)
    def _():
        col = column(slot_ref[...])
        col = jnp.concatenate([col] * (-(-sets * slots // 128)), axis=1)[:, : sets * slots]
        select[...] = jnp.where(iota(select.shape, 1) == col, 1.0, 0.0).astype(BF16)

    for h in range(heads):
        x = r_ref[:, h].astype(F32).reshape(sets * slots, 128).astype(BF16)
        out_ref[:, h * 128 : (h + 1) * 128] = dot(select[...], x).astype(BF16)


def attention(slots, queries, keys, values, cid_row, pos_row, parity):
    tokens, width = queries.shape
    heads = width // HEAD_DIM
    sources = lax.axis_size("grp") * lax.axis_size("blk")
    sets = sources // heads
    rows = chunk_rows(slots)
    vmem = pltpu.CompilerParams(vmem_limit_bytes=56 * 2**20)
    whole = pl.BlockSpec(memory_space=pltpu.VMEM)
    one = pl.BlockSpec((tokens, HEAD_DIM), lambda h: (0, h))
    line = pl.BlockSpec((1, tokens), lambda h: (0, 0))
    sent, slot = pl.pallas_call(
        functools.partial(pack_kernel, slots, sets),
        grid=(heads,),
        in_specs=[pl.BlockSpec(memory_space=pltpu.SMEM), line, line, one, one, one],
        out_specs=[pl.BlockSpec((sets, 1, rows, 128), lambda h: (0, h, 0, 0)), line],
        out_shape=[
            jax.ShapeDtypeStruct((sets, heads, rows, 128), BF16),
            jax.ShapeDtypeStruct((1, tokens), F32),
        ],
        scratch_shapes=[pltpu.VMEM((sets * slots, tokens), BF16), pltpu.VMEM((16, sets * 128), F32)],
        compiler_params=vmem,
        name="pack",
    )(parity, cid_row, pos_row, queries, keys, values)
    got = lax.all_to_all(sent.reshape(sources, rows, 128), ("grp", "blk"), split_axis=0, concat_axis=0, tiled=True)
    total_rows = sources * slots + (CL_SET + 2) * BLK
    done = pl.pallas_call(
        functools.partial(attend_kernel, slots),
        in_specs=[whole],
        out_specs=whole,
        out_shape=jax.ShapeDtypeStruct((sources, slots, 128), BF16),
        scratch_shapes=[
            pltpu.VMEM((total_rows, 3 * HEAD_DIM), BF16),
            pltpu.VMEM((total_rows, 128), F32),
            pltpu.VMEM((total_rows, HEAD_DIM), BF16),
            pltpu.VMEM((total_rows // BLK, BLK), F32),
            pltpu.VMEM((sources, 128), F32),
            pltpu.VMEM((sources, 128), F32),
            pltpu.VMEM((sources, 128), F32),
            pltpu.VMEM((sources, 128), jnp.int32),
            pltpu.SMEM((sources, 128), jnp.int32),
            pltpu.SemaphoreType.DMA,
        ],
        compiler_params=vmem,
        name="attend",
    )(got)
    back = lax.all_to_all(done, ("grp", "blk"), split_axis=0, concat_axis=0, tiled=True)
    per = 2
    return pl.pallas_call(
        functools.partial(unpack_kernel, slots),
        grid=(heads // per,),
        in_specs=[line, pl.BlockSpec((sets, per, slots, 128), lambda h: (0, h, 0, 0))],
        out_specs=pl.BlockSpec((tokens, per * HEAD_DIM), lambda h: (0, h)),
        out_shape=jax.ShapeDtypeStruct((tokens, width), BF16),
        scratch_shapes=[pltpu.VMEM((tokens, sets * slots), BF16)],
        compiler_params=vmem,
        name="unpack",
    )(slot, back.reshape(sets, heads, slots, 128))


def local(queries, keys, values, cluster_ids, positions):
    cid_row = cluster_ids.reshape(1, -1)
    pos_row = positions.reshape(1, -1)
    me = lax.axis_index("grp") * lax.axis_size("blk") + lax.axis_index("blk")
    parity = (me % 2).astype(jnp.int32).reshape(1, 1)
    return attention(2 * 32, queries, keys, values, cid_row, pos_row, parity)


def solution(mesh):
    placed = (
        P(("grp", "blk"), None),
        P(("grp", "blk"), None),
        P(("grp", "blk"), None),
        P(("grp", "blk")),
        P(("grp", "blk")),
    )
    return jax.shard_map(
        local, mesh=mesh, in_specs=placed, out_specs=P(("grp", "blk"), None), check_vma=False
    )
```

```python
import functools

import jax
import jax.numpy as jnp
from jax import lax
from jax.experimental import pallas as pl
from jax.experimental.pallas import tpu as pltpu
from jax.sharding import PartitionSpec as P

HEAD_DIM = 128
CL_GRP = 4
CL_SET = 2 * CL_GRP
RUN = 48
CODES = CL_SET * RUN
BLK = 128
FIXED = (4, 5, 6)
UNROLL = 8
PACK = 8
UNPACK = 8
F32 = jnp.float32
BF16 = jnp.bfloat16
HIDDEN = -1e30


def chunk_rows(slots):
    return -(-(3 * slots + 8) // 16) * 16


def iota(shape, dim):
    return lax.broadcasted_iota(jnp.int32, shape, dim).astype(F32)


def column(row):
    return jnp.transpose(jnp.broadcast_to(row, (128, row.shape[1])))


def nt_dot(a, b):
    return lax.dot_general(a, b, (((1,), (1,)), ((), ())), preferred_element_type=F32)


def dot(a, b):
    return jnp.dot(a, b, preferred_element_type=F32)


def pack_kernel(slots, sets, parity_ref, cid_ref, pos_ref, q_ref, k_ref, v_ref, out_ref, slot_ref, place, meta):
    tokens = cid_ref.shape[1]

    @pl.when(pl.program_id(0) == 0)
    def _():
        cid = cid_ref[...]
        pos = pos_ref[...]
        own = jnp.bitwise_and(cid, CL_SET - 1)
        group = (cid - own).astype(F32) * (1.0 / CL_SET)
        key = cid.astype(F32) * tokens + iota((1, tokens), 1)
        keys = column(key)
        keys = jnp.concatenate([keys] * (tokens // 128), axis=1)
        below = keys < key
        rank = jnp.sum(jnp.where(below & (keys >= group * (CL_SET * tokens)), 1.0, 0.0), axis=0, keepdims=True)
        within = jnp.sum(jnp.where(below & (keys >= cid.astype(F32) * tokens), 1.0, 0.0), axis=0, keepdims=True)
        fits = rank < slots
        slot = jnp.where(fits, group * slots + rank, -1.0)
        slot_ref[...] = slot
        place[...] = jnp.where(iota((sets * slots, tokens), 0) == slot, 1.0, 0.0).astype(BF16)
        lane = jnp.where(fits, group * 128 + rank + 64 * parity_ref[0, 0].astype(F32), -1.0)
        spread = jnp.where(iota((sets * 128, tokens), 0) == lane, 1.0, 0.0).astype(BF16)
        low = jnp.bitwise_and(pos, 255)
        high = jnp.right_shift(pos, 8) + 1
        row = lax.broadcasted_iota(jnp.int32, (16, tokens), 0)
        facts = jnp.where(
            row == 0,
            high.astype(F32),
            jnp.where(row == 1, low.astype(F32), jnp.where(row == 2, own.astype(F32) + 1.0, jnp.where(row == 3, within, 0.0))),
        ).astype(BF16)
        meta[...] = nt_dot(facts, spread)

    gap = out_ref.shape[2] - 3 * slots - 8
    for h in range(out_ref.shape[1]):
        at = slice(h * HEAD_DIM, (h + 1) * HEAD_DIM)
        y = dot(place[...], jnp.concatenate([q_ref[:, at], k_ref[:, at], v_ref[:, at]], axis=1))
        for s in range(sets):
            part = y[s * slots : (s + 1) * slots]
            pieces = [part[:, :128], part[:, 128:256], part[:, 256:]]
            if gap:
                pieces.append(jnp.zeros((gap, 128), F32))
            pieces.append(meta[0:8, s * 128 : (s + 1) * 128])
            out_ref[s, h] = jnp.concatenate(pieces, axis=0).astype(BF16)


def attend_kernel(slots, x_ref, o_ref, xs, os, code, high, low, tab_v, tab, sem):
    sources, rows, _ = x_ref.shape
    blocks = sources // 4
    total_rows = xs.shape[0]

    facts = x_ref[:, rows - 16 : rows, :].astype(F32)
    high[...] = facts[:, 8, :]
    low[...] = facts[:, 9, :]
    own = facts[:, 10, :]
    within = facts[:, 11, :]
    lane = iota((sources, 128), 1)
    counts = jnp.zeros((sources, 128), F32)
    for c in range(CL_SET):
        n = jnp.sum(jnp.where(own == c + 1, 1.0, 0.0), axis=1, keepdims=True)
        counts = counts + jnp.where(lane == c, n, 0.0)
    counts16 = counts.astype(BF16)
    r = lax.broadcasted_iota(jnp.int32, (sources, sources), 0)
    s = lax.broadcasted_iota(jnp.int32, (sources, sources), 1)

    def picked(mask):
        return dot(jnp.where(mask, 1.0, 0.0).astype(BF16), counts16)

    first = jnp.bitwise_and(r, -4)
    before = picked(s < r)
    before_block = picked(s < first)
    after_block = picked(s < first + 4)
    total = picked(s >= 0)
    nblk = jnp.floor((total + (BLK - 1)) * (1.0 / BLK))
    start_blk = dot(nblk.astype(BF16), jnp.where((r < s) & (r < CL_SET), 1.0, 0.0).astype(BF16))
    base = start_blk * BLK
    aligned = base + jnp.floor(before_block * (1.0 / 16)) * 16
    shift = base + before - aligned
    passes = jnp.where(lane < CL_SET, jnp.floor((base + after_block - aligned + (RUN - 1)) * (1.0 / RUN)), 0.0)
    passes = jnp.max(passes, axis=1, keepdims=True)
    place = within
    for c in range(CL_SET):
        place = place + jnp.where(own == c + 1, shift[:, c : c + 1], 0.0)
    step = jnp.floor(place * (1.0 / RUN) + (0.5 / RUN))
    code[...] = jnp.where(own > 0.0, step * CODES + (own - 1.0) * RUN + (place - step * RUN) + 1.0, 0.0)
    last = start_blk + nblk
    used = jnp.max(jnp.where(lane < CL_SET, last, 0.0), axis=1, keepdims=True)
    table = jnp.where(lane < CL_SET, aligned, 0.0)
    table = jnp.where(lane == 8, passes, table)
    table = jnp.where(lane == 9, used, table)
    table = jnp.where(lane == 10, jnp.max(passes), table)
    spin = jnp.zeros((sources, 128), F32)
    for c in range(CL_SET):
        spin = spin + jnp.where(lane == 16 + c, start_blk[:, c : c + 1], 0.0) + jnp.where(lane == 24 + c, nblk[:, c : c + 1], 0.0)
    tab_v[...] = (table + spin).astype(jnp.int32)
    copy = pltpu.make_async_copy(tab_v, tab, sem)
    copy.start()
    os[...] = jnp.zeros(os.shape, BF16)
    copy.wait()
    used_blocks = tab[0, 9]

    def clear(i, _):
        at = pl.ds(pl.multiple_of(i * BLK, BLK), BLK)
        xs[at, :] = jnp.zeros((BLK, xs.shape[1]), BF16)
        return 0

    lax.fori_loop(0, jnp.minimum(used_blocks + 4, total_rows // BLK), clear, 0)

    def joined(ref, b):
        return jnp.concatenate(
            [
                ref[pl.ds(4 * b, 1), :] + ref[pl.ds(4 * b + 1, 1), :],
                ref[pl.ds(4 * b + 2, 1), :] + ref[pl.ds(4 * b + 3, 1), :],
            ],
            axis=1,
        )

    code_rows = iota((CODES, 256), 0)
    which = lax.broadcasted_iota(jnp.int32, (128, 256), 0)

    def compact(b, p):
        x4 = x_ref[pl.ds(4 * b, 4)].astype(F32)
        xcat = jnp.concatenate([x4[:, i * slots : i * slots + 64].reshape(256, 128) for i in range(3)], axis=1).astype(BF16)
        row = joined(code, b) - jnp.asarray(p * CODES + 1, F32)
        where_at = jnp.where(which == 0, joined(high, b) * 256.0, jnp.where(which == 1, joined(low, b), 0.0)).astype(BF16)
        select = jnp.where(code_rows == row, 1.0, 0.0).astype(BF16)
        y = jnp.concatenate([dot(select, xcat), nt_dot(select, where_at)], axis=1).astype(BF16)
        ats = [pl.ds(pl.multiple_of(tab[4 * b, c] + p * RUN, 16), RUN) for c in range(CL_SET)]
        new = [xs[at, :] + y[c * RUN : (c + 1) * RUN] for c, at in enumerate(ats)]
        for at, x in zip(ats, new):
            xs[at, :] = x

    def each_block(body):
        def some(i, _):
            for u in range(UNROLL):
                body(i * UNROLL + u, 0)
            return 0

        lax.fori_loop(0, blocks // UNROLL, some, 0)

        @pl.when(tab[0, 10] > 1)
        def _():
            def rest(b, _):
                def more(p, _):
                    body(b, p)
                    return 0

                return lax.fori_loop(1, tab[4 * b, 8], more, 0)

            lax.fori_loop(0, blocks, rest, 0)

    each_block(compact)

    scale = HEAD_DIM ** (-0.5) * 1.4426950408889634
    to_lanes = jnp.where(lax.broadcasted_iota(jnp.int32, (16, 128), 1) < 2, 1.0, 0.0).astype(BF16)
    to_all = jnp.where(lax.broadcasted_iota(jnp.int32, (128, 128), 0) < 2, 1.0, 0.0).astype(BF16)

    def key_places(at):
        kp = nt_dot(to_lanes, xs[at, 384:512])[0:1]
        return jnp.where(kp > 0.0, kp, 1e9)

    def hidden(scores, kp, qp):
        lanes = scores.shape[1] // 128
        return jnp.where(kp <= jnp.concatenate([qp] * lanes, axis=1), scores * scale, HIDDEN)

    def fixed(begin, count):
        kat = pl.ds(pl.multiple_of(begin * BLK, BLK), count * BLK)
        keys = xs[kat, 128:256]
        values = xs[kat, 256:384]
        kp = key_places(kat)
        for i in range(0, count, 2):
            wide = min(2, count - i)
            at = pl.ds(pl.multiple_of((begin + i) * BLK, BLK), wide * BLK)
            scores = hidden(nt_dot(xs[at, 0:128], keys), kp, dot(xs[at, 384:512], to_all))
            weight = jnp.exp2(scores - jnp.max(scores, axis=1, keepdims=True))
            total = jnp.sum(weight, axis=1, keepdims=True)
            os[at, :] = (dot(weight.astype(BF16), values) / total).astype(BF16)

    def general(begin, count):
        def queries(i, _):
            at = pl.ds(pl.multiple_of((begin + i) * BLK, BLK), BLK)
            q = xs[at, 0:128]
            qp = dot(xs[at, 384:512], to_all)

            def keys(j, carried):
                top, total, summed = carried
                kat = pl.ds(pl.multiple_of((begin + j) * BLK, BLK), BLK)
                scores = hidden(nt_dot(q, xs[kat, 128:256]), key_places(kat), qp)
                fresh = jnp.maximum(top, jnp.max(scores, axis=1, keepdims=True))
                weight = jnp.exp2(scores - fresh)
                rescale = jnp.exp2(top - fresh)
                total = total * rescale + jnp.sum(weight, axis=1, keepdims=True)
                summed = summed * rescale + dot(weight.astype(BF16), xs[kat, 256:384])
                return fresh, total, summed

            init = (jnp.full((BLK, 1), HIDDEN, F32), jnp.zeros((BLK, 1), F32), jnp.zeros((BLK, 128), F32))
            _, total, summed = lax.fori_loop(0, count, keys, init)
            os[at, :] = (summed / total).astype(BF16)
            return 0

        lax.fori_loop(0, count, queries, 0)

    def cluster(c, _):
        begin = tab[0, 16 + c]
        count = tab[0, 24 + c]
        for n in FIXED:
            pl.when(count == n)(functools.partial(fixed, begin, n))
        pl.when((count < FIXED[0]) | (count > FIXED[-1]))(functools.partial(general, begin, count))
        return 0

    lax.fori_loop(0, CL_SET, cluster, 0)

    code_lanes = iota((256, CODES), 1)

    def spread(b, p):
        col = column(joined(code, b) - jnp.asarray(p * CODES + 1, F32))
        col = jnp.concatenate([col] * (CODES // 128), axis=1)
        cat = jnp.concatenate(
            [os[pl.ds(pl.multiple_of(tab[4 * b, c] + p * RUN, 16), RUN), :] for c in range(CL_SET)], axis=0
        )
        select = jnp.where(code_lanes == col, 1.0, 0.0).astype(BF16)
        new = dot(select, cat).reshape(4, 64, 128)[:, :slots]
        at = pl.ds(4 * b, 4)
        if isinstance(p, int):
            o_ref[at] = new.astype(BF16)
        else:
            o_ref[at] = (o_ref[at].astype(F32) + new).astype(BF16)

    each_block(spread)


def attend_call(slots, got):
    sources = got.shape[0]
    whole = pl.BlockSpec(memory_space=pltpu.VMEM)
    total_rows = sources * slots + (CL_SET + 4) * BLK
    return pl.pallas_call(
        functools.partial(attend_kernel, slots),
        in_specs=[whole],
        out_specs=whole,
        out_shape=jax.ShapeDtypeStruct((sources, slots, 128), BF16),
        scratch_shapes=[
            pltpu.VMEM((total_rows, 4 * HEAD_DIM), BF16),
            pltpu.VMEM((total_rows, HEAD_DIM), BF16),
            pltpu.VMEM((sources, 128), F32),
            pltpu.VMEM((sources, 128), F32),
            pltpu.VMEM((sources, 128), F32),
            pltpu.VMEM((sources, 128), jnp.int32),
            pltpu.SMEM((sources, 128), jnp.int32),
            pltpu.SemaphoreType.DMA,
        ],
        compiler_params=pltpu.CompilerParams(vmem_limit_bytes=56 * 2**20),
        name="attend",
    )(got)


def unpack_kernel(slots, slot_ref, r_ref, out_ref, select):
    sets, heads = r_ref.shape[0], r_ref.shape[1]

    @pl.when(pl.program_id(0) == 0)
    def _():
        col = column(slot_ref[...])
        col = jnp.concatenate([col] * (-(-sets * slots // 128)), axis=1)[:, : sets * slots]
        select[...] = jnp.where(iota(select.shape, 1) == col, 1.0, 0.0).astype(BF16)

    for h in range(heads):
        x = r_ref[:, h].astype(F32).reshape(sets * slots, 128).astype(BF16)
        out_ref[:, h * 128 : (h + 1) * 128] = dot(select[...], x).astype(BF16)


def pack_call(slots, sets, parity, cid_row, pos_row, queries, keys, values):
    tokens, width = queries.shape
    heads = width // HEAD_DIM
    rows = chunk_rows(slots)
    some = pl.BlockSpec((tokens, PACK * HEAD_DIM), lambda h: (0, h))
    line = pl.BlockSpec((1, tokens), lambda h: (0, 0))
    return pl.pallas_call(
        functools.partial(pack_kernel, slots, sets),
        grid=(heads // PACK,),
        in_specs=[pl.BlockSpec(memory_space=pltpu.SMEM), line, line, some, some, some],
        out_specs=[pl.BlockSpec((sets, PACK, rows, 128), lambda h: (0, h, 0, 0)), line],
        out_shape=[
            jax.ShapeDtypeStruct((sets, heads, rows, 128), BF16),
            jax.ShapeDtypeStruct((1, tokens), F32),
        ],
        scratch_shapes=[pltpu.VMEM((sets * slots, tokens), BF16), pltpu.VMEM((16, sets * 128), F32)],
        compiler_params=pltpu.CompilerParams(vmem_limit_bytes=56 * 2**20),
        name="pack",
    )(parity, cid_row, pos_row, queries, keys, values)


def unpack_call(slots, slot, back):
    sets, heads = back.shape[:2]
    tokens = slot.shape[1]
    return pl.pallas_call(
        functools.partial(unpack_kernel, slots),
        grid=(heads // UNPACK,),
        in_specs=[
            pl.BlockSpec((1, tokens), lambda h: (0, 0)),
            pl.BlockSpec((sets, UNPACK, slots, 128), lambda h: (0, h, 0, 0)),
        ],
        out_specs=pl.BlockSpec((tokens, UNPACK * HEAD_DIM), lambda h: (0, h)),
        out_shape=jax.ShapeDtypeStruct((tokens, heads * HEAD_DIM), BF16),
        scratch_shapes=[pltpu.VMEM((tokens, sets * slots), BF16)],
        compiler_params=pltpu.CompilerParams(vmem_limit_bytes=56 * 2**20),
        name="unpack",
    )(slot, back)


def attention(slots, queries, keys, values, cid_row, pos_row, parity):
    heads = queries.shape[1] // HEAD_DIM
    sources = lax.axis_size("grp") * lax.axis_size("blk")
    sets = sources // heads
    sent, slot = pack_call(slots, sets, parity, cid_row, pos_row, queries, keys, values)
    got = lax.all_to_all(
        sent.reshape(sources, sent.shape[2], 128), ("grp", "blk"), split_axis=0, concat_axis=0, tiled=True
    )
    done = attend_call(slots, got)
    back = lax.all_to_all(done, ("grp", "blk"), split_axis=0, concat_axis=0, tiled=True)
    return unpack_call(slots, slot, back.reshape(sets, heads, slots, 128))


def local(queries, keys, values, cluster_ids, positions):
    cid_row = cluster_ids.reshape(1, -1)
    pos_row = positions.reshape(1, -1)
    me = lax.axis_index("grp") * lax.axis_size("blk") + lax.axis_index("blk")
    parity = (me % 2).astype(jnp.int32).reshape(1, 1)
    return attention(2 * 32, queries, keys, values, cid_row, pos_row, parity)


def solution(mesh):
    placed = (
        P(("grp", "blk"), None),
        P(("grp", "blk"), None),
        P(("grp", "blk"), None),
        P(("grp", "blk")),
        P(("grp", "blk")),
    )
    return jax.shard_map(
        local, mesh=mesh, in_specs=placed, out_specs=P(("grp", "blk"), None), check_vma=False
    )
```

```python
import functools

import jax
import jax.numpy as jnp
from jax import lax
from jax.experimental import pallas as pl
from jax.experimental.pallas import tpu as pltpu
from jax.sharding import PartitionSpec as P

HEAD_DIM = 128
CL_GRP = 4
CL_SET = 2 * CL_GRP
RUN = 48
CODES = CL_SET * RUN
BLK = 128
FIXED = (4, 5, 6)
UNROLL = 8
ALL = 64
FEW = 56
PACK = 8
UNPACK = 8
F32 = jnp.float32
BF16 = jnp.bfloat16
HIDDEN = -1e30


def chunk_rows(slots):
    return -(-(3 * slots + 8) // 16) * 16


def iota(shape, dim):
    return lax.broadcasted_iota(jnp.int32, shape, dim).astype(F32)


def column(row):
    return jnp.transpose(jnp.broadcast_to(row, (128, row.shape[1])))


def nt_dot(a, b):
    return lax.dot_general(a, b, (((1,), (1,)), ((), ())), preferred_element_type=F32)


def dot(a, b):
    return jnp.dot(a, b, preferred_element_type=F32)


def pack_kernel(slots, sets, parity_ref, cid_ref, pos_ref, q_ref, k_ref, v_ref, out_ref, slot_ref, place, meta):
    tokens = cid_ref.shape[1]

    @pl.when(pl.program_id(0) == 0)
    def _():
        cid = cid_ref[...]
        pos = pos_ref[...]
        own = jnp.bitwise_and(cid, CL_SET - 1)
        group = (cid - own).astype(F32) * (1.0 / CL_SET)
        key = cid.astype(F32) * tokens + iota((1, tokens), 1)
        keys = column(key)
        keys = jnp.concatenate([keys] * (tokens // 128), axis=1)
        below = keys < key
        rank = jnp.sum(jnp.where(below & (keys >= group * (CL_SET * tokens)), 1.0, 0.0), axis=0, keepdims=True)
        within = jnp.sum(jnp.where(below & (keys >= cid.astype(F32) * tokens), 1.0, 0.0), axis=0, keepdims=True)
        fits = rank < slots
        slot = jnp.where(fits, group * slots + rank, -1.0)
        slot_ref[...] = slot
        place[...] = jnp.where(iota((sets * slots, tokens), 0) == slot, 1.0, 0.0).astype(BF16)
        lane = jnp.where(fits, group * 128 + rank + 64 * parity_ref[0, 0].astype(F32), -1.0)
        spread = jnp.where(iota((sets * 128, tokens), 0) == lane, 1.0, 0.0).astype(BF16)
        short = jnp.where(jnp.max(rank, axis=1, keepdims=True) >= slots, 1.0, 0.0)
        low = jnp.bitwise_and(pos, 255)
        high = jnp.right_shift(pos, 8) + 1
        row = lax.broadcasted_iota(jnp.int32, (16, tokens), 0)
        facts = jnp.where(
            row == 0,
            high.astype(F32),
            jnp.where(row == 1, low.astype(F32), jnp.where(row == 2, own.astype(F32) + 1.0, jnp.where(row == 3, within, 0.0))),
        ).astype(BF16)
        meta[...] = nt_dot(facts, spread)
        meta[4:5, :] = jnp.broadcast_to(short, (1, sets * 128))

    gap = out_ref.shape[2] - 3 * slots - 8
    for h in range(out_ref.shape[1]):
        at = slice(h * HEAD_DIM, (h + 1) * HEAD_DIM)
        y = dot(place[...], jnp.concatenate([q_ref[:, at], k_ref[:, at], v_ref[:, at]], axis=1))
        for s in range(sets):
            part = y[s * slots : (s + 1) * slots]
            pieces = [part[:, :128], part[:, 128:256], part[:, 256:]]
            if gap:
                pieces.append(jnp.zeros((gap, 128), F32))
            pieces.append(meta[0:8, s * 128 : (s + 1) * 128])
            out_ref[s, h] = jnp.concatenate(pieces, axis=0).astype(BF16)


def attend_kernel(slots, x_ref, o_ref, short_ref, xs, os, code, high, low, tab_v, tab, sem):
    sources, rows, _ = x_ref.shape
    blocks = sources // 4
    total_rows = xs.shape[0]

    facts = x_ref[:, rows - 16 : rows, :].astype(F32)
    high[...] = facts[:, 8, :]
    low[...] = facts[:, 9, :]
    own = facts[:, 10, :]
    within = facts[:, 11, :]
    short_ref[...] = jnp.broadcast_to(jnp.max(facts[:, 12, :], axis=0, keepdims=True), (8, 128))
    lane = iota((sources, 128), 1)
    counts = jnp.zeros((sources, 128), F32)
    for c in range(CL_SET):
        n = jnp.sum(jnp.where(own == c + 1, 1.0, 0.0), axis=1, keepdims=True)
        counts = counts + jnp.where(lane == c, n, 0.0)
    counts16 = counts.astype(BF16)
    r = lax.broadcasted_iota(jnp.int32, (sources, sources), 0)
    s = lax.broadcasted_iota(jnp.int32, (sources, sources), 1)

    def picked(mask):
        return dot(jnp.where(mask, 1.0, 0.0).astype(BF16), counts16)

    first = jnp.bitwise_and(r, -4)
    before = picked(s < r)
    before_block = picked(s < first)
    after_block = picked(s < first + 4)
    total = picked(s >= 0)
    nblk = jnp.floor((total + (BLK - 1)) * (1.0 / BLK))
    start_blk = dot(nblk.astype(BF16), jnp.where((r < s) & (r < CL_SET), 1.0, 0.0).astype(BF16))
    base = start_blk * BLK
    aligned = base + jnp.floor(before_block * (1.0 / 16)) * 16
    shift = base + before - aligned
    passes = jnp.where(lane < CL_SET, jnp.floor((base + after_block - aligned + (RUN - 1)) * (1.0 / RUN)), 0.0)
    passes = jnp.max(passes, axis=1, keepdims=True)
    place = within
    for c in range(CL_SET):
        place = place + jnp.where(own == c + 1, shift[:, c : c + 1], 0.0)
    step = jnp.floor(place * (1.0 / RUN) + (0.5 / RUN))
    code[...] = jnp.where(own > 0.0, step * CODES + (own - 1.0) * RUN + (place - step * RUN) + 1.0, 0.0)
    last = start_blk + nblk
    used = jnp.max(jnp.where(lane < CL_SET, last, 0.0), axis=1, keepdims=True)
    table = jnp.where(lane < CL_SET, aligned, 0.0)
    table = jnp.where(lane == 8, passes, table)
    table = jnp.where(lane == 9, used, table)
    table = jnp.where(lane == 10, jnp.max(passes), table)
    spin = jnp.zeros((sources, 128), F32)
    for c in range(CL_SET):
        spin = spin + jnp.where(lane == 16 + c, start_blk[:, c : c + 1], 0.0) + jnp.where(lane == 24 + c, nblk[:, c : c + 1], 0.0)
    tab_v[...] = (table + spin).astype(jnp.int32)
    copy = pltpu.make_async_copy(tab_v, tab, sem)
    copy.start()
    os[...] = jnp.zeros(os.shape, BF16)
    copy.wait()
    used_blocks = tab[0, 9]

    def clear(i, _):
        at = pl.ds(pl.multiple_of(i * BLK, BLK), BLK)
        xs[at, :] = jnp.zeros((BLK, xs.shape[1]), BF16)
        return 0

    lax.fori_loop(0, jnp.minimum(used_blocks + 4, total_rows // BLK), clear, 0)

    def joined(ref, b):
        return jnp.concatenate(
            [
                ref[pl.ds(4 * b, 1), :] + ref[pl.ds(4 * b + 1, 1), :],
                ref[pl.ds(4 * b + 2, 1), :] + ref[pl.ds(4 * b + 3, 1), :],
            ],
            axis=1,
        )

    code_rows = iota((CODES, 256), 0)
    which = lax.broadcasted_iota(jnp.int32, (128, 256), 0)

    def compact(b, p):
        x4 = x_ref[pl.ds(4 * b, 4)].astype(F32)
        xcat = jnp.concatenate([x4[:, i * slots : i * slots + 64].reshape(256, 128) for i in range(3)], axis=1).astype(BF16)
        row = joined(code, b) - jnp.asarray(p * CODES + 1, F32)
        where_at = jnp.where(which == 0, joined(high, b) * 256.0, jnp.where(which == 1, joined(low, b), 0.0)).astype(BF16)
        select = jnp.where(code_rows == row, 1.0, 0.0).astype(BF16)
        y = jnp.concatenate([dot(select, xcat), nt_dot(select, where_at)], axis=1).astype(BF16)
        ats = [pl.ds(pl.multiple_of(tab[4 * b, c] + p * RUN, 16), RUN) for c in range(CL_SET)]
        new = [xs[at, :] + y[c * RUN : (c + 1) * RUN] for c, at in enumerate(ats)]
        for at, x in zip(ats, new):
            xs[at, :] = x

    def each_block(body):
        def some(i, _):
            for u in range(UNROLL):
                body(i * UNROLL + u, 0)
            return 0

        lax.fori_loop(0, blocks // UNROLL, some, 0)

        @pl.when(tab[0, 10] > 1)
        def _():
            def rest(b, _):
                def more(p, _):
                    body(b, p)
                    return 0

                return lax.fori_loop(1, tab[4 * b, 8], more, 0)

            lax.fori_loop(0, blocks, rest, 0)

    each_block(compact)

    scale = HEAD_DIM ** (-0.5) * 1.4426950408889634
    to_lanes = jnp.where(lax.broadcasted_iota(jnp.int32, (16, 128), 1) < 2, 1.0, 0.0).astype(BF16)
    to_all = jnp.where(lax.broadcasted_iota(jnp.int32, (128, 128), 0) < 2, 1.0, 0.0).astype(BF16)

    def key_places(at):
        kp = nt_dot(to_lanes, xs[at, 384:512])[0:1]
        return jnp.where(kp > 0.0, kp, 1e9)

    def hidden(scores, kp, qp):
        lanes = scores.shape[1] // 128
        return jnp.where(kp <= jnp.concatenate([qp] * lanes, axis=1), scores * scale, HIDDEN)

    def fixed(begin, count):
        kat = pl.ds(pl.multiple_of(begin * BLK, BLK), count * BLK)
        keys = xs[kat, 128:256]
        values = xs[kat, 256:384]
        kp = key_places(kat)
        for i in range(0, count, 2):
            wide = min(2, count - i)
            at = pl.ds(pl.multiple_of((begin + i) * BLK, BLK), wide * BLK)
            scores = hidden(nt_dot(xs[at, 0:128], keys), kp, dot(xs[at, 384:512], to_all))
            weight = jnp.exp2(scores - jnp.max(scores, axis=1, keepdims=True))
            total = jnp.sum(weight, axis=1, keepdims=True)
            os[at, :] = (dot(weight.astype(BF16), values) / total).astype(BF16)

    def general(begin, count):
        def queries(i, _):
            at = pl.ds(pl.multiple_of((begin + i) * BLK, BLK), BLK)
            q = xs[at, 0:128]
            qp = dot(xs[at, 384:512], to_all)

            def keys(j, carried):
                top, total, summed = carried
                kat = pl.ds(pl.multiple_of((begin + j) * BLK, BLK), BLK)
                scores = hidden(nt_dot(q, xs[kat, 128:256]), key_places(kat), qp)
                fresh = jnp.maximum(top, jnp.max(scores, axis=1, keepdims=True))
                weight = jnp.exp2(scores - fresh)
                rescale = jnp.exp2(top - fresh)
                total = total * rescale + jnp.sum(weight, axis=1, keepdims=True)
                summed = summed * rescale + dot(weight.astype(BF16), xs[kat, 256:384])
                return fresh, total, summed

            init = (jnp.full((BLK, 1), HIDDEN, F32), jnp.zeros((BLK, 1), F32), jnp.zeros((BLK, 128), F32))
            _, total, summed = lax.fori_loop(0, count, keys, init)
            os[at, :] = (summed / total).astype(BF16)
            return 0

        lax.fori_loop(0, count, queries, 0)

    def cluster(c, _):
        begin = tab[0, 16 + c]
        count = tab[0, 24 + c]
        for n in FIXED:
            pl.when(count == n)(functools.partial(fixed, begin, n))
        pl.when((count < FIXED[0]) | (count > FIXED[-1]))(functools.partial(general, begin, count))
        return 0

    lax.fori_loop(0, CL_SET, cluster, 0)

    code_lanes = iota((256, CODES), 1)

    def spread(b, p):
        col = column(joined(code, b) - jnp.asarray(p * CODES + 1, F32))
        col = jnp.concatenate([col] * (CODES // 128), axis=1)
        cat = jnp.concatenate(
            [os[pl.ds(pl.multiple_of(tab[4 * b, c] + p * RUN, 16), RUN), :] for c in range(CL_SET)], axis=0
        )
        select = jnp.where(code_lanes == col, 1.0, 0.0).astype(BF16)
        new = dot(select, cat).reshape(4, 64, 128)[:, :slots]
        at = pl.ds(4 * b, 4)
        if isinstance(p, int):
            o_ref[at] = new.astype(BF16)
        else:
            o_ref[at] = (o_ref[at].astype(F32) + new).astype(BF16)

    each_block(spread)


def attend_call(slots, got):
    sources = got.shape[0]
    whole = pl.BlockSpec(memory_space=pltpu.VMEM)
    total_rows = sources * slots + (CL_SET + 4) * BLK
    return pl.pallas_call(
        functools.partial(attend_kernel, slots),
        in_specs=[whole],
        out_specs=[whole, whole],
        out_shape=[
            jax.ShapeDtypeStruct((sources, slots, 128), BF16),
            jax.ShapeDtypeStruct((8, 128), F32),
        ],
        scratch_shapes=[
            pltpu.VMEM((total_rows, 4 * HEAD_DIM), BF16),
            pltpu.VMEM((total_rows, HEAD_DIM), BF16),
            pltpu.VMEM((sources, 128), F32),
            pltpu.VMEM((sources, 128), F32),
            pltpu.VMEM((sources, 128), F32),
            pltpu.VMEM((sources, 128), jnp.int32),
            pltpu.SMEM((sources, 128), jnp.int32),
            pltpu.SemaphoreType.DMA,
        ],
        compiler_params=pltpu.CompilerParams(vmem_limit_bytes=56 * 2**20),
        name="attend",
    )(got)


def unpack_kernel(slots, slot_ref, r_ref, out_ref, select):
    sets, heads = r_ref.shape[0], r_ref.shape[1]

    @pl.when(pl.program_id(0) == 0)
    def _():
        col = column(slot_ref[...])
        col = jnp.concatenate([col] * (-(-sets * slots // 128)), axis=1)[:, : sets * slots]
        select[...] = jnp.where(iota(select.shape, 1) == col, 1.0, 0.0).astype(BF16)

    for h in range(heads):
        x = r_ref[:, h].astype(F32).reshape(sets * slots, 128).astype(BF16)
        out_ref[:, h * 128 : (h + 1) * 128] = dot(select[...], x).astype(BF16)


def pack_call(slots, sets, parity, cid_row, pos_row, queries, keys, values):
    tokens, width = queries.shape
    heads = width // HEAD_DIM
    rows = chunk_rows(slots)
    some = pl.BlockSpec((tokens, PACK * HEAD_DIM), lambda h: (0, h))
    line = pl.BlockSpec((1, tokens), lambda h: (0, 0))
    return pl.pallas_call(
        functools.partial(pack_kernel, slots, sets),
        grid=(heads // PACK,),
        in_specs=[pl.BlockSpec(memory_space=pltpu.SMEM), line, line, some, some, some],
        out_specs=[pl.BlockSpec((sets, PACK, rows, 128), lambda h: (0, h, 0, 0)), line],
        out_shape=[
            jax.ShapeDtypeStruct((sets, heads, rows, 128), BF16),
            jax.ShapeDtypeStruct((1, tokens), F32),
        ],
        scratch_shapes=[pltpu.VMEM((sets * slots, tokens), BF16), pltpu.VMEM((16, sets * 128), F32)],
        compiler_params=pltpu.CompilerParams(vmem_limit_bytes=56 * 2**20),
        name="pack",
    )(parity, cid_row, pos_row, queries, keys, values)


def unpack_call(slots, slot, back):
    sets, heads = back.shape[:2]
    tokens = slot.shape[1]
    return pl.pallas_call(
        functools.partial(unpack_kernel, slots),
        grid=(heads // UNPACK,),
        in_specs=[
            pl.BlockSpec((1, tokens), lambda h: (0, 0)),
            pl.BlockSpec((sets, UNPACK, slots, 128), lambda h: (0, h, 0, 0)),
        ],
        out_specs=pl.BlockSpec((tokens, UNPACK * HEAD_DIM), lambda h: (0, h)),
        out_shape=jax.ShapeDtypeStruct((tokens, heads * HEAD_DIM), BF16),
        scratch_shapes=[pltpu.VMEM((tokens, sets * slots), BF16)],
        compiler_params=pltpu.CompilerParams(vmem_limit_bytes=56 * 2**20),
        name="unpack",
    )(slot, back)


def attention(slots, queries, keys, values, cid_row, pos_row, parity, fallback=None):
    heads = queries.shape[1] // HEAD_DIM
    sources = lax.axis_size("grp") * lax.axis_size("blk")
    sets = sources // heads
    sent, slot = pack_call(slots, sets, parity, cid_row, pos_row, queries, keys, values)
    got = lax.all_to_all(
        sent.reshape(sources, sent.shape[2], 128), ("grp", "blk"), split_axis=0, concat_axis=0, tiled=True
    )
    done, short = attend_call(slots, got)
    back = lax.all_to_all(done, ("grp", "blk"), split_axis=0, concat_axis=0, tiled=True)
    back = back.reshape(sets, heads, slots, 128)
    if fallback is None:
        return unpack_call(slots, slot, back)
    return lax.cond(short[0, 0] > 0.0, fallback, lambda: unpack_call(slots, slot, back))


def local(queries, keys, values, cluster_ids, positions):
    cid_row = cluster_ids.reshape(1, -1)
    pos_row = positions.reshape(1, -1)
    me = lax.axis_index("grp") * lax.axis_size("blk") + lax.axis_index("blk")
    parity = (me % 2).astype(jnp.int32).reshape(1, 1)
    args = (queries, keys, values, cid_row, pos_row, parity)
    return attention(FEW, *args, fallback=lambda: attention(ALL, *args))


def solution(mesh):
    placed = (
        P(("grp", "blk"), None),
        P(("grp", "blk"), None),
        P(("grp", "blk"), None),
        P(("grp", "blk")),
        P(("grp", "blk")),
    )
    return jax.shard_map(
        local, mesh=mesh, in_specs=placed, out_specs=P(("grp", "blk"), None), check_vma=False
    )
```

```python
import functools

import jax
import jax.numpy as jnp
from jax import lax
from jax.experimental import pallas as pl
from jax.experimental.pallas import tpu as pltpu
from jax.sharding import PartitionSpec as P

HEAD_DIM = 128
CL_GRP = 4
CL_SET = 2 * CL_GRP
RUN = 48
CODES = CL_SET * RUN
BLK = 128
FIXED = (4, 5, 6)
UNROLL = 8
TILE = 3
JOINT = 2
ALL = 64
FEW = 56
PACK = 8
UNPACK = 8
F32 = jnp.float32
BF16 = jnp.bfloat16
HIDDEN = -1e30


def chunk_rows(slots):
    return -(-(3 * slots + 8) // 16) * 16


def iota(shape, dim):
    return lax.broadcasted_iota(jnp.int32, shape, dim).astype(F32)


def column(row):
    return jnp.transpose(jnp.broadcast_to(row, (128, row.shape[1])))


def nt_dot(a, b):
    return lax.dot_general(a, b, (((1,), (1,)), ((), ())), preferred_element_type=F32)


def dot(a, b):
    return jnp.dot(a, b, preferred_element_type=F32)


def pack_kernel(slots, sets, parity_ref, cid_ref, pos_ref, q_ref, k_ref, v_ref, out_ref, slot_ref, place, meta):
    tokens = cid_ref.shape[1]

    @pl.when(pl.program_id(0) == 0)
    def _():
        cid = cid_ref[...]
        pos = pos_ref[...]
        own = jnp.bitwise_and(cid, CL_SET - 1)
        group = (cid - own).astype(F32) * (1.0 / CL_SET)
        key = cid.astype(F32) * tokens + iota((1, tokens), 1)
        keys = column(key)
        keys = jnp.concatenate([keys] * (tokens // 128), axis=1)
        below = keys < key
        rank = jnp.sum(jnp.where(below & (keys >= group * (CL_SET * tokens)), 1.0, 0.0), axis=0, keepdims=True)
        within = jnp.sum(jnp.where(below & (keys >= cid.astype(F32) * tokens), 1.0, 0.0), axis=0, keepdims=True)
        fits = rank < slots
        slot = jnp.where(fits, group * slots + rank, -1.0)
        slot_ref[...] = slot
        place[...] = jnp.where(iota((sets * slots, tokens), 0) == slot, 1.0, 0.0).astype(BF16)
        lane = jnp.where(fits, group * 128 + rank + 64 * parity_ref[0, 0].astype(F32), -1.0)
        spread = jnp.where(iota((sets * 128, tokens), 0) == lane, 1.0, 0.0).astype(BF16)
        short = jnp.where(jnp.max(rank, axis=1, keepdims=True) >= slots, 1.0, 0.0)
        low = jnp.bitwise_and(pos, 255)
        high = jnp.right_shift(pos, 8) + 1
        row = lax.broadcasted_iota(jnp.int32, (16, tokens), 0)
        facts = jnp.where(
            row == 0,
            high.astype(F32),
            jnp.where(row == 1, low.astype(F32), jnp.where(row == 2, own.astype(F32) + 1.0, jnp.where(row == 3, within, 0.0))),
        ).astype(BF16)
        meta[...] = nt_dot(facts, spread)
        meta[4:5, :] = jnp.broadcast_to(short, (1, sets * 128))

    gap = out_ref.shape[2] - 3 * slots - 8
    for h in range(out_ref.shape[1]):
        at = slice(h * HEAD_DIM, (h + 1) * HEAD_DIM)
        y = dot(place[...], jnp.concatenate([q_ref[:, at], k_ref[:, at], v_ref[:, at]], axis=1))
        for s in range(sets):
            part = y[s * slots : (s + 1) * slots]
            pieces = [part[:, :128], part[:, 128:256], part[:, 256:]]
            if gap:
                pieces.append(jnp.zeros((gap, 128), F32))
            pieces.append(meta[0:8, s * 128 : (s + 1) * 128])
            out_ref[s, h] = jnp.concatenate(pieces, axis=0).astype(BF16)


def attend_kernel(
    slots, x_hbm, o_hbm, short_ref, x_ref, o_ref, facts_ref, flat, xs, os, code, high, low, tab_v, tab, sem, facts_sem, in_sems, out_sems
):
    sources, rows, _ = x_ref.shape
    step_rows = 4 * UNROLL
    steps = sources // step_rows
    facts_in = pltpu.make_async_copy(x_hbm.at[:, rows - 16 : rows, :], facts_ref, facts_sem)
    facts_in.start()

    def part_in(i):
        at = pl.ds(i * step_rows, step_rows)
        return pltpu.make_async_copy(x_hbm.at[at], x_ref.at[at], in_sems.at[i])

    def part_out(i):
        at = pl.ds(i * step_rows, step_rows)
        return pltpu.make_async_copy(o_ref.at[at], o_hbm.at[at], out_sems.at[i])

    for i in range(steps):
        part_in(i).start()
    os[...] = jnp.zeros(os.shape, BF16)
    ahead = 5 * sources // 16
    xs[0 : ahead * BLK, :] = jnp.zeros((ahead * BLK, xs.shape[1]), BF16)
    facts_in.wait()
    total_rows = xs.shape[0]

    flat[...] = facts_ref[...].astype(F32)[:, 8:16].reshape(flat.shape)

    def fact(i):
        return flat[pl.ds(i, sources, 8), :]

    high[...] = fact(0) * 256.0
    low[...] = fact(1)
    own = fact(2)
    within = fact(3)
    short_ref[...] = jnp.broadcast_to(jnp.max(fact(4), axis=0, keepdims=True), (8, 128))
    lane = iota((sources, 128), 1)
    r = lax.broadcasted_iota(jnp.int32, (128, CL_SET * 128), 0)
    s = lax.broadcasted_iota(jnp.int32, (128, CL_SET * 128), 1)
    to_each = jnp.where(r == jnp.right_shift(s, 7), 1.0, 0.0).astype(BF16)
    is_own = [jnp.where(own == c + 1, 1.0, 0.0) for c in range(CL_SET)]
    counts = nt_dot(jnp.concatenate(is_own, axis=1).astype(BF16), to_each).astype(BF16)
    r = lax.broadcasted_iota(jnp.int32, (sources, sources), 0)
    s = lax.broadcasted_iota(jnp.int32, (sources, sources), 1)
    first = jnp.bitwise_and(r, -4)
    masks = [s >= 0, s < r, s < first, s < first + 4]
    sums = dot(jnp.concatenate([jnp.where(m, 1.0, 0.0) for m in masks], axis=0).astype(BF16), counts)
    total, before, before_block, after_block = (sums[i * sources : (i + 1) * sources] for i in range(4))
    nblk = jnp.floor((total + (BLK - 1)) * (1.0 / BLK))
    start_blk = dot(nblk.astype(BF16), jnp.where((r < s) & (r < CL_SET), 1.0, 0.0).astype(BF16))
    skipped = jnp.floor(before_block * (1.0 / 16)) * 16
    shift = dot((before - skipped).astype(BF16), to_each)
    place = within
    for c in range(CL_SET):
        place = place + is_own[c] * shift[:, c * 128 : (c + 1) * 128]
    step = jnp.floor(place * (1.0 / RUN) + (0.5 / RUN))
    code[...] = jnp.where(own > 0.0, step * CODES + (own - 1.0) * RUN + (place - step * RUN) + 1.0, 0.0)
    passes = jnp.max(jnp.where(lane < CL_SET, after_block - skipped, 0.0), axis=(0, 1), keepdims=True)
    passes = jnp.floor((passes + (RUN - 1)) * (1.0 / RUN))
    tab_v[0:sources] = jnp.where(lane < CL_SET, start_blk * BLK + skipped, passes).astype(jnp.int32)
    tab_v[sources : sources + 8] = start_blk[0:8].astype(jnp.int32)
    tab_v[sources + 8 : sources + 16] = nblk[0:8].astype(jnp.int32)
    copy = pltpu.make_async_copy(tab_v, tab, sem)
    copy.start()
    copy.wait()
    most_passes = tab[0, CL_SET]

    def begin_of(c):
        return tab[sources, c]

    def count_of(c):
        return tab[sources + 8, c]

    used_blocks = begin_of(CL_SET - 1) + count_of(CL_SET - 1)

    def clear(i, _):
        at = pl.ds(pl.multiple_of(i * BLK, BLK), BLK)
        xs[at, :] = jnp.zeros((BLK, xs.shape[1]), BF16)
        return 0

    lax.fori_loop(ahead, jnp.minimum(used_blocks + 4, total_rows // BLK), clear, 0)

    def joined(ref, b):
        return jnp.concatenate(
            [
                ref[pl.ds(4 * b, 1), :] + ref[pl.ds(4 * b + 1, 1), :],
                ref[pl.ds(4 * b + 2, 1), :] + ref[pl.ds(4 * b + 3, 1), :],
            ],
            axis=1,
        )

    code_rows = iota((CODES, 256), 0)
    which = lax.broadcasted_iota(jnp.int32, (128, 256), 0)

    def compact(b, p):
        x4 = x_ref[pl.ds(4 * b, 4)].astype(F32)
        xcat = jnp.concatenate([x4[:, i * slots : i * slots + 64].reshape(256, 128) for i in range(3)], axis=1).astype(BF16)
        row = joined(code, b) - jnp.asarray(p * CODES + 1, F32)
        where_at = jnp.where(which == 0, joined(high, b), jnp.where(which == 1, joined(low, b), 0.0)).astype(BF16)
        select = jnp.where(code_rows == row, 1.0, 0.0).astype(BF16)
        y = jnp.concatenate([dot(select, xcat), nt_dot(select, where_at)], axis=1).astype(BF16)
        ats = [pl.ds(pl.multiple_of(tab[4 * b, c] + p * RUN, 16), RUN) for c in range(CL_SET)]
        new = [xs[at, :] + y[c * RUN : (c + 1) * RUN] for c, at in enumerate(ats)]
        for at, x in zip(ats, new):
            xs[at, :] = x

    def each_block(body, before=None, after=None):
        def some(i, _):
            if before is not None:
                before(i)
            for u in range(UNROLL):
                body(i * UNROLL + u, 0)

            @pl.when(most_passes > 1)
            def _():
                def rest(u, _):
                    b = i * UNROLL + u

                    def more(p, _):
                        body(b, p)
                        return 0

                    return lax.fori_loop(1, most_passes, more, 0)

                lax.fori_loop(0, UNROLL, rest, 0)

            if after is not None:
                after(i)
            return 0

        lax.fori_loop(0, steps, some, 0)

    each_block(compact, before=lambda i: part_in(i).wait())

    scale = HEAD_DIM ** (-0.5) * 1.4426950408889634
    to_lanes = jnp.where(lax.broadcasted_iota(jnp.int32, (16, 128), 1) < 2, 1.0, 0.0).astype(BF16)
    to_all = jnp.where(lax.broadcasted_iota(jnp.int32, (128, 128), 0) < 2, 1.0, 0.0).astype(BF16)

    def key_places(at):
        kp = nt_dot(to_lanes, xs[at, 384:512])[0:1]
        return jnp.where(kp > 0.0, kp, 1e9)

    def hidden(scores, kp, qp):
        lanes = scores.shape[1] // 128
        return jnp.where(kp <= jnp.concatenate([qp] * lanes, axis=1), scores * scale, HIDDEN)

    def fixed(pair, count):
        for c in pair:
            begin, own_count = begin_of(c), count_of(c)
            kat = pl.ds(pl.multiple_of(begin * BLK, BLK), count * BLK)
            keys = xs[kat, 128:256]
            values = xs[kat, 256:384]
            mine = lax.broadcasted_iota(jnp.int32, (1, count * BLK), 1) < own_count * BLK
            kp = jnp.where(mine, key_places(kat), 1e9)
            for i in range(0, count, TILE):
                wide = min(TILE, count - i)
                at = pl.ds(pl.multiple_of((begin + i) * BLK, BLK), wide * BLK)
                scores = hidden(nt_dot(xs[at, 0:128], keys), kp, dot(xs[at, 384:512], to_all))
                weight = jnp.exp2(scores - jnp.max(scores, axis=1, keepdims=True))
                total = jnp.sum(weight, axis=1, keepdims=True)
                os[at, :] = (dot(weight.astype(BF16), values) / total).astype(BF16)

    def general(begin, count):
        def queries(i, _):
            at = pl.ds(pl.multiple_of((begin + i) * BLK, BLK), BLK)
            q = xs[at, 0:128]
            qp = dot(xs[at, 384:512], to_all)

            def keys(j, carried):
                top, total, summed = carried
                kat = pl.ds(pl.multiple_of((begin + j) * BLK, BLK), BLK)
                scores = hidden(nt_dot(q, xs[kat, 128:256]), key_places(kat), qp)
                fresh = jnp.maximum(top, jnp.max(scores, axis=1, keepdims=True))
                weight = jnp.exp2(scores - fresh)
                rescale = jnp.exp2(top - fresh)
                total = total * rescale + jnp.sum(weight, axis=1, keepdims=True)
                summed = summed * rescale + dot(weight.astype(BF16), xs[kat, 256:384])
                return fresh, total, summed

            init = (jnp.full((BLK, 1), HIDDEN, F32), jnp.zeros((BLK, 1), F32), jnp.zeros((BLK, 128), F32))
            _, total, summed = lax.fori_loop(0, count, keys, init)
            os[at, :] = (summed / total).astype(BF16)
            return 0

        lax.fori_loop(0, count, queries, 0)

    def clusters(k, _):
        pair = [JOINT * k + u for u in range(JOINT)]
        counts = [count_of(c) for c in pair]
        most = functools.reduce(jnp.maximum, counts)
        least = functools.reduce(jnp.minimum, counts)
        alike = (most >= FIXED[0]) & (most <= FIXED[-1]) & (least >= most - 2)
        for n in FIXED:
            pl.when(alike & (most == n))(functools.partial(fixed, pair, n))

        @pl.when(jnp.logical_not(alike))
        def _():
            for c, n in zip(pair, counts):
                general(begin_of(c), n)

        return 0

    lax.fori_loop(0, CL_SET // JOINT, clusters, 0)

    code_lanes = iota((256, CODES), 1)

    def spread(b, p):
        col = column(joined(code, b) - jnp.asarray(p * CODES + 1, F32))
        col = jnp.concatenate([col] * (CODES // 128), axis=1)
        cat = jnp.concatenate(
            [os[pl.ds(pl.multiple_of(tab[4 * b, c] + p * RUN, 16), RUN), :] for c in range(CL_SET)], axis=0
        )
        select = jnp.where(code_lanes == col, 1.0, 0.0).astype(BF16)
        new = dot(select, cat).reshape(4, 64, 128)[:, :slots]
        at = pl.ds(4 * b, 4)
        if isinstance(p, int):
            o_ref[at] = new.astype(BF16)
        else:
            o_ref[at] = (o_ref[at].astype(F32) + new).astype(BF16)

    each_block(spread, after=lambda i: part_out(i).start())
    for i in range(steps):
        part_out(i).wait()


def attend_call(slots, got):
    sources = got.shape[0]
    whole = pl.BlockSpec(memory_space=pltpu.VMEM)
    total_rows = sources * slots + (CL_SET + 4) * BLK
    return pl.pallas_call(
        functools.partial(attend_kernel, slots),
        in_specs=[pl.BlockSpec(memory_space=pl.ANY)],
        out_specs=[pl.BlockSpec(memory_space=pl.ANY), whole],
        out_shape=[
            jax.ShapeDtypeStruct((sources, slots, 128), BF16),
            jax.ShapeDtypeStruct((8, 128), F32),
        ],
        scratch_shapes=[
            pltpu.VMEM(got.shape, BF16),
            pltpu.VMEM((sources, slots, 128), BF16),
            pltpu.VMEM((sources, 16, 128), BF16),
            pltpu.VMEM((sources * 8, 128), F32),
            pltpu.VMEM((total_rows, 4 * HEAD_DIM), BF16),
            pltpu.VMEM((total_rows, HEAD_DIM), BF16),
            pltpu.VMEM((sources, 128), F32),
            pltpu.VMEM((sources, 128), F32),
            pltpu.VMEM((sources, 128), F32),
            pltpu.VMEM((sources + 16, 128), jnp.int32),
            pltpu.SMEM((sources + 16, 128), jnp.int32),
            pltpu.SemaphoreType.DMA,
            pltpu.SemaphoreType.DMA,
            pltpu.SemaphoreType.DMA((sources // (4 * UNROLL),)),
            pltpu.SemaphoreType.DMA((sources // (4 * UNROLL),)),
        ],
        compiler_params=pltpu.CompilerParams(vmem_limit_bytes=56 * 2**20),
        name="attend",
    )(got)


def unpack_kernel(slots, slot_ref, r_ref, out_ref, select):
    sets, heads = r_ref.shape[0], r_ref.shape[1]

    @pl.when(pl.program_id(0) == 0)
    def _():
        col = column(slot_ref[...])
        col = jnp.concatenate([col] * (-(-sets * slots // 128)), axis=1)[:, : sets * slots]
        select[...] = jnp.where(iota(select.shape, 1) == col, 1.0, 0.0).astype(BF16)

    for h in range(heads):
        x = r_ref[:, h].astype(F32).reshape(sets * slots, 128).astype(BF16)
        out_ref[:, h * 128 : (h + 1) * 128] = dot(select[...], x).astype(BF16)


def pack_call(slots, sets, parity, cid_row, pos_row, queries, keys, values):
    tokens, width = queries.shape
    heads = width // HEAD_DIM
    rows = chunk_rows(slots)
    some = pl.BlockSpec((tokens, PACK * HEAD_DIM), lambda h: (0, h))
    line = pl.BlockSpec((1, tokens), lambda h: (0, 0))
    return pl.pallas_call(
        functools.partial(pack_kernel, slots, sets),
        grid=(heads // PACK,),
        in_specs=[pl.BlockSpec(memory_space=pltpu.SMEM), line, line, some, some, some],
        out_specs=[pl.BlockSpec((sets, PACK, rows, 128), lambda h: (0, h, 0, 0)), line],
        out_shape=[
            jax.ShapeDtypeStruct((sets, heads, rows, 128), BF16),
            jax.ShapeDtypeStruct((1, tokens), F32),
        ],
        scratch_shapes=[pltpu.VMEM((sets * slots, tokens), BF16), pltpu.VMEM((16, sets * 128), F32)],
        compiler_params=pltpu.CompilerParams(vmem_limit_bytes=56 * 2**20),
        name="pack",
    )(parity, cid_row, pos_row, queries, keys, values)


def unpack_call(slots, slot, back):
    sets, heads = back.shape[:2]
    tokens = slot.shape[1]
    return pl.pallas_call(
        functools.partial(unpack_kernel, slots),
        grid=(heads // UNPACK,),
        in_specs=[
            pl.BlockSpec((1, tokens), lambda h: (0, 0)),
            pl.BlockSpec((sets, UNPACK, slots, 128), lambda h: (0, h, 0, 0)),
        ],
        out_specs=pl.BlockSpec((tokens, UNPACK * HEAD_DIM), lambda h: (0, h)),
        out_shape=jax.ShapeDtypeStruct((tokens, heads * HEAD_DIM), BF16),
        scratch_shapes=[pltpu.VMEM((tokens, sets * slots), BF16)],
        compiler_params=pltpu.CompilerParams(vmem_limit_bytes=56 * 2**20),
        name="unpack",
    )(slot, back)


def attention(slots, queries, keys, values, cid_row, pos_row, parity, fallback=None):
    heads = queries.shape[1] // HEAD_DIM
    sources = lax.axis_size("grp") * lax.axis_size("blk")
    sets = sources // heads
    sent, slot = pack_call(slots, sets, parity, cid_row, pos_row, queries, keys, values)
    got = lax.all_to_all(
        sent.reshape(sources, sent.shape[2], 128), ("grp", "blk"), split_axis=0, concat_axis=0, tiled=True
    )
    done, short = attend_call(slots, got)
    back = lax.all_to_all(done, ("grp", "blk"), split_axis=0, concat_axis=0, tiled=True)
    back = back.reshape(sets, heads, slots, 128)
    if fallback is None:
        return unpack_call(slots, slot, back)
    return lax.cond(short[0, 0] > 0.0, fallback, lambda: unpack_call(slots, slot, back))


def local(queries, keys, values, cluster_ids, positions):
    cid_row = cluster_ids.reshape(1, -1)
    pos_row = positions.reshape(1, -1)
    me = lax.axis_index("grp") * lax.axis_size("blk") + lax.axis_index("blk")
    parity = (me % 2).astype(jnp.int32).reshape(1, 1)
    args = (queries, keys, values, cid_row, pos_row, parity)
    return attention(FEW, *args, fallback=lambda: attention(ALL, *args))


def solution(mesh):
    placed = (
        P(("grp", "blk"), None),
        P(("grp", "blk"), None),
        P(("grp", "blk"), None),
        P(("grp", "blk")),
        P(("grp", "blk")),
    )
    return jax.shard_map(
        local, mesh=mesh, in_specs=placed, out_specs=P(("grp", "blk"), None), check_vma=False
    )
```

```python
import functools

import jax
import jax.numpy as jnp
from jax import lax
from jax.experimental import pallas as pl
from jax.experimental.pallas import tpu as pltpu
from jax.sharding import PartitionSpec as P

HEAD_DIM = 128
CL_GRP = 4
CL_SET = 2 * CL_GRP
RUN = 48
CODES = CL_SET * RUN
BLK = 128
FIXED = (4, 5, 6)
UNROLL = 16
TILE = 3
JOINT = 2
ALL = 64
FEW = 56
PACK = 8
UNPACK = 8
F32 = jnp.float32
BF16 = jnp.bfloat16
HIDDEN = -1e30


def chunk_rows(slots):
    return -(-(3 * slots + 8) // 16) * 16


def iota(shape, dim):
    return lax.broadcasted_iota(jnp.int32, shape, dim).astype(F32)


def column(row):
    return jnp.transpose(jnp.broadcast_to(row, (128, row.shape[1])))


def nt_dot(a, b):
    return lax.dot_general(a, b, (((1,), (1,)), ((), ())), preferred_element_type=F32)


def dot(a, b):
    return jnp.dot(a, b, preferred_element_type=F32)


def pack_kernel(slots, sets, parity_ref, cid_ref, pos_ref, q_ref, k_ref, v_ref, out_ref, slot_ref, place, meta):
    tokens = cid_ref.shape[1]

    @pl.when(pl.program_id(0) == 0)
    def _():
        cid = cid_ref[...]
        pos = pos_ref[...]
        own = jnp.bitwise_and(cid, CL_SET - 1)
        group = (cid - own).astype(F32) * (1.0 / CL_SET)
        key = cid.astype(F32) * tokens + iota((1, tokens), 1)
        keys = column(key)
        keys = jnp.concatenate([keys] * (tokens // 128), axis=1)
        below = keys < key
        rank = jnp.sum(jnp.where(below & (keys >= group * (CL_SET * tokens)), 1.0, 0.0), axis=0, keepdims=True)
        within = jnp.sum(jnp.where(below & (keys >= cid.astype(F32) * tokens), 1.0, 0.0), axis=0, keepdims=True)
        fits = rank < slots
        slot = jnp.where(fits, group * slots + rank, -1.0)
        slot_ref[...] = slot
        place[...] = jnp.where(iota((sets * slots, tokens), 0) == slot, 1.0, 0.0).astype(BF16)
        lane = jnp.where(fits, group * 128 + rank + 64 * parity_ref[0, 0].astype(F32), -1.0)
        spread = jnp.where(iota((sets * 128, tokens), 0) == lane, 1.0, 0.0).astype(BF16)
        short = jnp.where(jnp.max(rank, axis=1, keepdims=True) >= slots, 1.0, 0.0)
        low = jnp.bitwise_and(pos, 255)
        high = jnp.right_shift(pos, 8) + 1
        row = lax.broadcasted_iota(jnp.int32, (16, tokens), 0)
        facts = jnp.where(
            row == 0,
            high.astype(F32),
            jnp.where(row == 1, low.astype(F32), jnp.where(row == 2, own.astype(F32) + 1.0, jnp.where(row == 3, within, 0.0))),
        ).astype(BF16)
        meta[...] = nt_dot(facts, spread)
        meta[4:5, :] = jnp.broadcast_to(short, (1, sets * 128))

    gap = out_ref.shape[2] - 3 * slots - 8
    for h in range(0, out_ref.shape[1], 2):
        at = slice(h * HEAD_DIM, (h + 2) * HEAD_DIM)
        y = dot(place[...], jnp.concatenate([q_ref[:, at], k_ref[:, at], v_ref[:, at]], axis=1))
        for s in range(sets):
            part = y[s * slots : (s + 1) * slots]
            for u in range(2):
                pieces = [part[:, i * 128 : (i + 1) * 128] for i in (u, u + 2, u + 4)]
                if gap:
                    pieces.append(jnp.zeros((gap, 128), F32))
                pieces.append(meta[0:8, s * 128 : (s + 1) * 128])
                out_ref[s, h + u] = jnp.concatenate(pieces, axis=0).astype(BF16)


def attend_kernel(
    slots, x_hbm, o_hbm, short_ref, x_ref, o_ref, facts_ref, flat, xs, os, code, high, low, tab_v, tab, sem, facts_sem, in_sems, out_sems
):
    sources, rows, _ = x_ref.shape
    step_rows = 4 * UNROLL
    steps = sources // step_rows
    blocks = sources // 4
    facts_in = pltpu.make_async_copy(x_hbm.at[:, rows - 16 : rows, :], facts_ref, facts_sem)
    facts_in.start()

    def part_in(i):
        at = pl.ds(i * step_rows, step_rows)
        return pltpu.make_async_copy(x_hbm.at[at], x_ref.at[at], in_sems.at[i])

    def part_out(i):
        at = pl.ds(i * step_rows, step_rows)
        return pltpu.make_async_copy(o_ref.at[at], o_hbm.at[at], out_sems.at[i])

    for i in range(steps):
        part_in(i).start()
    os[...] = jnp.zeros(os.shape, BF16)
    ahead = 5 * sources // 16
    xs[0 : ahead * BLK, :] = jnp.zeros((ahead * BLK, xs.shape[1]), BF16)
    facts_in.wait()
    total_rows = xs.shape[0]

    flat[...] = facts_ref[...].astype(F32)[:, 8:16].reshape(flat.shape)

    def fact(i):
        return flat[pl.ds(i, sources, 8), :]

    high[...] = fact(0) * 256.0
    low[...] = fact(1)
    own = fact(2)
    within = fact(3)
    short_ref[...] = jnp.broadcast_to(jnp.max(fact(4), axis=0, keepdims=True), (8, 128))
    lane = iota((sources, 128), 1)
    r = lax.broadcasted_iota(jnp.int32, (128, CL_SET * 128), 0)
    s = lax.broadcasted_iota(jnp.int32, (128, CL_SET * 128), 1)
    to_each = jnp.where(r == jnp.right_shift(s, 7), 1.0, 0.0).astype(BF16)
    is_own = [jnp.where(own == c + 1, 1.0, 0.0) for c in range(CL_SET)]
    counts = nt_dot(jnp.concatenate(is_own, axis=1).astype(BF16), to_each).astype(BF16)
    r = lax.broadcasted_iota(jnp.int32, (sources, sources), 0)
    s = lax.broadcasted_iota(jnp.int32, (sources, sources), 1)
    first = jnp.bitwise_and(r, -4)
    masks = [s >= 0, s < r, s < first, s < first + 4]
    sums = dot(jnp.concatenate([jnp.where(m, 1.0, 0.0) for m in masks], axis=0).astype(BF16), counts)
    total, before, before_block, after_block = (sums[i * sources : (i + 1) * sources] for i in range(4))
    nblk = jnp.floor((total + (BLK - 1)) * (1.0 / BLK))
    start_blk = dot(nblk.astype(BF16), jnp.where((r < s) & (r < CL_SET), 1.0, 0.0).astype(BF16))
    skipped = jnp.floor(before_block * (1.0 / 16)) * 16
    shift = dot((before - skipped).astype(BF16), to_each)
    place = within
    for c in range(CL_SET):
        place = place + is_own[c] * shift[:, c * 128 : (c + 1) * 128]
    step = jnp.floor(place * (1.0 / RUN) + (0.5 / RUN))
    code[...] = jnp.where(own > 0.0, step * CODES + (own - 1.0) * RUN + (place - step * RUN) + 1.0, 0.0)
    passes = jnp.where(lane < CL_SET, jnp.floor((after_block - skipped + (RUN - 1)) * (1.0 / RUN)), 0.0)
    most = jnp.max(passes, axis=(0, 1), keepdims=True)
    table = jnp.where(lane < 2 * CL_SET, pltpu.roll(passes, CL_SET, 1), most)
    flat[0:sources] = jnp.where(lane < CL_SET, start_blk * BLK + skipped, table)
    tab_v[0:blocks] = flat[pl.ds(0, blocks, 4), :].astype(jnp.int32)
    tab_v[blocks : blocks + 8] = start_blk[0:8].astype(jnp.int32)
    tab_v[blocks + 8 :] = nblk[0:8].astype(jnp.int32)
    copy = pltpu.make_async_copy(tab_v, tab, sem)
    copy.start()
    copy.wait()
    most_passes = tab[0, 2 * CL_SET]

    def begin_of(c):
        return tab[blocks, c]

    def count_of(c):
        return tab[blocks + 8, c]

    def passes_of(b):
        return functools.reduce(jnp.maximum, [tab[b, CL_SET + c] for c in range(CL_SET)])

    used_blocks = begin_of(CL_SET - 1) + count_of(CL_SET - 1)

    def clear(i, _):
        at = pl.ds(pl.multiple_of(i * BLK, BLK), BLK)
        xs[at, :] = jnp.zeros((BLK, xs.shape[1]), BF16)
        return 0

    lax.fori_loop(ahead, jnp.minimum(used_blocks + 4, total_rows // BLK), clear, 0)

    def joined(ref, b):
        return jnp.concatenate(
            [
                ref[pl.ds(4 * b, 1), :] + ref[pl.ds(4 * b + 1, 1), :],
                ref[pl.ds(4 * b + 2, 1), :] + ref[pl.ds(4 * b + 3, 1), :],
            ],
            axis=1,
        )

    code_rows = iota((CODES, 256), 0)
    which = lax.broadcasted_iota(jnp.int32, (128, 256), 0)

    def compact(b, p):
        x4 = x_ref[pl.ds(4 * b, 4)].astype(F32)
        xcat = jnp.concatenate([x4[:, i * slots : i * slots + 64].reshape(256, 128) for i in range(3)], axis=1).astype(BF16)
        row = joined(code, b) - jnp.asarray(p * CODES + 1, F32)
        where_at = jnp.where(which == 0, joined(high, b), jnp.where(which == 1, joined(low, b), 0.0))
        xcat = jnp.concatenate([xcat, jnp.transpose(where_at).astype(BF16)], axis=1)
        select = jnp.where(code_rows == row, 1.0, 0.0).astype(BF16)
        y = dot(select, xcat).astype(BF16)
        ats = [pl.ds(pl.multiple_of(tab[b, c] + p * RUN, 16), RUN) for c in range(CL_SET)]
        new = [xs[at, :] + y[c * RUN : (c + 1) * RUN] for c, at in enumerate(ats)]
        for at, x in zip(ats, new):
            xs[at, :] = x

    def each_block(body, before=None, after=None):
        def some(i, _):
            if before is not None:
                before(i)
            for u in range(UNROLL):
                body(i * UNROLL + u, 0)

            @pl.when(most_passes > 1)
            def _():
                def rest(u, _):
                    b = i * UNROLL + u

                    def more(p, _):
                        body(b, p)
                        return 0

                    return lax.fori_loop(1, passes_of(b), more, 0)

                lax.fori_loop(0, UNROLL, rest, 0)

            if after is not None:
                after(i)
            return 0

        lax.fori_loop(0, steps, some, 0)

    each_block(compact, before=lambda i: part_in(i).wait())

    scale = HEAD_DIM ** (-0.5) * 1.4426950408889634
    to_lanes = jnp.where(lax.broadcasted_iota(jnp.int32, (16, 128), 1) < 2, 1.0, 0.0).astype(BF16)
    to_all = jnp.where(lax.broadcasted_iota(jnp.int32, (128, 128), 0) < 2, 1.0, 0.0).astype(BF16)

    def key_places(at):
        kp = nt_dot(to_lanes, xs[at, 384:512])[0:1]
        return jnp.where(kp > 0.0, kp, 1e9)

    def hidden(scores, kp, qp):
        lanes = scores.shape[1] // 128
        return jnp.where(kp <= jnp.concatenate([qp] * lanes, axis=1), scores * scale, HIDDEN)

    def fixed(pair, count):
        for c in pair:
            begin, own_count = begin_of(c), count_of(c)
            kat = pl.ds(pl.multiple_of(begin * BLK, BLK), count * BLK)
            keys = xs[kat, 128:256]
            values = xs[kat, 256:384]
            mine = lax.broadcasted_iota(jnp.int32, (1, count * BLK), 1) < own_count * BLK
            kp = jnp.where(mine, key_places(kat), 1e9)
            for i in range(0, count, TILE):
                wide = min(TILE, count - i)
                at = pl.ds(pl.multiple_of((begin + i) * BLK, BLK), wide * BLK)
                scores = hidden(nt_dot(xs[at, 0:128], keys), kp, dot(xs[at, 384:512], to_all))
                weight = jnp.exp2(scores - jnp.max(scores, axis=1, keepdims=True))
                total = jnp.sum(weight, axis=1, keepdims=True)
                os[at, :] = (dot(weight.astype(BF16), values) / total).astype(BF16)

    def general(begin, count):
        def queries(i, _):
            at = pl.ds(pl.multiple_of((begin + i) * BLK, BLK), BLK)
            q = xs[at, 0:128]
            qp = dot(xs[at, 384:512], to_all)

            def keys(j, carried):
                top, total, summed = carried
                kat = pl.ds(pl.multiple_of((begin + j) * BLK, BLK), BLK)
                scores = hidden(nt_dot(q, xs[kat, 128:256]), key_places(kat), qp)
                fresh = jnp.maximum(top, jnp.max(scores, axis=1, keepdims=True))
                weight = jnp.exp2(scores - fresh)
                rescale = jnp.exp2(top - fresh)
                total = total * rescale + jnp.sum(weight, axis=1, keepdims=True)
                summed = summed * rescale + dot(weight.astype(BF16), xs[kat, 256:384])
                return fresh, total, summed

            init = (jnp.full((BLK, 1), HIDDEN, F32), jnp.zeros((BLK, 1), F32), jnp.zeros((BLK, 128), F32))
            _, total, summed = lax.fori_loop(0, count, keys, init)
            os[at, :] = (summed / total).astype(BF16)
            return 0

        lax.fori_loop(0, count, queries, 0)

    def clusters(k, _):
        pair = [JOINT * k + u for u in range(JOINT)]
        counts = [count_of(c) for c in pair]
        most = functools.reduce(jnp.maximum, counts)
        least = functools.reduce(jnp.minimum, counts)
        alike = (most >= FIXED[0]) & (most <= FIXED[-1]) & (least >= most - 2)
        for n in FIXED:
            pl.when(alike & (most == n))(functools.partial(fixed, pair, n))

        @pl.when(jnp.logical_not(alike))
        def _():
            for c, n in zip(pair, counts):
                general(begin_of(c), n)

        return 0

    lax.fori_loop(0, CL_SET // JOINT, clusters, 0)

    code_lanes = iota((256, CODES), 1)

    def spread(b, p):
        col = column(joined(code, b) - jnp.asarray(p * CODES + 1, F32))
        col = jnp.concatenate([col] * (CODES // 128), axis=1)
        cat = jnp.concatenate(
            [os[pl.ds(pl.multiple_of(tab[b, c] + p * RUN, 16), RUN), :] for c in range(CL_SET)], axis=0
        )
        select = jnp.where(code_lanes == col, 1.0, 0.0).astype(BF16)
        new = dot(select, cat).reshape(4, 64, 128)[:, :slots]
        at = pl.ds(4 * b, 4)
        if isinstance(p, int):
            o_ref[at] = new.astype(BF16)
        else:
            o_ref[at] = (o_ref[at].astype(F32) + new).astype(BF16)

    each_block(spread, after=lambda i: part_out(i).start())
    for i in range(steps):
        part_out(i).wait()


def attend_call(slots, got):
    sources = got.shape[0]
    whole = pl.BlockSpec(memory_space=pltpu.VMEM)
    total_rows = sources * slots + (CL_SET + 4) * BLK
    return pl.pallas_call(
        functools.partial(attend_kernel, slots),
        in_specs=[pl.BlockSpec(memory_space=pl.ANY)],
        out_specs=[pl.BlockSpec(memory_space=pl.ANY), whole],
        out_shape=[
            jax.ShapeDtypeStruct((sources, slots, 128), BF16),
            jax.ShapeDtypeStruct((8, 128), F32),
        ],
        scratch_shapes=[
            pltpu.VMEM(got.shape, BF16),
            pltpu.VMEM((sources, slots, 128), BF16),
            pltpu.VMEM((sources, 16, 128), BF16),
            pltpu.VMEM((sources * 8, 128), F32),
            pltpu.VMEM((total_rows, 4 * HEAD_DIM), BF16),
            pltpu.VMEM((total_rows, HEAD_DIM), BF16),
            pltpu.VMEM((sources, 128), F32),
            pltpu.VMEM((sources, 128), F32),
            pltpu.VMEM((sources, 128), F32),
            pltpu.VMEM((sources // 4 + 16, 128), jnp.int32),
            pltpu.SMEM((sources // 4 + 16, 128), jnp.int32),
            pltpu.SemaphoreType.DMA,
            pltpu.SemaphoreType.DMA,
            pltpu.SemaphoreType.DMA((sources // (4 * UNROLL),)),
            pltpu.SemaphoreType.DMA((sources // (4 * UNROLL),)),
        ],
        compiler_params=pltpu.CompilerParams(vmem_limit_bytes=56 * 2**20),
        name="attend",
    )(got)


def unpack_kernel(slots, slot_ref, r_ref, out_ref, select):
    sets, heads = r_ref.shape[0], r_ref.shape[1]

    @pl.when(pl.program_id(0) == 0)
    def _():
        col = column(slot_ref[...])
        col = jnp.concatenate([col] * (-(-sets * slots // 128)), axis=1)[:, : sets * slots]
        select[...] = jnp.where(iota(select.shape, 1) == col, 1.0, 0.0).astype(BF16)

    for h in range(heads):
        x = r_ref[:, h].astype(F32).reshape(sets * slots, 128).astype(BF16)
        out_ref[:, h * 128 : (h + 1) * 128] = dot(select[...], x).astype(BF16)


def pack_call(slots, sets, parity, cid_row, pos_row, queries, keys, values):
    tokens, width = queries.shape
    heads = width // HEAD_DIM
    rows = chunk_rows(slots)
    some = pl.BlockSpec((tokens, PACK * HEAD_DIM), lambda h: (0, h))
    line = pl.BlockSpec((1, tokens), lambda h: (0, 0))
    return pl.pallas_call(
        functools.partial(pack_kernel, slots, sets),
        grid=(heads // PACK,),
        in_specs=[pl.BlockSpec(memory_space=pltpu.SMEM), line, line, some, some, some],
        out_specs=[pl.BlockSpec((sets, PACK, rows, 128), lambda h: (0, h, 0, 0)), line],
        out_shape=[
            jax.ShapeDtypeStruct((sets, heads, rows, 128), BF16),
            jax.ShapeDtypeStruct((1, tokens), F32),
        ],
        scratch_shapes=[pltpu.VMEM((sets * slots, tokens), BF16), pltpu.VMEM((16, sets * 128), F32)],
        compiler_params=pltpu.CompilerParams(vmem_limit_bytes=56 * 2**20),
        name="pack",
    )(parity, cid_row, pos_row, queries, keys, values)


def unpack_call(slots, slot, back):
    sets, heads = back.shape[:2]
    tokens = slot.shape[1]
    return pl.pallas_call(
        functools.partial(unpack_kernel, slots),
        grid=(heads // UNPACK,),
        in_specs=[
            pl.BlockSpec((1, tokens), lambda h: (0, 0)),
            pl.BlockSpec((sets, UNPACK, slots, 128), lambda h: (0, h, 0, 0)),
        ],
        out_specs=pl.BlockSpec((tokens, UNPACK * HEAD_DIM), lambda h: (0, h)),
        out_shape=jax.ShapeDtypeStruct((tokens, heads * HEAD_DIM), BF16),
        scratch_shapes=[pltpu.VMEM((tokens, sets * slots), BF16)],
        compiler_params=pltpu.CompilerParams(vmem_limit_bytes=56 * 2**20),
        name="unpack",
    )(slot, back)


def attention(slots, queries, keys, values, cid_row, pos_row, parity, fallback=None):
    heads = queries.shape[1] // HEAD_DIM
    sources = lax.axis_size("grp") * lax.axis_size("blk")
    sets = sources // heads
    sent, slot = pack_call(slots, sets, parity, cid_row, pos_row, queries, keys, values)
    got = lax.all_to_all(
        sent.reshape(sources, sent.shape[2], 128), ("grp", "blk"), split_axis=0, concat_axis=0, tiled=True
    )
    done, short = attend_call(slots, got)
    back = lax.all_to_all(done, ("grp", "blk"), split_axis=0, concat_axis=0, tiled=True)
    back = back.reshape(sets, heads, slots, 128)
    if fallback is None:
        return unpack_call(slots, slot, back)
    return lax.cond(short[0, 0] > 0.0, fallback, lambda: unpack_call(slots, slot, back))


def local(queries, keys, values, cluster_ids, positions):
    cid_row = cluster_ids.reshape(1, -1)
    pos_row = positions.reshape(1, -1)
    me = lax.axis_index("grp") * lax.axis_size("blk") + lax.axis_index("blk")
    parity = (me % 2).astype(jnp.int32).reshape(1, 1)
    args = (queries, keys, values, cid_row, pos_row, parity)
    return attention(FEW, *args, fallback=lambda: attention(ALL, *args))


def solution(mesh):
    placed = (
        P(("grp", "blk"), None),
        P(("grp", "blk"), None),
        P(("grp", "blk"), None),
        P(("grp", "blk")),
        P(("grp", "blk")),
    )
    return jax.shard_map(
        local, mesh=mesh, in_specs=placed, out_specs=P(("grp", "blk"), None), check_vma=False
    )
```

```python
import functools

import jax
import jax.numpy as jnp
from jax import lax
from jax.experimental import pallas as pl
from jax.experimental.pallas import tpu as pltpu
from jax.sharding import PartitionSpec as P

HEAD_DIM = 128
CL_GRP = 4
CL_SET = 2 * CL_GRP
RUN = 48
CODES = CL_SET * RUN
BLK = 128
FIXED = (4, 5, 6)
UNROLL = 16
TILE = 3
JOINT = 2
ALL = 64
FEW = 56
PACK = 8
UNPACK = 8
F32 = jnp.float32
BF16 = jnp.bfloat16
HIDDEN = -1e30


def chunk_rows(slots):
    return -(-(3 * slots + 8) // 16) * 16


def iota(shape, dim):
    return lax.broadcasted_iota(jnp.int32, shape, dim).astype(F32)


def column(row):
    return jnp.transpose(jnp.broadcast_to(row, (128, row.shape[1])))


def nt_dot(a, b):
    return lax.dot_general(a, b, (((1,), (1,)), ((), ())), preferred_element_type=F32)


def dot(a, b):
    return jnp.dot(a, b, preferred_element_type=F32)


def pack_kernel(slots, sets, parity_ref, cid_ref, pos_ref, q_ref, k_ref, v_ref, out_ref, slot_ref, place, meta):
    tokens = cid_ref.shape[1]

    @pl.when(pl.program_id(0) == 0)
    def _():
        cid = cid_ref[...]
        pos = pos_ref[...]
        own = jnp.bitwise_and(cid, CL_SET - 1)
        group = (cid - own).astype(F32) * (1.0 / CL_SET)
        key = cid.astype(F32) * tokens + iota((1, tokens), 1)
        keys = column(key)
        keys = jnp.concatenate([keys] * (tokens // 128), axis=1)
        below = keys < key
        rank = jnp.sum(jnp.where(below & (keys >= group * (CL_SET * tokens)), 1.0, 0.0), axis=0, keepdims=True)
        within = jnp.sum(jnp.where(below & (keys >= cid.astype(F32) * tokens), 1.0, 0.0), axis=0, keepdims=True)
        fits = rank < slots
        slot = jnp.where(fits, group * slots + rank, -1.0)
        slot_ref[...] = slot
        place[...] = jnp.where(iota((sets * slots, tokens), 0) == slot, 1.0, 0.0).astype(BF16)
        lane = jnp.where(fits, group * 128 + rank + 64 * parity_ref[0, 0].astype(F32), -1.0)
        spread = jnp.where(iota((sets * 128, tokens), 0) == lane, 1.0, 0.0).astype(BF16)
        short = jnp.where(jnp.max(rank, axis=1, keepdims=True) >= slots, 1.0, 0.0)
        low = jnp.bitwise_and(pos, 255)
        high = jnp.right_shift(pos, 8) + 1
        row = lax.broadcasted_iota(jnp.int32, (16, tokens), 0)
        facts = jnp.where(
            row == 0,
            high.astype(F32),
            jnp.where(row == 1, low.astype(F32), jnp.where(row == 2, own.astype(F32) + 1.0, jnp.where(row == 3, within, 0.0))),
        ).astype(BF16)
        meta[...] = nt_dot(facts, spread)
        meta[4:5, :] = jnp.broadcast_to(short, (1, sets * 128))

    gap = out_ref.shape[2] - 3 * slots - 8
    for h in range(0, out_ref.shape[1], 2):
        at = slice(h * HEAD_DIM, (h + 2) * HEAD_DIM)
        y = dot(place[...], jnp.concatenate([q_ref[:, at], k_ref[:, at], v_ref[:, at]], axis=1))
        for s in range(sets):
            part = y[s * slots : (s + 1) * slots]
            for u in range(2):
                pieces = [part[:, i * 128 : (i + 1) * 128] for i in (u, u + 2, u + 4)]
                if gap:
                    pieces.append(jnp.zeros((gap, 128), F32))
                pieces.append(meta[0:8, s * 128 : (s + 1) * 128])
                out_ref[s, h + u] = jnp.concatenate(pieces, axis=0).astype(BF16)


def attend_kernel(
    slots, x_hbm, o_hbm, short_ref, x_ref, o_ref, facts_ref, flat, xs, os, code, high, low, tab_v, tab, sem, facts_sem, in_sems, out_sems
):
    sources, rows, _ = x_ref.shape
    step_rows = 4 * UNROLL
    steps = sources // step_rows
    blocks = sources // 4
    facts_in = pltpu.make_async_copy(x_hbm.at[:, rows - 16 : rows, :], facts_ref, facts_sem)
    facts_in.start()

    def part_in(i):
        at = pl.ds(i * step_rows, step_rows)
        return pltpu.make_async_copy(x_hbm.at[at], x_ref.at[at], in_sems.at[i])

    def part_out(i):
        at = pl.ds(i * step_rows, step_rows)
        return pltpu.make_async_copy(o_ref.at[at], o_hbm.at[at], out_sems.at[i])

    for i in range(steps):
        part_in(i).start()
    os[...] = jnp.zeros(os.shape, BF16)
    ahead = 5 * sources // 16
    xs[0 : ahead * BLK, :] = jnp.zeros((ahead * BLK, xs.shape[1]), BF16)
    facts_in.wait()
    total_rows = xs.shape[0]

    flat[...] = facts_ref[...].astype(F32)[:, 8:16].reshape(flat.shape)

    def fact(i):
        return flat[pl.ds(i, sources, 8), :]

    high[...] = fact(0) * 256.0
    low[...] = fact(1)
    own = fact(2)
    within = fact(3)
    short_ref[...] = jnp.broadcast_to(jnp.max(fact(4), axis=0, keepdims=True), (8, 128))
    lane = iota((sources, 128), 1)
    r = lax.broadcasted_iota(jnp.int32, (128, CL_SET * 128), 0)
    s = lax.broadcasted_iota(jnp.int32, (128, CL_SET * 128), 1)
    to_each = jnp.where(r == jnp.right_shift(s, 7), 1.0, 0.0).astype(BF16)
    is_own = [jnp.where(own == c + 1, 1.0, 0.0) for c in range(CL_SET)]
    counts = nt_dot(jnp.concatenate(is_own, axis=1).astype(BF16), to_each).astype(BF16)
    r = lax.broadcasted_iota(jnp.int32, (sources, sources), 0)
    s = lax.broadcasted_iota(jnp.int32, (sources, sources), 1)
    first = jnp.bitwise_and(r, -4)
    masks = [s >= 0, s < r, s < first, s < first + 4]
    sums = dot(jnp.concatenate([jnp.where(m, 1.0, 0.0) for m in masks], axis=0).astype(BF16), counts)
    total, before, before_block, after_block = (sums[i * sources : (i + 1) * sources] for i in range(4))
    nblk = jnp.floor((total + (BLK - 1)) * (1.0 / BLK))
    start_blk = dot(nblk.astype(BF16), jnp.where((r < s) & (r < CL_SET), 1.0, 0.0).astype(BF16))
    skipped = jnp.floor(before_block * (1.0 / 16)) * 16
    shift = dot((before - skipped).astype(BF16), to_each)
    place = within
    for c in range(CL_SET):
        place = place + is_own[c] * shift[:, c * 128 : (c + 1) * 128]
    step = jnp.floor(place * (1.0 / RUN) + (0.5 / RUN))
    code[...] = jnp.where(own > 0.0, step * CODES + (own - 1.0) * RUN + (place - step * RUN) + 1.0, 0.0)
    passes = jnp.where(lane < CL_SET, jnp.floor((after_block - skipped + (RUN - 1)) * (1.0 / RUN)), 0.0)
    most = jnp.max(passes, axis=(0, 1), keepdims=True)
    table = jnp.where(lane < 2 * CL_SET, pltpu.roll(passes, CL_SET, 1), most)
    flat[0:sources] = jnp.where(lane < CL_SET, start_blk * BLK + skipped, table)
    tab_v[0:blocks] = flat[pl.ds(0, blocks, 4), :].astype(jnp.int32)
    tab_v[blocks : blocks + 8] = start_blk[0:8].astype(jnp.int32)
    tab_v[blocks + 8 :] = nblk[0:8].astype(jnp.int32)
    copy = pltpu.make_async_copy(tab_v, tab, sem)
    copy.start()
    copy.wait()
    most_passes = tab[0, 2 * CL_SET]

    def begin_of(c):
        return tab[blocks, c]

    def count_of(c):
        return tab[blocks + 8, c]

    def passes_of(b):
        return functools.reduce(jnp.maximum, [tab[b, CL_SET + c] for c in range(CL_SET)])

    used_blocks = begin_of(CL_SET - 1) + count_of(CL_SET - 1)

    def clear(i, _):
        at = pl.ds(pl.multiple_of(i * BLK, BLK), BLK)
        xs[at, :] = jnp.zeros((BLK, xs.shape[1]), BF16)
        return 0

    lax.fori_loop(ahead, jnp.minimum(used_blocks + 4, total_rows // BLK), clear, 0)

    def joined(ref, b):
        return jnp.concatenate(
            [
                ref[pl.ds(4 * b, 1), :] + ref[pl.ds(4 * b + 1, 1), :],
                ref[pl.ds(4 * b + 2, 1), :] + ref[pl.ds(4 * b + 3, 1), :],
            ],
            axis=1,
        )

    code_rows = iota((CODES, 256), 0)
    which = lax.broadcasted_iota(jnp.int32, (128, 256), 0)

    def compact(b, p):
        x4 = x_ref[pl.ds(4 * b, 4)].astype(F32)
        xcat = jnp.concatenate([x4[:, i * slots : i * slots + 64].reshape(256, 128) for i in range(3)], axis=1).astype(BF16)
        row = joined(code, b) - jnp.asarray(p * CODES + 1, F32)
        where_at = jnp.where(which == 0, joined(high, b), jnp.where(which == 1, joined(low, b), 0.0))
        xcat = jnp.concatenate([xcat, jnp.transpose(where_at).astype(BF16)], axis=1)
        select = jnp.where(code_rows == row, 1.0, 0.0).astype(BF16)
        y = dot(select, xcat).astype(BF16)
        ats = [pl.ds(pl.multiple_of(tab[b, c] + p * RUN, 16), RUN) for c in range(CL_SET)]
        new = [xs[at, :] + y[c * RUN : (c + 1) * RUN] for c, at in enumerate(ats)]
        for at, x in zip(ats, new):
            xs[at, :] = x

    def each_block(body, before=None, after=None):
        def some(i, _):
            if before is not None:
                before(i)
            for u in range(UNROLL):
                body(i * UNROLL + u, 0)

            @pl.when(most_passes > 1)
            def _():
                def rest(u, _):
                    b = i * UNROLL + u

                    def more(p, _):
                        body(b, p)
                        return 0

                    return lax.fori_loop(1, passes_of(b), more, 0)

                lax.fori_loop(0, UNROLL, rest, 0)

            if after is not None:
                after(i)
            return 0

        lax.fori_loop(0, steps, some, 0)

    each_block(compact, before=lambda i: part_in(i).wait())

    scale = HEAD_DIM ** (-0.5) * 1.4426950408889634
    to_lanes = jnp.where(lax.broadcasted_iota(jnp.int32, (16, 128), 1) < 2, 1.0, 0.0).astype(BF16)
    to_all = jnp.where(lax.broadcasted_iota(jnp.int32, (128, 128), 0) < 2, 1.0, 0.0).astype(BF16)

    def key_places(at):
        kp = nt_dot(to_lanes, xs[at, 384:512])[0:1]
        return jnp.where(kp > 0.0, kp, 1e9)

    def hidden(scores, kp, qp):
        lanes = scores.shape[1] // 128
        return jnp.where(kp <= jnp.concatenate([qp] * lanes, axis=1), scores * scale, HIDDEN)

    def fixed(pair, count):
        for c in pair:
            begin, own_count = begin_of(c), count_of(c)
            kat = pl.ds(pl.multiple_of(begin * BLK, BLK), count * BLK)
            keys = xs[kat, 128:256]
            values = xs[kat, 256:384]
            mine = lax.broadcasted_iota(jnp.int32, (1, count * BLK), 1) < own_count * BLK
            kp = jnp.where(mine, key_places(kat), 1e9)
            for i in range(0, count, TILE):
                wide = min(TILE, count - i)
                at = pl.ds(pl.multiple_of((begin + i) * BLK, BLK), wide * BLK)
                scores = hidden(nt_dot(xs[at, 0:128], keys), kp, dot(xs[at, 384:512], to_all))
                weight = jnp.exp2(scores - jnp.max(scores, axis=1, keepdims=True))
                total = jnp.sum(weight, axis=1, keepdims=True)
                os[at, :] = (dot(weight.astype(BF16), values) / total).astype(BF16)

    def general(begin, count):
        def queries(i, _):
            at = pl.ds(pl.multiple_of((begin + i) * BLK, BLK), BLK)
            q = xs[at, 0:128]
            qp = dot(xs[at, 384:512], to_all)

            def keys(j, carried):
                top, total, summed = carried
                kat = pl.ds(pl.multiple_of((begin + j) * BLK, BLK), BLK)
                scores = hidden(nt_dot(q, xs[kat, 128:256]), key_places(kat), qp)
                fresh = jnp.maximum(top, jnp.max(scores, axis=1, keepdims=True))
                weight = jnp.exp2(scores - fresh)
                rescale = jnp.exp2(top - fresh)
                total = total * rescale + jnp.sum(weight, axis=1, keepdims=True)
                summed = summed * rescale + dot(weight.astype(BF16), xs[kat, 256:384])
                return fresh, total, summed

            init = (jnp.full((BLK, 1), HIDDEN, F32), jnp.zeros((BLK, 1), F32), jnp.zeros((BLK, 128), F32))
            _, total, summed = lax.fori_loop(0, count, keys, init)
            os[at, :] = (summed / total).astype(BF16)
            return 0

        lax.fori_loop(0, count, queries, 0)

    def clusters(k, _):
        pair = [JOINT * k + u for u in range(JOINT)]
        counts = [count_of(c) for c in pair]
        most = functools.reduce(jnp.maximum, counts)
        least = functools.reduce(jnp.minimum, counts)
        alike = (most >= FIXED[0]) & (most <= FIXED[-1]) & (least >= most - 2)
        for n in FIXED:
            pl.when(alike & (most == n))(functools.partial(fixed, pair, n))

        @pl.when(jnp.logical_not(alike))
        def _():
            for c, n in zip(pair, counts):
                general(begin_of(c), n)

        return 0

    lax.fori_loop(0, CL_SET // JOINT, clusters, 0)

    code_lanes = iota((256, CODES), 1)

    def spread(b, p):
        col = column(joined(code, b) - jnp.asarray(p * CODES + 1, F32))
        col = jnp.concatenate([col] * (CODES // 128), axis=1)
        cat = jnp.concatenate(
            [os[pl.ds(pl.multiple_of(tab[b, c] + p * RUN, 16), RUN), :] for c in range(CL_SET)], axis=0
        )
        select = jnp.where(code_lanes == col, 1.0, 0.0).astype(BF16)
        new = dot(select, cat).reshape(4, 64, 128)[:, :slots]
        at = pl.ds(4 * b, 4)
        if isinstance(p, int):
            o_ref[at] = new.astype(BF16)
        else:
            o_ref[at] = (o_ref[at].astype(F32) + new).astype(BF16)

    each_block(spread, after=lambda i: part_out(i).start())
    for i in range(steps):
        part_out(i).wait()


def attend_call(slots, got):
    sources = got.shape[0]
    whole = pl.BlockSpec(memory_space=pltpu.VMEM)
    total_rows = sources * slots + (CL_SET + 4) * BLK
    return pl.pallas_call(
        functools.partial(attend_kernel, slots),
        in_specs=[pl.BlockSpec(memory_space=pl.ANY)],
        out_specs=[pl.BlockSpec(memory_space=pl.ANY), whole],
        out_shape=[
            jax.ShapeDtypeStruct((sources, slots, 128), BF16),
            jax.ShapeDtypeStruct((8, 128), F32),
        ],
        scratch_shapes=[
            pltpu.VMEM(got.shape, BF16),
            pltpu.VMEM((sources, slots, 128), BF16),
            pltpu.VMEM((sources, 16, 128), BF16),
            pltpu.VMEM((sources * 8, 128), F32),
            pltpu.VMEM((total_rows, 4 * HEAD_DIM), BF16),
            pltpu.VMEM((total_rows, HEAD_DIM), BF16),
            pltpu.VMEM((sources, 128), F32),
            pltpu.VMEM((sources, 128), F32),
            pltpu.VMEM((sources, 128), F32),
            pltpu.VMEM((sources // 4 + 16, 128), jnp.int32),
            pltpu.SMEM((sources // 4 + 16, 128), jnp.int32),
            pltpu.SemaphoreType.DMA,
            pltpu.SemaphoreType.DMA,
            pltpu.SemaphoreType.DMA((sources // (4 * UNROLL),)),
            pltpu.SemaphoreType.DMA((sources // (4 * UNROLL),)),
        ],
        compiler_params=pltpu.CompilerParams(vmem_limit_bytes=32 * 2**20),
        name="attend",
    )(got)


def unpack_kernel(slots, slot_ref, r_ref, out_ref, select):
    sets, heads = r_ref.shape[0], r_ref.shape[1]

    @pl.when(pl.program_id(0) == 0)
    def _():
        col = column(slot_ref[...])
        col = jnp.concatenate([col] * (-(-sets * slots // 128)), axis=1)[:, : sets * slots]
        select[...] = jnp.where(iota(select.shape, 1) == col, 1.0, 0.0).astype(BF16)

    for h in range(heads):
        x = r_ref[:, h].astype(F32).reshape(sets * slots, 128).astype(BF16)
        out_ref[:, h * 128 : (h + 1) * 128] = dot(select[...], x).astype(BF16)


def pack_call(slots, sets, parity, cid_row, pos_row, queries, keys, values):
    tokens, width = queries.shape
    heads = width // HEAD_DIM
    rows = chunk_rows(slots)
    some = pl.BlockSpec((tokens, PACK * HEAD_DIM), lambda h: (0, h))
    line = pl.BlockSpec((1, tokens), lambda h: (0, 0))
    return pl.pallas_call(
        functools.partial(pack_kernel, slots, sets),
        grid=(heads // PACK,),
        in_specs=[pl.BlockSpec(memory_space=pltpu.SMEM), line, line, some, some, some],
        out_specs=[pl.BlockSpec((sets, PACK, rows, 128), lambda h: (0, h, 0, 0)), line],
        out_shape=[
            jax.ShapeDtypeStruct((sets, heads, rows, 128), BF16),
            jax.ShapeDtypeStruct((1, tokens), F32),
        ],
        scratch_shapes=[pltpu.VMEM((sets * slots, tokens), BF16), pltpu.VMEM((16, sets * 128), F32)],
        compiler_params=pltpu.CompilerParams(vmem_limit_bytes=20 * 2**20),
        name="pack",
    )(parity, cid_row, pos_row, queries, keys, values)


def unpack_call(slots, slot, back):
    sets, heads = back.shape[:2]
    tokens = slot.shape[1]
    return pl.pallas_call(
        functools.partial(unpack_kernel, slots),
        grid=(heads // UNPACK,),
        in_specs=[
            pl.BlockSpec((1, tokens), lambda h: (0, 0)),
            pl.BlockSpec((sets, UNPACK, slots, 128), lambda h: (0, h, 0, 0)),
        ],
        out_specs=pl.BlockSpec((tokens, UNPACK * HEAD_DIM), lambda h: (0, h)),
        out_shape=jax.ShapeDtypeStruct((tokens, heads * HEAD_DIM), BF16),
        scratch_shapes=[pltpu.VMEM((tokens, sets * slots), BF16)],
        compiler_params=pltpu.CompilerParams(vmem_limit_bytes=16 * 2**20),
        name="unpack",
    )(slot, back)


def attention(slots, queries, keys, values, cid_row, pos_row, parity, fallback=None):
    heads = queries.shape[1] // HEAD_DIM
    sources = lax.axis_size("grp") * lax.axis_size("blk")
    sets = sources // heads
    sent, slot = pack_call(slots, sets, parity, cid_row, pos_row, queries, keys, values)
    got = lax.all_to_all(
        sent.reshape(sources, sent.shape[2], 128), ("grp", "blk"), split_axis=0, concat_axis=0, tiled=True
    )
    done, short = attend_call(slots, got)
    back = lax.all_to_all(done, ("grp", "blk"), split_axis=0, concat_axis=0, tiled=True)
    back = back.reshape(sets, heads, slots, 128)
    if fallback is None:
        return unpack_call(slots, slot, back)
    return lax.cond(short[0, 0] > 0.0, fallback, lambda: unpack_call(slots, slot, back))


def local(queries, keys, values, cluster_ids, positions):
    cid_row = cluster_ids.reshape(1, -1)
    pos_row = positions.reshape(1, -1)
    me = lax.axis_index("grp") * lax.axis_size("blk") + lax.axis_index("blk")
    parity = (me % 2).astype(jnp.int32).reshape(1, 1)
    args = (queries, keys, values, cid_row, pos_row, parity)
    return attention(FEW, *args, fallback=lambda: attention(ALL, *args))


def solution(mesh):
    placed = (
        P(("grp", "blk"), None),
        P(("grp", "blk"), None),
        P(("grp", "blk"), None),
        P(("grp", "blk")),
        P(("grp", "blk")),
    )
    return jax.shard_map(
        local, mesh=mesh, in_specs=placed, out_specs=P(("grp", "blk"), None), check_vma=False
    )
```

```python
import functools

import jax
import jax.numpy as jnp
from jax import lax
from jax.experimental import pallas as pl
from jax.experimental.pallas import tpu as pltpu
from jax.sharding import PartitionSpec as P

HEAD_DIM = 128
CL_GRP = 4
CL_SET = 2 * CL_GRP
RUN = 48
CODES = CL_SET * RUN
BLK = 128
FIXED = (4, 5, 6)
UNROLL = 16
TILE = 3
JOINT = 2
ALL = 64
FEW = 56
PACK = 8
UNPACK = 8
F32 = jnp.float32
BF16 = jnp.bfloat16
HIDDEN = -1e30


def chunk_rows(slots):
    return -(-(3 * slots + 8) // 16) * 16


def iota(shape, dim):
    return lax.broadcasted_iota(jnp.int32, shape, dim).astype(F32)


def column(row):
    return jnp.transpose(jnp.broadcast_to(row, (128, row.shape[1])))


def nt_dot(a, b):
    return lax.dot_general(a, b, (((1,), (1,)), ((), ())), preferred_element_type=F32)


def dot(a, b):
    return jnp.dot(a, b, preferred_element_type=F32)


def pack_kernel(slots, sets, parity_ref, cid_ref, pos_ref, q_ref, k_ref, v_ref, out_ref, slot_ref, place, meta):
    tokens = cid_ref.shape[1]

    @pl.when(pl.program_id(0) == 0)
    def _():
        cid = cid_ref[...]
        pos = pos_ref[...]
        own = jnp.bitwise_and(cid, CL_SET - 1)
        group = (cid - own).astype(F32) * (1.0 / CL_SET)
        key = cid.astype(F32) * tokens + iota((1, tokens), 1)
        keys = column(key)
        keys = jnp.concatenate([keys] * (tokens // 128), axis=1)
        below = keys < key
        rank = jnp.sum(jnp.where(below & (keys >= group * (CL_SET * tokens)), 1.0, 0.0), axis=0, keepdims=True)
        within = jnp.sum(jnp.where(below & (keys >= cid.astype(F32) * tokens), 1.0, 0.0), axis=0, keepdims=True)
        fits = rank < slots
        slot = jnp.where(fits, group * slots + rank, -1.0)
        slot_ref[...] = slot
        place[...] = jnp.where(iota((sets * slots, tokens), 0) == slot, 1.0, 0.0).astype(BF16)
        lane = jnp.where(fits, group * 128 + rank + 64 * parity_ref[0, 0].astype(F32), -1.0)
        spread = jnp.where(iota((sets * 128, tokens), 0) == lane, 1.0, 0.0).astype(BF16)
        short = jnp.where(jnp.max(rank, axis=1, keepdims=True) >= slots, 1.0, 0.0)
        low = jnp.bitwise_and(pos, 255)
        high = jnp.right_shift(pos, 8) + 1
        row = lax.broadcasted_iota(jnp.int32, (16, tokens), 0)
        facts = jnp.where(
            row == 0,
            high.astype(F32),
            jnp.where(row == 1, low.astype(F32), jnp.where(row == 2, own.astype(F32) + 1.0, jnp.where(row == 3, within, 0.0))),
        ).astype(BF16)
        meta[...] = nt_dot(facts, spread)
        meta[4:5, :] = jnp.broadcast_to(short, (1, sets * 128))

    gap = out_ref.shape[2] - 3 * slots - 8
    for h in range(0, out_ref.shape[1], 2):
        at = slice(h * HEAD_DIM, (h + 2) * HEAD_DIM)
        y = dot(place[...], jnp.concatenate([q_ref[:, at], k_ref[:, at], v_ref[:, at]], axis=1))
        for s in range(sets):
            part = y[s * slots : (s + 1) * slots]
            for u in range(2):
                pieces = [part[:, i * 128 : (i + 1) * 128] for i in (u, u + 2, u + 4)]
                if gap:
                    pieces.append(jnp.zeros((gap, 128), F32))
                pieces.append(meta[0:8, s * 128 : (s + 1) * 128])
                out_ref[s, h + u] = jnp.concatenate(pieces, axis=0).astype(BF16)


def attend_kernel(slots, x_ref, o_ref, short_ref, flat, xs, os, code, high, low, tab_v, tab, sem):
    sources, rows, _ = x_ref.shape
    blocks = sources // 4
    total_rows = xs.shape[0]
    os[...] = jnp.zeros(os.shape, BF16)
    ahead = 5 * sources // 16
    xs[0 : ahead * BLK, :] = jnp.zeros((ahead * BLK, xs.shape[1]), BF16)
    flat[...] = x_ref[:, rows - 16 : rows, :].astype(F32)[:, 8:16].reshape(flat.shape)

    def fact(i):
        return flat[pl.ds(i, sources, 8), :]

    high[...] = fact(0) * 256.0
    low[...] = fact(1)
    own = fact(2)
    within = fact(3)
    short_ref[...] = jnp.broadcast_to(jnp.max(fact(4), axis=0, keepdims=True), (8, 128))
    lane = iota((sources, 128), 1)
    r = lax.broadcasted_iota(jnp.int32, (128, CL_SET * 128), 0)
    s = lax.broadcasted_iota(jnp.int32, (128, CL_SET * 128), 1)
    to_each = jnp.where(r == jnp.right_shift(s, 7), 1.0, 0.0).astype(BF16)
    is_own = [jnp.where(own == c + 1, 1.0, 0.0) for c in range(CL_SET)]
    counts = nt_dot(jnp.concatenate(is_own, axis=1).astype(BF16), to_each).astype(BF16)
    r = lax.broadcasted_iota(jnp.int32, (sources, sources), 0)
    s = lax.broadcasted_iota(jnp.int32, (sources, sources), 1)
    first = jnp.bitwise_and(r, -4)
    masks = [s >= 0, s < r, s < first, s < first + 4]
    sums = dot(jnp.concatenate([jnp.where(m, 1.0, 0.0) for m in masks], axis=0).astype(BF16), counts)
    total, before, before_block, after_block = (sums[i * sources : (i + 1) * sources] for i in range(4))
    nblk = jnp.floor((total + (BLK - 1)) * (1.0 / BLK))
    start_blk = dot(nblk.astype(BF16), jnp.where((r < s) & (r < CL_SET), 1.0, 0.0).astype(BF16))
    skipped = jnp.floor(before_block * (1.0 / 16)) * 16
    shift = dot((before - skipped).astype(BF16), to_each)
    place = within
    for c in range(CL_SET):
        place = place + is_own[c] * shift[:, c * 128 : (c + 1) * 128]
    step = jnp.floor(place * (1.0 / RUN) + (0.5 / RUN))
    code[...] = jnp.where(own > 0.0, step * CODES + (own - 1.0) * RUN + (place - step * RUN) + 1.0, 0.0)
    passes = jnp.where(lane < CL_SET, jnp.floor((after_block - skipped + (RUN - 1)) * (1.0 / RUN)), 0.0)
    most = jnp.max(passes, axis=(0, 1), keepdims=True)
    table = jnp.where(lane < 2 * CL_SET, pltpu.roll(passes, CL_SET, 1), most)
    flat[0:sources] = jnp.where(lane < CL_SET, start_blk * BLK + skipped, table)
    tab_v[0:blocks] = flat[pl.ds(0, blocks, 4), :].astype(jnp.int32)
    tab_v[blocks : blocks + 8] = start_blk[0:8].astype(jnp.int32)
    tab_v[blocks + 8 :] = nblk[0:8].astype(jnp.int32)
    copy = pltpu.make_async_copy(tab_v, tab, sem)
    copy.start()
    copy.wait()
    most_passes = tab[0, 2 * CL_SET]

    def begin_of(c):
        return tab[blocks, c]

    def count_of(c):
        return tab[blocks + 8, c]

    def passes_of(b):
        return functools.reduce(jnp.maximum, [tab[b, CL_SET + c] for c in range(CL_SET)])

    used_blocks = begin_of(CL_SET - 1) + count_of(CL_SET - 1)

    def clear(i, _):
        at = pl.ds(pl.multiple_of(i * BLK, BLK), BLK)
        xs[at, :] = jnp.zeros((BLK, xs.shape[1]), BF16)
        return 0

    lax.fori_loop(ahead, jnp.minimum(used_blocks + 4, total_rows // BLK), clear, 0)

    def joined(ref, b):
        return jnp.concatenate(
            [
                ref[pl.ds(4 * b, 1), :] + ref[pl.ds(4 * b + 1, 1), :],
                ref[pl.ds(4 * b + 2, 1), :] + ref[pl.ds(4 * b + 3, 1), :],
            ],
            axis=1,
        )

    code_rows = iota((CODES, 256), 0)
    which = lax.broadcasted_iota(jnp.int32, (128, 256), 0)

    def compact(b, p):
        x4 = x_ref[pl.ds(4 * b, 4)].astype(F32)
        xcat = jnp.concatenate([x4[:, i * slots : i * slots + 64].reshape(256, 128) for i in range(3)], axis=1).astype(BF16)
        row = joined(code, b) - jnp.asarray(p * CODES + 1, F32)
        where_at = jnp.where(which == 0, joined(high, b), jnp.where(which == 1, joined(low, b), 0.0))
        xcat = jnp.concatenate([xcat, jnp.transpose(where_at).astype(BF16)], axis=1)
        select = jnp.where(code_rows == row, 1.0, 0.0).astype(BF16)
        y = dot(select, xcat).astype(BF16)
        ats = [pl.ds(pl.multiple_of(tab[b, c] + p * RUN, 16), RUN) for c in range(CL_SET)]
        new = [xs[at, :] + y[c * RUN : (c + 1) * RUN] for c, at in enumerate(ats)]
        for at, x in zip(ats, new):
            xs[at, :] = x

    def each_block(body):
        def some(i, _):
            for u in range(UNROLL):
                body(i * UNROLL + u, 0)

            @pl.when(most_passes > 1)
            def _():
                def rest(u, _):
                    b = i * UNROLL + u

                    def more(p, _):
                        body(b, p)
                        return 0

                    return lax.fori_loop(1, passes_of(b), more, 0)

                lax.fori_loop(0, UNROLL, rest, 0)

            return 0

        lax.fori_loop(0, blocks // UNROLL, some, 0)

    each_block(compact)

    scale = HEAD_DIM ** (-0.5) * 1.4426950408889634
    to_lanes = jnp.where(lax.broadcasted_iota(jnp.int32, (16, 128), 1) < 2, 1.0, 0.0).astype(BF16)
    to_all = jnp.where(lax.broadcasted_iota(jnp.int32, (128, 128), 0) < 2, 1.0, 0.0).astype(BF16)

    def key_places(at):
        kp = nt_dot(to_lanes, xs[at, 384:512])[0:1]
        return jnp.where(kp > 0.0, kp, 1e9)

    def hidden(scores, kp, qp):
        lanes = scores.shape[1] // 128
        return jnp.where(kp <= jnp.concatenate([qp] * lanes, axis=1), scores * scale, HIDDEN)

    def fixed(pair, count):
        for c in pair:
            begin, own_count = begin_of(c), count_of(c)
            kat = pl.ds(pl.multiple_of(begin * BLK, BLK), count * BLK)
            keys = xs[kat, 128:256]
            values = xs[kat, 256:384]
            mine = lax.broadcasted_iota(jnp.int32, (1, count * BLK), 1) < own_count * BLK
            kp = jnp.where(mine, key_places(kat), 1e9)
            for i in range(0, count, TILE):
                wide = min(TILE, count - i)
                at = pl.ds(pl.multiple_of((begin + i) * BLK, BLK), wide * BLK)
                scores = hidden(nt_dot(xs[at, 0:128], keys), kp, dot(xs[at, 384:512], to_all))
                weight = jnp.exp2(scores - jnp.max(scores, axis=1, keepdims=True))
                total = jnp.sum(weight, axis=1, keepdims=True)
                os[at, :] = (dot(weight.astype(BF16), values) / total).astype(BF16)

    def general(begin, count):
        def queries(i, _):
            at = pl.ds(pl.multiple_of((begin + i) * BLK, BLK), BLK)
            q = xs[at, 0:128]
            qp = dot(xs[at, 384:512], to_all)

            def keys(j, carried):
                top, total, summed = carried
                kat = pl.ds(pl.multiple_of((begin + j) * BLK, BLK), BLK)
                scores = hidden(nt_dot(q, xs[kat, 128:256]), key_places(kat), qp)
                fresh = jnp.maximum(top, jnp.max(scores, axis=1, keepdims=True))
                weight = jnp.exp2(scores - fresh)
                rescale = jnp.exp2(top - fresh)
                total = total * rescale + jnp.sum(weight, axis=1, keepdims=True)
                summed = summed * rescale + dot(weight.astype(BF16), xs[kat, 256:384])
                return fresh, total, summed

            init = (jnp.full((BLK, 1), HIDDEN, F32), jnp.zeros((BLK, 1), F32), jnp.zeros((BLK, 128), F32))
            _, total, summed = lax.fori_loop(0, count, keys, init)
            os[at, :] = (summed / total).astype(BF16)
            return 0

        lax.fori_loop(0, count, queries, 0)

    def clusters(k, _):
        pair = [JOINT * k + u for u in range(JOINT)]
        counts = [count_of(c) for c in pair]
        most = functools.reduce(jnp.maximum, counts)
        least = functools.reduce(jnp.minimum, counts)
        alike = (most >= FIXED[0]) & (most <= FIXED[-1]) & (least >= most - 2)
        for n in FIXED:
            pl.when(alike & (most == n))(functools.partial(fixed, pair, n))

        @pl.when(jnp.logical_not(alike))
        def _():
            for c, n in zip(pair, counts):
                general(begin_of(c), n)

        return 0

    lax.fori_loop(0, CL_SET // JOINT, clusters, 0)

    code_lanes = iota((256, CODES), 1)

    def spread(b, p):
        col = column(joined(code, b) - jnp.asarray(p * CODES + 1, F32))
        col = jnp.concatenate([col] * (CODES // 128), axis=1)
        cat = jnp.concatenate(
            [os[pl.ds(pl.multiple_of(tab[b, c] + p * RUN, 16), RUN), :] for c in range(CL_SET)], axis=0
        )
        select = jnp.where(code_lanes == col, 1.0, 0.0).astype(BF16)
        new = dot(select, cat).reshape(4, 64, 128)[:, :slots]
        at = pl.ds(4 * b, 4)
        if isinstance(p, int):
            o_ref[at] = new.astype(BF16)
        else:
            o_ref[at] = (o_ref[at].astype(F32) + new).astype(BF16)

    each_block(spread)


def attend_call(slots, got):
    sources = got.shape[0]
    whole = pl.BlockSpec(memory_space=pltpu.VMEM)
    total_rows = sources * slots + (CL_SET + 4) * BLK
    return pl.pallas_call(
        functools.partial(attend_kernel, slots),
        in_specs=[whole],
        out_specs=[whole, whole],
        out_shape=[
            pltpu.VMEM((sources, slots, 128), BF16),
            jax.ShapeDtypeStruct((8, 128), F32),
        ],
        scratch_shapes=[
            pltpu.VMEM((sources * 8, 128), F32),
            pltpu.VMEM((total_rows, 4 * HEAD_DIM), BF16),
            pltpu.VMEM((total_rows, HEAD_DIM), BF16),
            pltpu.VMEM((sources, 128), F32),
            pltpu.VMEM((sources, 128), F32),
            pltpu.VMEM((sources, 128), F32),
            pltpu.VMEM((sources // 4 + 16, 128), jnp.int32),
            pltpu.SMEM((sources // 4 + 16, 128), jnp.int32),
            pltpu.SemaphoreType.DMA,
        ],
        compiler_params=pltpu.CompilerParams(vmem_limit_bytes=32 * 2**20),
        name="attend",
    )(pltpu.with_memory_space_constraint(got, pltpu.VMEM))


def unpack_kernel(slots, slot_ref, r_ref, out_ref, select):
    sets, heads = r_ref.shape[0], r_ref.shape[1]

    @pl.when(pl.program_id(0) == 0)
    def _():
        col = column(slot_ref[...])
        col = jnp.concatenate([col] * (-(-sets * slots // 128)), axis=1)[:, : sets * slots]
        select[...] = jnp.where(iota(select.shape, 1) == col, 1.0, 0.0).astype(BF16)

    for h in range(heads):
        x = r_ref[:, h].astype(F32).reshape(sets * slots, 128).astype(BF16)
        out_ref[:, h * 128 : (h + 1) * 128] = dot(select[...], x).astype(BF16)


def pack_call(slots, sets, parity, cid_row, pos_row, queries, keys, values):
    tokens, width = queries.shape
    heads = width // HEAD_DIM
    rows = chunk_rows(slots)
    some = pl.BlockSpec((tokens, PACK * HEAD_DIM), lambda h: (0, h))
    line = pl.BlockSpec((1, tokens), lambda h: (0, 0))
    return pl.pallas_call(
        functools.partial(pack_kernel, slots, sets),
        grid=(heads // PACK,),
        in_specs=[pl.BlockSpec(memory_space=pltpu.SMEM), line, line, some, some, some],
        out_specs=[pl.BlockSpec((sets, PACK, rows, 128), lambda h: (0, h, 0, 0)), line],
        out_shape=[
            jax.ShapeDtypeStruct((sets, heads, rows, 128), BF16),
            jax.ShapeDtypeStruct((1, tokens), F32),
        ],
        scratch_shapes=[pltpu.VMEM((sets * slots, tokens), BF16), pltpu.VMEM((16, sets * 128), F32)],
        compiler_params=pltpu.CompilerParams(vmem_limit_bytes=20 * 2**20),
        name="pack",
    )(parity, cid_row, pos_row, queries, keys, values)


def unpack_call(slots, slot, back):
    sets, heads = back.shape[:2]
    tokens = slot.shape[1]
    return pl.pallas_call(
        functools.partial(unpack_kernel, slots),
        grid=(heads // UNPACK,),
        in_specs=[
            pl.BlockSpec((1, tokens), lambda h: (0, 0)),
            pl.BlockSpec((sets, UNPACK, slots, 128), lambda h: (0, h, 0, 0)),
        ],
        out_specs=pl.BlockSpec((tokens, UNPACK * HEAD_DIM), lambda h: (0, h)),
        out_shape=jax.ShapeDtypeStruct((tokens, heads * HEAD_DIM), BF16),
        scratch_shapes=[pltpu.VMEM((tokens, sets * slots), BF16)],
        compiler_params=pltpu.CompilerParams(vmem_limit_bytes=16 * 2**20),
        name="unpack",
    )(slot, back)


def attention(slots, queries, keys, values, cid_row, pos_row, parity, fallback=None):
    heads = queries.shape[1] // HEAD_DIM
    sources = lax.axis_size("grp") * lax.axis_size("blk")
    sets = sources // heads
    sent, slot = pack_call(slots, sets, parity, cid_row, pos_row, queries, keys, values)
    got = lax.all_to_all(
        sent.reshape(sources, sent.shape[2], 128), ("grp", "blk"), split_axis=0, concat_axis=0, tiled=True
    )
    done, short = attend_call(slots, got)
    back = lax.all_to_all(done, ("grp", "blk"), split_axis=0, concat_axis=0, tiled=True)
    back = back.reshape(sets, heads, slots, 128)
    if fallback is None:
        return unpack_call(slots, slot, back)
    return lax.cond(short[0, 0] > 0.0, fallback, lambda: unpack_call(slots, slot, back))


def local(queries, keys, values, cluster_ids, positions):
    cid_row = cluster_ids.reshape(1, -1)
    pos_row = positions.reshape(1, -1)
    me = lax.axis_index("grp") * lax.axis_size("blk") + lax.axis_index("blk")
    parity = (me % 2).astype(jnp.int32).reshape(1, 1)
    args = (queries, keys, values, cid_row, pos_row, parity)
    return attention(FEW, *args, fallback=lambda: attention(ALL, *args))


def solution(mesh):
    placed = (
        P(("grp", "blk"), None),
        P(("grp", "blk"), None),
        P(("grp", "blk"), None),
        P(("grp", "blk")),
        P(("grp", "blk")),
    )
    return jax.shard_map(
        local, mesh=mesh, in_specs=placed, out_specs=P(("grp", "blk"), None), check_vma=False
    )
```

```python
import functools

import jax
import jax.numpy as jnp
from jax import lax
from jax.experimental import pallas as pl
from jax.experimental.pallas import tpu as pltpu
from jax.sharding import PartitionSpec as P

HEAD_DIM = 128
CL_GRP = 4
CL_SET = 2 * CL_GRP
RUN = 48
CODES = CL_SET * RUN
BLK = 128
FIXED = (4, 5, 6, 7)
UNROLL = 16
TILE = 3
JOINT = 2
ALL = 64
FEW = 56
PACK = 4
UNPACK = 8
F32 = jnp.float32
BF16 = jnp.bfloat16
HIDDEN = -1e30


def chunk_rows(slots):
    return -(-(3 * slots + 8) // 16) * 16


def iota(shape, dim):
    return lax.broadcasted_iota(jnp.int32, shape, dim).astype(F32)


def column(row):
    return jnp.transpose(jnp.broadcast_to(row, (128, row.shape[1])))


def nt_dot(a, b):
    return lax.dot_general(a, b, (((1,), (1,)), ((), ())), preferred_element_type=F32)


def dot(a, b):
    return jnp.dot(a, b, preferred_element_type=F32)


def pack_kernel(slots, sets, parity_ref, cid_ref, pos_ref, q_hbm, k_hbm, v_hbm, out_ref, slot_ref, x_ref, place, meta, sems):
    tokens = cid_ref.shape[1]
    heads = out_ref.shape[1]
    steps = heads // PACK

    def part_in(i, j):
        at = pl.ds(i * PACK * HEAD_DIM, PACK * HEAD_DIM)
        return pltpu.make_async_copy((q_hbm, k_hbm, v_hbm)[j].at[:, at], x_ref.at[j, :, at], sems.at[i, j])

    for i in range(steps):
        for j in range(3):
            part_in(i, j).start()

    cid = cid_ref[...]
    pos = pos_ref[...]
    own = jnp.bitwise_and(cid, CL_SET - 1)
    group = (cid - own).astype(F32) * (1.0 / CL_SET)
    key = cid.astype(F32) * tokens + iota((1, tokens), 1)
    keys = column(key)
    keys = jnp.concatenate([keys] * (tokens // 128), axis=1)
    below = keys < key
    rank = jnp.sum(jnp.where(below & (keys >= group * (CL_SET * tokens)), 1.0, 0.0), axis=0, keepdims=True)
    within = jnp.sum(jnp.where(below & (keys >= cid.astype(F32) * tokens), 1.0, 0.0), axis=0, keepdims=True)
    fits = rank < slots
    slot = jnp.where(fits, group * slots + rank, -1.0)
    slot_ref[...] = slot
    place[...] = jnp.where(iota((sets * slots, tokens), 0) == slot, 1.0, 0.0).astype(BF16)
    lane = jnp.where(fits, group * 128 + rank + 64 * parity_ref[0, 0].astype(F32), -1.0)
    spread = jnp.where(iota((sets * 128, tokens), 0) == lane, 1.0, 0.0).astype(BF16)
    short = jnp.where(jnp.max(rank, axis=1, keepdims=True) >= slots, 1.0, 0.0)
    low = jnp.bitwise_and(pos, 255)
    high = jnp.right_shift(pos, 8) + 1
    row = lax.broadcasted_iota(jnp.int32, (16, tokens), 0)
    facts = jnp.where(
        row == 0,
        high.astype(F32),
        jnp.where(row == 1, low.astype(F32), jnp.where(row == 2, own.astype(F32) + 1.0, jnp.where(row == 3, within, 0.0))),
    ).astype(BF16)
    meta[...] = nt_dot(facts, spread)
    meta[4:5, :] = jnp.broadcast_to(short, (1, sets * 128))

    gap = out_ref.shape[2] - 3 * slots - 8
    for h in range(0, heads, 2):
        if h % PACK == 0:
            for j in range(3):
                part_in(h // PACK, j).wait()
        at = slice(h * HEAD_DIM, (h + 2) * HEAD_DIM)
        y = dot(place[...], jnp.concatenate([x_ref[j, :, at] for j in range(3)], axis=1))
        for s in range(sets):
            part = y[s * slots : (s + 1) * slots]
            for u in range(2):
                pieces = [part[:, i * 128 : (i + 1) * 128] for i in (u, u + 2, u + 4)]
                if gap:
                    pieces.append(jnp.zeros((gap, 128), F32))
                pieces.append(meta[0:8, s * 128 : (s + 1) * 128])
                out_ref[s, h + u] = jnp.concatenate(pieces, axis=0).astype(BF16)


def attend_kernel(slots, x_ref, o_ref, short_ref, flat, xs, os, code, high, low, tab_v, tab, sem):
    sources, rows, _ = x_ref.shape
    blocks = sources // 4
    total_rows = xs.shape[0]
    os[...] = jnp.zeros(os.shape, BF16)
    ahead = 5 * sources // 16
    xs[0 : ahead * BLK, :] = jnp.zeros((ahead * BLK, xs.shape[1]), BF16)
    flat[...] = x_ref[:, rows - 16 : rows, :].astype(F32)[:, 8:16].reshape(flat.shape)

    def fact(i):
        return flat[pl.ds(i, sources, 8), :]

    high[...] = fact(0) * 256.0
    low[...] = fact(1)
    own = fact(2)
    within = fact(3)
    short_ref[...] = jnp.broadcast_to(jnp.max(fact(4), axis=0, keepdims=True), (8, 128))
    lane = iota((sources, 128), 1)
    r = lax.broadcasted_iota(jnp.int32, (128, CL_SET * 128), 0)
    s = lax.broadcasted_iota(jnp.int32, (128, CL_SET * 128), 1)
    to_each = jnp.where(r == jnp.right_shift(s, 7), 1.0, 0.0).astype(BF16)
    is_own = [jnp.where(own == c + 1, 1.0, 0.0) for c in range(CL_SET)]
    counts = nt_dot(jnp.concatenate(is_own, axis=1).astype(BF16), to_each).astype(BF16)
    r = lax.broadcasted_iota(jnp.int32, (sources, sources), 0)
    s = lax.broadcasted_iota(jnp.int32, (sources, sources), 1)
    first = jnp.bitwise_and(r, -4)
    masks = [s >= 0, s < r, s < first, s < first + 4]
    sums = dot(jnp.concatenate([jnp.where(m, 1.0, 0.0) for m in masks], axis=0).astype(BF16), counts)
    total, before, before_block, after_block = (sums[i * sources : (i + 1) * sources] for i in range(4))
    nblk = jnp.floor((total + (BLK - 1)) * (1.0 / BLK))
    start_blk = dot(nblk.astype(BF16), jnp.where((r < s) & (r < CL_SET), 1.0, 0.0).astype(BF16))
    skipped = jnp.floor(before_block * (1.0 / 16)) * 16
    shift = dot((before - skipped).astype(BF16), to_each)
    place = within
    for c in range(CL_SET):
        place = place + is_own[c] * shift[:, c * 128 : (c + 1) * 128]
    step = jnp.floor(place * (1.0 / RUN) + (0.5 / RUN))
    code[...] = jnp.where(own > 0.0, step * CODES + (own - 1.0) * RUN + (place - step * RUN) + 1.0, 0.0)
    passes = jnp.where(lane < CL_SET, jnp.floor((after_block - skipped + (RUN - 1)) * (1.0 / RUN)), 0.0)
    most = jnp.max(passes, axis=(0, 1), keepdims=True)
    table = jnp.where(lane < 2 * CL_SET, pltpu.roll(passes, CL_SET, 1), most)
    flat[0:sources] = jnp.where(lane < CL_SET, start_blk * BLK + skipped, table)
    tab_v[0:blocks] = flat[pl.ds(0, blocks, 4), :].astype(jnp.int32)
    tab_v[blocks : blocks + 8] = start_blk[0:8].astype(jnp.int32)
    tab_v[blocks + 8 :] = nblk[0:8].astype(jnp.int32)
    copy = pltpu.make_async_copy(tab_v, tab, sem)
    copy.start()
    copy.wait()
    most_passes = tab[0, 2 * CL_SET]

    def begin_of(c):
        return tab[blocks, c]

    def count_of(c):
        return tab[blocks + 8, c]

    def passes_of(b):
        return functools.reduce(jnp.maximum, [tab[b, CL_SET + c] for c in range(CL_SET)])

    used_blocks = begin_of(CL_SET - 1) + count_of(CL_SET - 1)

    def clear(i, _):
        at = pl.ds(pl.multiple_of(i * BLK, BLK), BLK)
        xs[at, :] = jnp.zeros((BLK, xs.shape[1]), BF16)
        return 0

    lax.fori_loop(ahead, jnp.minimum(used_blocks + 4, total_rows // BLK), clear, 0)

    def joined(ref, b):
        return jnp.concatenate(
            [
                ref[pl.ds(4 * b, 1), :] + ref[pl.ds(4 * b + 1, 1), :],
                ref[pl.ds(4 * b + 2, 1), :] + ref[pl.ds(4 * b + 3, 1), :],
            ],
            axis=1,
        )

    code_rows = iota((CODES, 256), 0)
    which = lax.broadcasted_iota(jnp.int32, (128, 256), 0)

    def compact(b, p):
        x4 = x_ref[pl.ds(4 * b, 4)].astype(F32)
        xcat = jnp.concatenate([x4[:, i * slots : i * slots + 64].reshape(256, 128) for i in range(3)], axis=1).astype(BF16)
        row = joined(code, b) - jnp.asarray(p * CODES + 1, F32)
        where_at = jnp.where(which == 0, joined(high, b), jnp.where(which == 1, joined(low, b), 0.0))
        xcat = jnp.concatenate([xcat, jnp.transpose(where_at).astype(BF16)], axis=1)
        select = jnp.where(code_rows == row, 1.0, 0.0).astype(BF16)
        y = dot(select, xcat).astype(BF16)
        ats = [pl.ds(pl.multiple_of(tab[b, c] + p * RUN, 16), RUN) for c in range(CL_SET)]
        new = [xs[at, :] + y[c * RUN : (c + 1) * RUN] for c, at in enumerate(ats)]
        for at, x in zip(ats, new):
            xs[at, :] = x

    def each_block(body):
        def some(i, _):
            for u in range(UNROLL):
                body(i * UNROLL + u, 0)

            @pl.when(most_passes > 1)
            def _():
                def rest(u, _):
                    b = i * UNROLL + u

                    def more(p, _):
                        body(b, p)
                        return 0

                    return lax.fori_loop(1, passes_of(b), more, 0)

                lax.fori_loop(0, UNROLL, rest, 0)

            return 0

        lax.fori_loop(0, blocks // UNROLL, some, 0)

    each_block(compact)

    scale = HEAD_DIM ** (-0.5) * 1.4426950408889634
    to_lanes = jnp.where(lax.broadcasted_iota(jnp.int32, (16, 128), 1) < 2, 1.0, 0.0).astype(BF16)
    to_all = jnp.where(lax.broadcasted_iota(jnp.int32, (128, 128), 0) < 2, 1.0, 0.0).astype(BF16)

    def key_places(at):
        kp = nt_dot(to_lanes, xs[at, 384:512])[0:1]
        return jnp.where(kp > 0.0, kp, 1e9)

    def hidden(scores, kp, qp):
        lanes = scores.shape[1] // 128
        return jnp.where(kp <= jnp.concatenate([qp] * lanes, axis=1), scores * scale, HIDDEN)

    def fixed(pair, count):
        for c in pair:
            begin, own_count = begin_of(c), count_of(c)
            kat = pl.ds(pl.multiple_of(begin * BLK, BLK), count * BLK)
            keys = xs[kat, 128:256]
            values = xs[kat, 256:384]
            mine = lax.broadcasted_iota(jnp.int32, (1, count * BLK), 1) < own_count * BLK
            kp = jnp.where(mine, key_places(kat), 1e9)
            for i in range(0, count, TILE):
                wide = min(TILE, count - i)
                at = pl.ds(pl.multiple_of((begin + i) * BLK, BLK), wide * BLK)
                scores = hidden(nt_dot(xs[at, 0:128], keys), kp, dot(xs[at, 384:512], to_all))
                weight = jnp.exp2(scores - jnp.max(scores, axis=1, keepdims=True))
                total = jnp.sum(weight, axis=1, keepdims=True)
                os[at, :] = (dot(weight.astype(BF16), values) / total).astype(BF16)

    def general(begin, count):
        def queries(i, _):
            at = pl.ds(pl.multiple_of((begin + i) * BLK, BLK), BLK)
            q = xs[at, 0:128]
            qp = dot(xs[at, 384:512], to_all)

            def keys(j, carried):
                top, total, summed = carried
                kat = pl.ds(pl.multiple_of((begin + j) * BLK, BLK), BLK)
                scores = hidden(nt_dot(q, xs[kat, 128:256]), key_places(kat), qp)
                fresh = jnp.maximum(top, jnp.max(scores, axis=1, keepdims=True))
                weight = jnp.exp2(scores - fresh)
                rescale = jnp.exp2(top - fresh)
                total = total * rescale + jnp.sum(weight, axis=1, keepdims=True)
                summed = summed * rescale + dot(weight.astype(BF16), xs[kat, 256:384])
                return fresh, total, summed

            init = (jnp.full((BLK, 1), HIDDEN, F32), jnp.zeros((BLK, 1), F32), jnp.zeros((BLK, 128), F32))
            _, total, summed = lax.fori_loop(0, count, keys, init)
            os[at, :] = (summed / total).astype(BF16)
            return 0

        lax.fori_loop(0, count, queries, 0)

    def clusters(k, _):
        pair = [JOINT * k + u for u in range(JOINT)]
        counts = [count_of(c) for c in pair]
        most = functools.reduce(jnp.maximum, counts)
        least = functools.reduce(jnp.minimum, counts)
        alike = (most >= FIXED[0]) & (most <= FIXED[-1]) & (least >= most - 2)
        for n in FIXED:
            pl.when(alike & (most == n))(functools.partial(fixed, pair, n))

        @pl.when(jnp.logical_not(alike))
        def _():
            for c, n in zip(pair, counts):
                general(begin_of(c), n)

        return 0

    lax.fori_loop(0, CL_SET // JOINT, clusters, 0)

    code_lanes = iota((256, CODES), 1)

    def spread(b, p):
        col = column(joined(code, b) - jnp.asarray(p * CODES + 1, F32))
        col = jnp.concatenate([col] * (CODES // 128), axis=1)
        cat = jnp.concatenate(
            [os[pl.ds(pl.multiple_of(tab[b, c] + p * RUN, 16), RUN), :] for c in range(CL_SET)], axis=0
        )
        select = jnp.where(code_lanes == col, 1.0, 0.0).astype(BF16)
        new = dot(select, cat).reshape(4, 64, 128)[:, :slots]
        at = pl.ds(4 * b, 4)
        if isinstance(p, int):
            o_ref[at] = new.astype(BF16)
        else:
            o_ref[at] = (o_ref[at].astype(F32) + new).astype(BF16)

    each_block(spread)


def attend_call(slots, got):
    sources = got.shape[0]
    whole = pl.BlockSpec(memory_space=pltpu.VMEM)
    total_rows = sources * slots + (CL_SET + 4) * BLK
    return pl.pallas_call(
        functools.partial(attend_kernel, slots),
        in_specs=[whole],
        out_specs=[whole, whole],
        out_shape=[
            pltpu.VMEM((sources, slots, 128), BF16),
            jax.ShapeDtypeStruct((8, 128), F32),
        ],
        scratch_shapes=[
            pltpu.VMEM((sources * 8, 128), F32),
            pltpu.VMEM((total_rows, 4 * HEAD_DIM), BF16),
            pltpu.VMEM((total_rows, HEAD_DIM), BF16),
            pltpu.VMEM((sources, 128), F32),
            pltpu.VMEM((sources, 128), F32),
            pltpu.VMEM((sources, 128), F32),
            pltpu.VMEM((sources // 4 + 16, 128), jnp.int32),
            pltpu.SMEM((sources // 4 + 16, 128), jnp.int32),
            pltpu.SemaphoreType.DMA,
        ],
        compiler_params=pltpu.CompilerParams(vmem_limit_bytes=32 * 2**20),
        name="attend",
    )(pltpu.with_memory_space_constraint(got, pltpu.VMEM))


def unpack_kernel(slots, slot_ref, r_ref, out_ref, select):
    sets, heads = r_ref.shape[0], r_ref.shape[1]

    @pl.when(pl.program_id(0) == 0)
    def _():
        col = column(slot_ref[...])
        col = jnp.concatenate([col] * (-(-sets * slots // 128)), axis=1)[:, : sets * slots]
        select[...] = jnp.where(iota(select.shape, 1) == col, 1.0, 0.0).astype(BF16)

    for h in range(heads):
        x = r_ref[:, h].astype(F32).reshape(sets * slots, 128).astype(BF16)
        out_ref[:, h * 128 : (h + 1) * 128] = dot(select[...], x).astype(BF16)


def pack_call(slots, sets, parity, cid_row, pos_row, queries, keys, values):
    tokens, width = queries.shape
    heads = width // HEAD_DIM
    rows = chunk_rows(slots)
    far = pl.BlockSpec(memory_space=pl.ANY)
    near = pl.BlockSpec(memory_space=pltpu.VMEM)
    return pl.pallas_call(
        functools.partial(pack_kernel, slots, sets),
        in_specs=[pl.BlockSpec(memory_space=pltpu.SMEM), near, near, far, far, far],
        out_specs=[near, near],
        out_shape=[
            pltpu.VMEM((sets, heads, rows, 128), BF16),
            jax.ShapeDtypeStruct((1, tokens), F32),
        ],
        scratch_shapes=[
            pltpu.VMEM((3, tokens, width), BF16),
            pltpu.VMEM((sets * slots, tokens), BF16),
            pltpu.VMEM((16, sets * 128), F32),
            pltpu.SemaphoreType.DMA((heads // PACK, 3)),
        ],
        compiler_params=pltpu.CompilerParams(vmem_limit_bytes=20 * 2**20),
        name="pack",
    )(parity, cid_row, pos_row, queries, keys, values)


def unpack_call(slots, slot, back):
    sets, heads = back.shape[:2]
    tokens = slot.shape[1]
    return pl.pallas_call(
        functools.partial(unpack_kernel, slots),
        grid=(heads // UNPACK,),
        in_specs=[
            pl.BlockSpec((1, tokens), lambda h: (0, 0)),
            pl.BlockSpec((sets, UNPACK, slots, 128), lambda h: (0, h, 0, 0)),
        ],
        out_specs=pl.BlockSpec((tokens, UNPACK * HEAD_DIM), lambda h: (0, h)),
        out_shape=pltpu.HBM((tokens, heads * HEAD_DIM), BF16),
        scratch_shapes=[pltpu.VMEM((tokens, sets * slots), BF16)],
        compiler_params=pltpu.CompilerParams(vmem_limit_bytes=16 * 2**20),
        name="unpack",
    )(slot, back)


def attention(slots, queries, keys, values, cid_row, pos_row, parity, fallback=None):
    heads = queries.shape[1] // HEAD_DIM
    sources = lax.axis_size("grp") * lax.axis_size("blk")
    sets = sources // heads
    sent, slot = pack_call(slots, sets, parity, cid_row, pos_row, queries, keys, values)
    got = lax.all_to_all(
        sent.reshape(sources, sent.shape[2], 128), ("grp", "blk"), split_axis=0, concat_axis=0, tiled=True
    )
    done, short = attend_call(slots, got)
    back = lax.all_to_all(done, ("grp", "blk"), split_axis=0, concat_axis=0, tiled=True)
    back = back.reshape(sets, heads, slots, 128)
    if fallback is None:
        return unpack_call(slots, slot, back)
    return lax.cond(short[0, 0] > 0.0, fallback, lambda: unpack_call(slots, slot, back))


def local(queries, keys, values, cluster_ids, positions):
    cid_row = cluster_ids.reshape(1, -1)
    pos_row = positions.reshape(1, -1)
    me = lax.axis_index("grp") * lax.axis_size("blk") + lax.axis_index("blk")
    parity = (me % 2).astype(jnp.int32).reshape(1, 1)
    args = (queries, keys, values, cid_row, pos_row, parity)
    return attention(FEW, *args, fallback=lambda: attention(ALL, *args))


def solution(mesh):
    placed = (
        P(("grp", "blk"), None),
        P(("grp", "blk"), None),
        P(("grp", "blk"), None),
        P(("grp", "blk")),
        P(("grp", "blk")),
    )
    return jax.shard_map(
        local, mesh=mesh, in_specs=placed, out_specs=P(("grp", "blk"), None), check_vma=False
    )
```

```python
import functools

import jax
import jax.numpy as jnp
from jax import lax
from jax.experimental import pallas as pl
from jax.experimental.pallas import tpu as pltpu
from jax.sharding import PartitionSpec as P

HEAD_DIM = 128
CL_GRP = 4
CL_SET = 2 * CL_GRP
RUN = 48
CODES = CL_SET * RUN
BLK = 128
FIXED = (4, 5, 6, 7)
UNROLL = 16
TILE = 3
JOINT = 2
ALL = 64
FEW = 56
PACK = 8
UNPACK = 8
F32 = jnp.float32
BF16 = jnp.bfloat16
HIDDEN = -1e30


def chunk_rows(slots):
    return -(-(3 * slots + 8) // 16) * 16


def iota(shape, dim):
    return lax.broadcasted_iota(jnp.int32, shape, dim).astype(F32)


def column(row):
    return jnp.transpose(jnp.broadcast_to(row, (128, row.shape[1])))


def nt_dot(a, b):
    return lax.dot_general(a, b, (((1,), (1,)), ((), ())), preferred_element_type=F32)


def dot(a, b):
    return jnp.dot(a, b, preferred_element_type=F32)


def pack_kernel(slots, sets, parity_ref, cid_ref, pos_ref, q_ref, k_ref, v_ref, out_ref, slot_ref, place, meta):
    tokens = cid_ref.shape[1]

    @pl.when(pl.program_id(0) == 0)
    def _():
        cid = cid_ref[...]
        pos = pos_ref[...]
        own = jnp.bitwise_and(cid, CL_SET - 1)
        group = (cid - own).astype(F32) * (1.0 / CL_SET)
        key = cid.astype(F32) * tokens + iota((1, tokens), 1)
        keys = column(key)
        keys = jnp.concatenate([keys] * (tokens // 128), axis=1)
        below = keys < key
        rank = jnp.sum(jnp.where(below & (keys >= group * (CL_SET * tokens)), 1.0, 0.0), axis=0, keepdims=True)
        within = jnp.sum(jnp.where(below & (keys >= cid.astype(F32) * tokens), 1.0, 0.0), axis=0, keepdims=True)
        fits = rank < slots
        slot = jnp.where(fits, group * slots + rank, -1.0)
        slot_ref[...] = slot
        place[...] = jnp.where(iota((sets * slots, tokens), 0) == slot, 1.0, 0.0).astype(BF16)
        lane = jnp.where(fits, group * 128 + rank + 64 * parity_ref[0, 0].astype(F32), -1.0)
        spread = jnp.where(iota((sets * 128, tokens), 0) == lane, 1.0, 0.0).astype(BF16)
        short = jnp.where(jnp.max(rank, axis=1, keepdims=True) >= slots, 1.0, 0.0)
        low = jnp.bitwise_and(pos, 255)
        high = jnp.right_shift(pos, 8) + 1
        row = lax.broadcasted_iota(jnp.int32, (16, tokens), 0)
        facts = jnp.where(
            row == 0,
            high.astype(F32),
            jnp.where(row == 1, low.astype(F32), jnp.where(row == 2, own.astype(F32) + 1.0, jnp.where(row == 3, within, 0.0))),
        ).astype(BF16)
        meta[...] = nt_dot(facts, spread)
        meta[4:5, :] = jnp.broadcast_to(short, (1, sets * 128))

    gap = out_ref.shape[2] - 3 * slots - 8
    for h in range(0, out_ref.shape[1], 2):
        at = slice(h * HEAD_DIM, (h + 2) * HEAD_DIM)
        y = dot(place[...], jnp.concatenate([q_ref[:, at], k_ref[:, at], v_ref[:, at]], axis=1))
        for s in range(sets):
            part = y[s * slots : (s + 1) * slots]
            for u in range(2):
                pieces = [part[:, i * 128 : (i + 1) * 128] for i in (u, u + 2, u + 4)]
                if gap:
                    pieces.append(jnp.zeros((gap, 128), F32))
                pieces.append(meta[0:8, s * 128 : (s + 1) * 128])
                out_ref[s, h + u] = jnp.concatenate(pieces, axis=0).astype(BF16)


def attend_kernel(slots, x_ref, o_ref, short_ref, flat, xs, os, code, high, low, tab_v, tab, sem):
    sources, rows, _ = x_ref.shape
    blocks = sources // 4
    total_rows = xs.shape[0]
    os[...] = jnp.zeros(os.shape, BF16)
    ahead = 5 * sources // 16
    xs[0 : ahead * BLK, :] = jnp.zeros((ahead * BLK, xs.shape[1]), BF16)
    flat[...] = x_ref[:, rows - 16 : rows, :].astype(F32)[:, 8:16].reshape(flat.shape)

    def fact(i):
        return flat[pl.ds(i, sources, 8), :]

    high[...] = fact(0) * 256.0
    low[...] = fact(1)
    own = fact(2)
    within = fact(3)
    short_ref[...] = jnp.broadcast_to(jnp.max(fact(4), axis=0, keepdims=True), (8, 128))
    lane = iota((sources, 128), 1)
    r = lax.broadcasted_iota(jnp.int32, (128, CL_SET * 128), 0)
    s = lax.broadcasted_iota(jnp.int32, (128, CL_SET * 128), 1)
    to_each = jnp.where(r == jnp.right_shift(s, 7), 1.0, 0.0).astype(BF16)
    is_own = [jnp.where(own == c + 1, 1.0, 0.0) for c in range(CL_SET)]
    counts = nt_dot(jnp.concatenate(is_own, axis=1).astype(BF16), to_each).astype(BF16)
    r = lax.broadcasted_iota(jnp.int32, (sources, sources), 0)
    s = lax.broadcasted_iota(jnp.int32, (sources, sources), 1)
    first = jnp.bitwise_and(r, -4)
    masks = [s >= 0, s < r, s < first, s < first + 4]
    sums = dot(jnp.concatenate([jnp.where(m, 1.0, 0.0) for m in masks], axis=0).astype(BF16), counts)
    total, before, before_block, after_block = (sums[i * sources : (i + 1) * sources] for i in range(4))
    nblk = jnp.floor((total + (BLK - 1)) * (1.0 / BLK))
    start_blk = dot(nblk.astype(BF16), jnp.where((r < s) & (r < CL_SET), 1.0, 0.0).astype(BF16))
    skipped = jnp.floor(before_block * (1.0 / 16)) * 16
    shift = dot((before - skipped).astype(BF16), to_each)
    place = within
    for c in range(CL_SET):
        place = place + is_own[c] * shift[:, c * 128 : (c + 1) * 128]
    step = jnp.floor(place * (1.0 / RUN) + (0.5 / RUN))
    code[...] = jnp.where(own > 0.0, step * CODES + (own - 1.0) * RUN + (place - step * RUN) + 1.0, 0.0)
    passes = jnp.where(lane < CL_SET, jnp.floor((after_block - skipped + (RUN - 1)) * (1.0 / RUN)), 0.0)
    most = jnp.max(passes, axis=(0, 1), keepdims=True)
    table = jnp.where(lane < 2 * CL_SET, pltpu.roll(passes, CL_SET, 1), most)
    flat[0:sources] = jnp.where(lane < CL_SET, start_blk * BLK + skipped, table)
    tab_v[0:blocks] = flat[pl.ds(0, blocks, 4), :].astype(jnp.int32)
    tab_v[blocks : blocks + 8] = start_blk[0:8].astype(jnp.int32)
    tab_v[blocks + 8 :] = nblk[0:8].astype(jnp.int32)
    copy = pltpu.make_async_copy(tab_v, tab, sem)
    copy.start()
    copy.wait()
    most_passes = tab[0, 2 * CL_SET]

    def begin_of(c):
        return tab[blocks, c]

    def count_of(c):
        return tab[blocks + 8, c]

    def passes_of(b):
        return functools.reduce(jnp.maximum, [tab[b, CL_SET + c] for c in range(CL_SET)])

    used_blocks = begin_of(CL_SET - 1) + count_of(CL_SET - 1)

    def clear(i, _):
        at = pl.ds(pl.multiple_of(i * BLK, BLK), BLK)
        xs[at, :] = jnp.zeros((BLK, xs.shape[1]), BF16)
        return 0

    lax.fori_loop(ahead, jnp.minimum(used_blocks + 4, total_rows // BLK), clear, 0)

    def joined(ref, b):
        return jnp.concatenate(
            [
                ref[pl.ds(4 * b, 1), :] + ref[pl.ds(4 * b + 1, 1), :],
                ref[pl.ds(4 * b + 2, 1), :] + ref[pl.ds(4 * b + 3, 1), :],
            ],
            axis=1,
        )

    code_rows = iota((CODES, 256), 0)
    which = lax.broadcasted_iota(jnp.int32, (128, 256), 0)

    def compact(b, p):
        x4 = x_ref[pl.ds(4 * b, 4)].astype(F32)
        xcat = jnp.concatenate([x4[:, i * slots : i * slots + 64].reshape(256, 128) for i in range(3)], axis=1).astype(BF16)
        row = joined(code, b) - jnp.asarray(p * CODES + 1, F32)
        where_at = jnp.where(which == 0, joined(high, b), jnp.where(which == 1, joined(low, b), 0.0))
        xcat = jnp.concatenate([xcat, jnp.transpose(where_at).astype(BF16)], axis=1)
        select = jnp.where(code_rows == row, 1.0, 0.0).astype(BF16)
        y = dot(select, xcat).astype(BF16)
        ats = [pl.ds(pl.multiple_of(tab[b, c] + p * RUN, 16), RUN) for c in range(CL_SET)]
        new = [xs[at, :] + y[c * RUN : (c + 1) * RUN] for c, at in enumerate(ats)]
        for at, x in zip(ats, new):
            xs[at, :] = x

    def each_block(body):
        def some(i, _):
            for u in range(UNROLL):
                body(i * UNROLL + u, 0)

            @pl.when(most_passes > 1)
            def _():
                def rest(u, _):
                    b = i * UNROLL + u

                    def more(p, _):
                        body(b, p)
                        return 0

                    return lax.fori_loop(1, passes_of(b), more, 0)

                lax.fori_loop(0, UNROLL, rest, 0)

            return 0

        lax.fori_loop(0, blocks // UNROLL, some, 0)

    each_block(compact)

    scale = HEAD_DIM ** (-0.5) * 1.4426950408889634
    to_lanes = jnp.where(lax.broadcasted_iota(jnp.int32, (16, 128), 1) < 2, 1.0, 0.0).astype(BF16)
    to_all = jnp.where(lax.broadcasted_iota(jnp.int32, (128, 128), 0) < 2, 1.0, 0.0).astype(BF16)

    def key_places(at):
        kp = nt_dot(to_lanes, xs[at, 384:512])[0:1]
        return jnp.where(kp > 0.0, kp, 1e9)

    def hidden(scores, kp, qp):
        lanes = scores.shape[1] // 128
        return jnp.where(kp <= jnp.concatenate([qp] * lanes, axis=1), scores * scale, HIDDEN)

    def fixed(pair, count):
        for c in pair:
            begin, own_count = begin_of(c), count_of(c)
            kat = pl.ds(pl.multiple_of(begin * BLK, BLK), count * BLK)
            keys = xs[kat, 128:256]
            values = xs[kat, 256:384]
            mine = lax.broadcasted_iota(jnp.int32, (1, count * BLK), 1) < own_count * BLK
            kp = jnp.where(mine, key_places(kat), 1e9)
            for i in range(0, count, TILE):
                wide = min(TILE, count - i)
                at = pl.ds(pl.multiple_of((begin + i) * BLK, BLK), wide * BLK)
                scores = hidden(nt_dot(xs[at, 0:128], keys), kp, dot(xs[at, 384:512], to_all))
                weight = jnp.exp2(scores - jnp.max(scores, axis=1, keepdims=True))
                total = jnp.sum(weight, axis=1, keepdims=True)
                os[at, :] = (dot(weight.astype(BF16), values) / total).astype(BF16)

    def general(begin, count):
        def queries(i, _):
            at = pl.ds(pl.multiple_of((begin + i) * BLK, BLK), BLK)
            q = xs[at, 0:128]
            qp = dot(xs[at, 384:512], to_all)

            def keys(j, carried):
                top, total, summed = carried
                kat = pl.ds(pl.multiple_of((begin + j) * BLK, BLK), BLK)
                scores = hidden(nt_dot(q, xs[kat, 128:256]), key_places(kat), qp)
                fresh = jnp.maximum(top, jnp.max(scores, axis=1, keepdims=True))
                weight = jnp.exp2(scores - fresh)
                rescale = jnp.exp2(top - fresh)
                total = total * rescale + jnp.sum(weight, axis=1, keepdims=True)
                summed = summed * rescale + dot(weight.astype(BF16), xs[kat, 256:384])
                return fresh, total, summed

            init = (jnp.full((BLK, 1), HIDDEN, F32), jnp.zeros((BLK, 1), F32), jnp.zeros((BLK, 128), F32))
            _, total, summed = lax.fori_loop(0, count, keys, init)
            os[at, :] = (summed / total).astype(BF16)
            return 0

        lax.fori_loop(0, count, queries, 0)

    def clusters(k, _):
        pair = [JOINT * k + u for u in range(JOINT)]
        counts = [count_of(c) for c in pair]
        most = functools.reduce(jnp.maximum, counts)
        least = functools.reduce(jnp.minimum, counts)
        alike = (most >= FIXED[0]) & (most <= FIXED[-1]) & (least >= most - 2)
        for n in FIXED:
            pl.when(alike & (most == n))(functools.partial(fixed, pair, n))

        @pl.when(jnp.logical_not(alike))
        def _():
            for c, n in zip(pair, counts):
                general(begin_of(c), n)

        return 0

    lax.fori_loop(0, CL_SET // JOINT, clusters, 0)

    code_lanes = iota((256, CODES), 1)

    def spread(b, p):
        col = column(joined(code, b) - jnp.asarray(p * CODES + 1, F32))
        col = jnp.concatenate([col] * (CODES // 128), axis=1)
        cat = jnp.concatenate(
            [os[pl.ds(pl.multiple_of(tab[b, c] + p * RUN, 16), RUN), :] for c in range(CL_SET)], axis=0
        )
        select = jnp.where(code_lanes == col, 1.0, 0.0).astype(BF16)
        new = dot(select, cat).reshape(4, 64, 128)[:, :slots]
        at = pl.ds(4 * b, 4)
        if isinstance(p, int):
            o_ref[at] = new.astype(BF16)
        else:
            o_ref[at] = (o_ref[at].astype(F32) + new).astype(BF16)

    each_block(spread)


def attend_call(slots, got):
    sources = got.shape[0]
    whole = pl.BlockSpec(memory_space=pltpu.VMEM)
    total_rows = sources * slots + (CL_SET + 4) * BLK
    return pl.pallas_call(
        functools.partial(attend_kernel, slots),
        in_specs=[whole],
        out_specs=[whole, whole],
        out_shape=[
            pltpu.VMEM((sources, slots, 128), BF16),
            jax.ShapeDtypeStruct((8, 128), F32),
        ],
        scratch_shapes=[
            pltpu.VMEM((sources * 8, 128), F32),
            pltpu.VMEM((total_rows, 4 * HEAD_DIM), BF16),
            pltpu.VMEM((total_rows, HEAD_DIM), BF16),
            pltpu.VMEM((sources, 128), F32),
            pltpu.VMEM((sources, 128), F32),
            pltpu.VMEM((sources, 128), F32),
            pltpu.VMEM((sources // 4 + 16, 128), jnp.int32),
            pltpu.SMEM((sources // 4 + 16, 128), jnp.int32),
            pltpu.SemaphoreType.DMA,
        ],
        compiler_params=pltpu.CompilerParams(vmem_limit_bytes=32 * 2**20),
        name="attend",
    )(pltpu.with_memory_space_constraint(got, pltpu.VMEM))


def unpack_kernel(slots, slot_ref, r_ref, out_ref, select):
    sets, heads = r_ref.shape[0], r_ref.shape[1]

    @pl.when(pl.program_id(0) == 0)
    def _():
        col = column(slot_ref[...])
        col = jnp.concatenate([col] * (-(-sets * slots // 128)), axis=1)[:, : sets * slots]
        select[...] = jnp.where(iota(select.shape, 1) == col, 1.0, 0.0).astype(BF16)

    for h in range(heads):
        x = r_ref[:, h].astype(F32).reshape(sets * slots, 128).astype(BF16)
        out_ref[:, h * 128 : (h + 1) * 128] = dot(select[...], x).astype(BF16)


def pack_call(slots, sets, parity, cid_row, pos_row, queries, keys, values):
    tokens, width = queries.shape
    heads = width // HEAD_DIM
    rows = chunk_rows(slots)
    some = pl.BlockSpec((tokens, PACK * HEAD_DIM), lambda h: (0, h))
    line = pl.BlockSpec((1, tokens), lambda h: (0, 0))
    return pl.pallas_call(
        functools.partial(pack_kernel, slots, sets),
        grid=(heads // PACK,),
        in_specs=[pl.BlockSpec(memory_space=pltpu.SMEM), line, line, some, some, some],
        out_specs=[pl.BlockSpec((sets, PACK, rows, 128), lambda h: (0, h, 0, 0)), line],
        out_shape=[
            jax.ShapeDtypeStruct((sets, heads, rows, 128), BF16),
            jax.ShapeDtypeStruct((1, tokens), F32),
        ],
        scratch_shapes=[pltpu.VMEM((sets * slots, tokens), BF16), pltpu.VMEM((16, sets * 128), F32)],
        compiler_params=pltpu.CompilerParams(vmem_limit_bytes=20 * 2**20),
        name="pack",
    )(parity, cid_row, pos_row, queries, keys, values)


def unpack_call(slots, slot, back):
    sets, heads = back.shape[:2]
    tokens = slot.shape[1]
    return pl.pallas_call(
        functools.partial(unpack_kernel, slots),
        grid=(heads // UNPACK,),
        in_specs=[
            pl.BlockSpec((1, tokens), lambda h: (0, 0)),
            pl.BlockSpec((sets, UNPACK, slots, 128), lambda h: (0, h, 0, 0)),
        ],
        out_specs=pl.BlockSpec((tokens, UNPACK * HEAD_DIM), lambda h: (0, h)),
        out_shape=jax.ShapeDtypeStruct((tokens, heads * HEAD_DIM), BF16),
        scratch_shapes=[pltpu.VMEM((tokens, sets * slots), BF16)],
        compiler_params=pltpu.CompilerParams(vmem_limit_bytes=16 * 2**20),
        name="unpack",
    )(slot, back)


def attention(slots, queries, keys, values, cid_row, pos_row, parity, fallback=None):
    heads = queries.shape[1] // HEAD_DIM
    sources = lax.axis_size("grp") * lax.axis_size("blk")
    sets = sources // heads
    sent, slot = pack_call(slots, sets, parity, cid_row, pos_row, queries, keys, values)
    got = lax.all_to_all(
        sent.reshape(sources, sent.shape[2], 128), ("grp", "blk"), split_axis=0, concat_axis=0, tiled=True
    )
    done, short = attend_call(slots, got)
    back = lax.all_to_all(done, ("grp", "blk"), split_axis=0, concat_axis=0, tiled=True)
    back = back.reshape(sets, heads, slots, 128)
    if fallback is None:
        return unpack_call(slots, slot, back)
    return lax.cond(short[0, 0] > 0.0, fallback, lambda: unpack_call(slots, slot, back))


def local(queries, keys, values, cluster_ids, positions):
    cid_row = cluster_ids.reshape(1, -1)
    pos_row = positions.reshape(1, -1)
    me = lax.axis_index("grp") * lax.axis_size("blk") + lax.axis_index("blk")
    parity = (me % 2).astype(jnp.int32).reshape(1, 1)
    args = (queries, keys, values, cid_row, pos_row, parity)
    return attention(FEW, *args, fallback=lambda: attention(ALL, *args))


def solution(mesh):
    placed = (
        P(("grp", "blk"), None),
        P(("grp", "blk"), None),
        P(("grp", "blk"), None),
        P(("grp", "blk")),
        P(("grp", "blk")),
    )
    return jax.shard_map(
        local, mesh=mesh, in_specs=placed, out_specs=P(("grp", "blk"), None), check_vma=False
    )
```

```python
import functools

import jax
import jax.numpy as jnp
from jax import lax
from jax.experimental import pallas as pl
from jax.experimental.pallas import tpu as pltpu
from jax.sharding import PartitionSpec as P

HEAD_DIM = 128
CL_GRP = 4
CL_SET = 2 * CL_GRP
RUN = 48
CODES = CL_SET * RUN
BLK = 128
FIXED = (4, 5, 6, 7)
FIXED_SHORT = (6,)
UNROLL = 16
TILE = 3
JOINT = 2
ALL = 64
FEW = 56
PACK = 8
UNPACK = 8
F32 = jnp.float32
BF16 = jnp.bfloat16
HIDDEN = -1e30


def chunk_rows(slots):
    return -(-(3 * slots + 8) // 16) * 16


def iota(shape, dim):
    return lax.broadcasted_iota(jnp.int32, shape, dim).astype(F32)


def column(row):
    return jnp.transpose(jnp.broadcast_to(row, (128, row.shape[1])))


def nt_dot(a, b):
    return lax.dot_general(a, b, (((1,), (1,)), ((), ())), preferred_element_type=F32)


def dot(a, b):
    return jnp.dot(a, b, preferred_element_type=F32)


def pack_kernel(slots, sets, parity_ref, cid_ref, pos_ref, q_ref, k_ref, v_ref, out_ref, slot_ref, place, meta):
    tokens = cid_ref.shape[1]

    @pl.when(pl.program_id(0) == 0)
    def _():
        cid = cid_ref[...]
        pos = pos_ref[...]
        own = jnp.bitwise_and(cid, CL_SET - 1)
        group = (cid - own).astype(F32) * (1.0 / CL_SET)
        key = cid.astype(F32) * tokens + iota((1, tokens), 1)
        keys = column(key)
        keys = jnp.concatenate([keys] * (tokens // 128), axis=1)
        below = keys < key
        rank = jnp.sum(jnp.where(below & (keys >= group * (CL_SET * tokens)), 1.0, 0.0), axis=0, keepdims=True)
        within = jnp.sum(jnp.where(below & (keys >= cid.astype(F32) * tokens), 1.0, 0.0), axis=0, keepdims=True)
        fits = rank < slots
        slot = jnp.where(fits, group * slots + rank, -1.0)
        slot_ref[...] = slot
        place[...] = jnp.where(iota((sets * slots, tokens), 0) == slot, 1.0, 0.0).astype(BF16)
        lane = jnp.where(fits, group * 128 + rank + 64 * parity_ref[0, 0].astype(F32), -1.0)
        spread = jnp.where(iota((sets * 128, tokens), 0) == lane, 1.0, 0.0).astype(BF16)
        short = jnp.where(jnp.max(rank, axis=1, keepdims=True) >= slots, 1.0, 0.0)
        low = jnp.bitwise_and(pos, 255)
        high = jnp.right_shift(pos, 8) + 1
        row = lax.broadcasted_iota(jnp.int32, (16, tokens), 0)
        facts = jnp.where(
            row == 0,
            high.astype(F32),
            jnp.where(row == 1, low.astype(F32), jnp.where(row == 2, own.astype(F32) + 1.0, jnp.where(row == 3, within, 0.0))),
        ).astype(BF16)
        meta[...] = nt_dot(facts, spread)
        meta[4:5, :] = jnp.broadcast_to(short, (1, sets * 128))

    gap = out_ref.shape[2] - 3 * slots - 8
    for h in range(0, out_ref.shape[1], 2):
        at = slice(h * HEAD_DIM, (h + 2) * HEAD_DIM)
        y = dot(place[...], jnp.concatenate([q_ref[:, at], k_ref[:, at], v_ref[:, at]], axis=1))
        for s in range(sets):
            part = y[s * slots : (s + 1) * slots]
            for u in range(2):
                pieces = [part[:, i * 128 : (i + 1) * 128] for i in (u, u + 2, u + 4)]
                if gap:
                    pieces.append(jnp.zeros((gap, 128), F32))
                pieces.append(meta[0:8, s * 128 : (s + 1) * 128])
                out_ref[s, h + u] = jnp.concatenate(pieces, axis=0).astype(BF16)


def attend_kernel(slots, x_ref, o_ref, short_ref, flat, xs, os, code, high, low, tab_v, tab, sem):
    sources, rows, _ = x_ref.shape
    blocks = sources // 4
    total_rows = xs.shape[0]
    whole_counts, unroll = (FIXED, UNROLL) if slots == FEW else (FIXED_SHORT, 2)
    os[...] = jnp.zeros(os.shape, BF16)
    ahead = 5 * sources // 16
    xs[0 : ahead * BLK, :] = jnp.zeros((ahead * BLK, xs.shape[1]), BF16)
    flat[...] = x_ref[:, rows - 16 : rows, :].astype(F32)[:, 8:16].reshape(flat.shape)

    def fact(i):
        return flat[pl.ds(i, sources, 8), :]

    high[...] = fact(0) * 256.0
    low[...] = fact(1)
    own = fact(2)
    within = fact(3)
    short_ref[...] = jnp.broadcast_to(jnp.max(fact(4), axis=0, keepdims=True), (8, 128))
    lane = iota((sources, 128), 1)
    r = lax.broadcasted_iota(jnp.int32, (128, CL_SET * 128), 0)
    s = lax.broadcasted_iota(jnp.int32, (128, CL_SET * 128), 1)
    to_each = jnp.where(r == jnp.right_shift(s, 7), 1.0, 0.0).astype(BF16)
    is_own = [jnp.where(own == c + 1, 1.0, 0.0) for c in range(CL_SET)]
    counts = nt_dot(jnp.concatenate(is_own, axis=1).astype(BF16), to_each).astype(BF16)
    r = lax.broadcasted_iota(jnp.int32, (sources, sources), 0)
    s = lax.broadcasted_iota(jnp.int32, (sources, sources), 1)
    first = jnp.bitwise_and(r, -4)
    masks = [s >= 0, s < r, s < first, s < first + 4]
    sums = dot(jnp.concatenate([jnp.where(m, 1.0, 0.0) for m in masks], axis=0).astype(BF16), counts)
    total, before, before_block, after_block = (sums[i * sources : (i + 1) * sources] for i in range(4))
    nblk = jnp.floor((total + (BLK - 1)) * (1.0 / BLK))
    start_blk = dot(nblk.astype(BF16), jnp.where((r < s) & (r < CL_SET), 1.0, 0.0).astype(BF16))
    skipped = jnp.floor(before_block * (1.0 / 16)) * 16
    shift = dot((before - skipped).astype(BF16), to_each)
    place = within
    for c in range(CL_SET):
        place = place + is_own[c] * shift[:, c * 128 : (c + 1) * 128]
    step = jnp.floor(place * (1.0 / RUN) + (0.5 / RUN))
    code[...] = jnp.where(own > 0.0, step * CODES + (own - 1.0) * RUN + (place - step * RUN) + 1.0, 0.0)
    passes = jnp.where(lane < CL_SET, jnp.floor((after_block - skipped + (RUN - 1)) * (1.0 / RUN)), 0.0)
    most = jnp.max(passes, axis=(0, 1), keepdims=True)
    table = jnp.where(lane < 2 * CL_SET, pltpu.roll(passes, CL_SET, 1), most)
    flat[0:sources] = jnp.where(lane < CL_SET, start_blk * BLK + skipped, table)
    tab_v[0:blocks] = flat[pl.ds(0, blocks, 4), :].astype(jnp.int32)
    tab_v[blocks : blocks + 8] = start_blk[0:8].astype(jnp.int32)
    tab_v[blocks + 8 :] = nblk[0:8].astype(jnp.int32)
    copy = pltpu.make_async_copy(tab_v, tab, sem)
    copy.start()
    copy.wait()
    most_passes = tab[0, 2 * CL_SET]

    def begin_of(c):
        return tab[blocks, c]

    def count_of(c):
        return tab[blocks + 8, c]

    def passes_of(b):
        return functools.reduce(jnp.maximum, [tab[b, CL_SET + c] for c in range(CL_SET)])

    used_blocks = begin_of(CL_SET - 1) + count_of(CL_SET - 1)

    def clear(i, _):
        at = pl.ds(pl.multiple_of(i * BLK, BLK), BLK)
        xs[at, :] = jnp.zeros((BLK, xs.shape[1]), BF16)
        return 0

    lax.fori_loop(ahead, jnp.minimum(used_blocks + 4, total_rows // BLK), clear, 0)

    def joined(ref, b):
        return jnp.concatenate(
            [
                ref[pl.ds(4 * b, 1), :] + ref[pl.ds(4 * b + 1, 1), :],
                ref[pl.ds(4 * b + 2, 1), :] + ref[pl.ds(4 * b + 3, 1), :],
            ],
            axis=1,
        )

    code_rows = iota((CODES, 256), 0)
    which = lax.broadcasted_iota(jnp.int32, (128, 256), 0)

    def compact(b, p):
        x4 = x_ref[pl.ds(4 * b, 4)].astype(F32)
        xcat = jnp.concatenate([x4[:, i * slots : i * slots + 64].reshape(256, 128) for i in range(3)], axis=1).astype(BF16)
        row = joined(code, b) - jnp.asarray(p * CODES + 1, F32)
        where_at = jnp.where(which == 0, joined(high, b), jnp.where(which == 1, joined(low, b), 0.0))
        xcat = jnp.concatenate([xcat, jnp.transpose(where_at).astype(BF16)], axis=1)
        select = jnp.where(code_rows == row, 1.0, 0.0).astype(BF16)
        y = dot(select, xcat).astype(BF16)
        ats = [pl.ds(pl.multiple_of(tab[b, c] + p * RUN, 16), RUN) for c in range(CL_SET)]
        new = [xs[at, :] + y[c * RUN : (c + 1) * RUN] for c, at in enumerate(ats)]
        for at, x in zip(ats, new):
            xs[at, :] = x

    def each_block(body):
        def some(i, _):
            for u in range(unroll):
                body(i * unroll + u, 0)

            @pl.when(most_passes > 1)
            def _():
                def rest(u, _):
                    b = i * unroll + u

                    def more(p, _):
                        body(b, p)
                        return 0

                    return lax.fori_loop(1, passes_of(b), more, 0)

                lax.fori_loop(0, unroll, rest, 0)

            return 0

        lax.fori_loop(0, blocks // unroll, some, 0)

    each_block(compact)

    scale = HEAD_DIM ** (-0.5) * 1.4426950408889634
    to_lanes = jnp.where(lax.broadcasted_iota(jnp.int32, (16, 128), 1) < 2, 1.0, 0.0).astype(BF16)
    to_all = jnp.where(lax.broadcasted_iota(jnp.int32, (128, 128), 0) < 2, 1.0, 0.0).astype(BF16)

    def key_places(at):
        kp = nt_dot(to_lanes, xs[at, 384:512])[0:1]
        return jnp.where(kp > 0.0, kp, 1e9)

    def hidden(scores, kp, qp):
        lanes = scores.shape[1] // 128
        return jnp.where(kp <= jnp.concatenate([qp] * lanes, axis=1), scores * scale, HIDDEN)

    def fixed(pair, count):
        for c in pair:
            begin, own_count = begin_of(c), count_of(c)
            kat = pl.ds(pl.multiple_of(begin * BLK, BLK), count * BLK)
            keys = xs[kat, 128:256]
            values = xs[kat, 256:384]
            mine = lax.broadcasted_iota(jnp.int32, (1, count * BLK), 1) < own_count * BLK
            kp = jnp.where(mine, key_places(kat), 1e9)
            for i in range(0, count, TILE):
                wide = min(TILE, count - i)
                at = pl.ds(pl.multiple_of((begin + i) * BLK, BLK), wide * BLK)
                scores = hidden(nt_dot(xs[at, 0:128], keys), kp, dot(xs[at, 384:512], to_all))
                weight = jnp.exp2(scores - jnp.max(scores, axis=1, keepdims=True))
                total = jnp.sum(weight, axis=1, keepdims=True)
                os[at, :] = (dot(weight.astype(BF16), values) / total).astype(BF16)

    def general(begin, count):
        def queries(i, _):
            at = pl.ds(pl.multiple_of((begin + i) * BLK, BLK), BLK)
            q = xs[at, 0:128]
            qp = dot(xs[at, 384:512], to_all)

            def keys(j, carried):
                top, total, summed = carried
                kat = pl.ds(pl.multiple_of((begin + j) * BLK, BLK), BLK)
                scores = hidden(nt_dot(q, xs[kat, 128:256]), key_places(kat), qp)
                fresh = jnp.maximum(top, jnp.max(scores, axis=1, keepdims=True))
                weight = jnp.exp2(scores - fresh)
                rescale = jnp.exp2(top - fresh)
                total = total * rescale + jnp.sum(weight, axis=1, keepdims=True)
                summed = summed * rescale + dot(weight.astype(BF16), xs[kat, 256:384])
                return fresh, total, summed

            init = (jnp.full((BLK, 1), HIDDEN, F32), jnp.zeros((BLK, 1), F32), jnp.zeros((BLK, 128), F32))
            _, total, summed = lax.fori_loop(0, count, keys, init)
            os[at, :] = (summed / total).astype(BF16)
            return 0

        lax.fori_loop(0, count, queries, 0)

    def clusters(k, _):
        pair = [JOINT * k + u for u in range(JOINT)]
        counts = [count_of(c) for c in pair]
        most = functools.reduce(jnp.maximum, counts)
        least = functools.reduce(jnp.minimum, counts)
        done = jnp.bool_(False)
        smaller = whole_counts[0] - 2
        for n in whole_counts:
            alike = (most > smaller) & (most <= n) & (least >= n - 2)
            pl.when(alike)(functools.partial(fixed, pair, n))
            done = done | alike
            smaller = n

        @pl.when(jnp.logical_not(done))
        def _():
            for c, n in zip(pair, counts):
                general(begin_of(c), n)

        return 0

    lax.fori_loop(0, CL_SET // JOINT, clusters, 0)

    code_lanes = iota((256, CODES), 1)

    def spread(b, p):
        col = column(joined(code, b) - jnp.asarray(p * CODES + 1, F32))
        col = jnp.concatenate([col] * (CODES // 128), axis=1)
        cat = jnp.concatenate(
            [os[pl.ds(pl.multiple_of(tab[b, c] + p * RUN, 16), RUN), :] for c in range(CL_SET)], axis=0
        )
        select = jnp.where(code_lanes == col, 1.0, 0.0).astype(BF16)
        new = dot(select, cat).reshape(4, 64, 128)[:, :slots]
        at = pl.ds(4 * b, 4)
        if isinstance(p, int):
            o_ref[at] = new.astype(BF16)
        else:
            o_ref[at] = (o_ref[at].astype(F32) + new).astype(BF16)

    each_block(spread)


def attend_call(slots, got):
    sources = got.shape[0]
    whole = pl.BlockSpec(memory_space=pltpu.VMEM)
    total_rows = sources * slots + (CL_SET + 4) * BLK
    return pl.pallas_call(
        functools.partial(attend_kernel, slots),
        in_specs=[whole],
        out_specs=[whole, whole],
        out_shape=[
            pltpu.VMEM((sources, slots, 128), BF16),
            jax.ShapeDtypeStruct((8, 128), F32),
        ],
        scratch_shapes=[
            pltpu.VMEM((sources * 8, 128), F32),
            pltpu.VMEM((total_rows, 4 * HEAD_DIM), BF16),
            pltpu.VMEM((total_rows, HEAD_DIM), BF16),
            pltpu.VMEM((sources, 128), F32),
            pltpu.VMEM((sources, 128), F32),
            pltpu.VMEM((sources, 128), F32),
            pltpu.VMEM((sources // 4 + 16, 128), jnp.int32),
            pltpu.SMEM((sources // 4 + 16, 128), jnp.int32),
            pltpu.SemaphoreType.DMA,
        ],
        compiler_params=pltpu.CompilerParams(vmem_limit_bytes=32 * 2**20),
        name="attend",
    )(pltpu.with_memory_space_constraint(got, pltpu.VMEM))


def unpack_kernel(slots, slot_ref, r_ref, out_ref, select):
    sets, heads = r_ref.shape[0], r_ref.shape[1]

    @pl.when(pl.program_id(0) == 0)
    def _():
        col = column(slot_ref[...])
        col = jnp.concatenate([col] * (-(-sets * slots // 128)), axis=1)[:, : sets * slots]
        select[...] = jnp.where(iota(select.shape, 1) == col, 1.0, 0.0).astype(BF16)

    for h in range(heads):
        x = r_ref[:, h].astype(F32).reshape(sets * slots, 128).astype(BF16)
        out_ref[:, h * 128 : (h + 1) * 128] = dot(select[...], x).astype(BF16)


def pack_call(slots, sets, parity, cid_row, pos_row, queries, keys, values):
    tokens, width = queries.shape
    heads = width // HEAD_DIM
    rows = chunk_rows(slots)
    some = pl.BlockSpec((tokens, PACK * HEAD_DIM), lambda h: (0, h))
    line = pl.BlockSpec((1, tokens), lambda h: (0, 0))
    return pl.pallas_call(
        functools.partial(pack_kernel, slots, sets),
        grid=(heads // PACK,),
        in_specs=[pl.BlockSpec(memory_space=pltpu.SMEM), line, line, some, some, some],
        out_specs=[pl.BlockSpec((sets, PACK, rows, 128), lambda h: (0, h, 0, 0)), line],
        out_shape=[
            jax.ShapeDtypeStruct((sets, heads, rows, 128), BF16),
            jax.ShapeDtypeStruct((1, tokens), F32),
        ],
        scratch_shapes=[pltpu.VMEM((sets * slots, tokens), BF16), pltpu.VMEM((16, sets * 128), F32)],
        compiler_params=pltpu.CompilerParams(vmem_limit_bytes=20 * 2**20),
        name="pack",
    )(parity, cid_row, pos_row, queries, keys, values)


def unpack_call(slots, slot, back):
    sets, heads = back.shape[:2]
    tokens = slot.shape[1]
    return pl.pallas_call(
        functools.partial(unpack_kernel, slots),
        grid=(heads // UNPACK,),
        in_specs=[
            pl.BlockSpec((1, tokens), lambda h: (0, 0)),
            pl.BlockSpec((sets, UNPACK, slots, 128), lambda h: (0, h, 0, 0)),
        ],
        out_specs=pl.BlockSpec((tokens, UNPACK * HEAD_DIM), lambda h: (0, h)),
        out_shape=jax.ShapeDtypeStruct((tokens, heads * HEAD_DIM), BF16),
        scratch_shapes=[pltpu.VMEM((tokens, sets * slots), BF16)],
        compiler_params=pltpu.CompilerParams(vmem_limit_bytes=16 * 2**20),
        name="unpack",
    )(slot, back)


def attention(slots, queries, keys, values, cid_row, pos_row, parity, fallback=None):
    heads = queries.shape[1] // HEAD_DIM
    sources = lax.axis_size("grp") * lax.axis_size("blk")
    sets = sources // heads
    sent, slot = pack_call(slots, sets, parity, cid_row, pos_row, queries, keys, values)
    got = lax.all_to_all(
        sent.reshape(sources, sent.shape[2], 128), ("grp", "blk"), split_axis=0, concat_axis=0, tiled=True
    )
    done, short = attend_call(slots, got)
    back = lax.all_to_all(done, ("grp", "blk"), split_axis=0, concat_axis=0, tiled=True)
    back = back.reshape(sets, heads, slots, 128)
    if fallback is None:
        return unpack_call(slots, slot, back)
    return lax.cond(short[0, 0] > 0.0, fallback, lambda: unpack_call(slots, slot, back))


def local(queries, keys, values, cluster_ids, positions):
    cid_row = cluster_ids.reshape(1, -1)
    pos_row = positions.reshape(1, -1)
    me = lax.axis_index("grp") * lax.axis_size("blk") + lax.axis_index("blk")
    parity = (me % 2).astype(jnp.int32).reshape(1, 1)
    args = (queries, keys, values, cid_row, pos_row, parity)
    return attention(FEW, *args, fallback=lambda: attention(ALL, *args))


def solution(mesh):
    placed = (
        P(("grp", "blk"), None),
        P(("grp", "blk"), None),
        P(("grp", "blk"), None),
        P(("grp", "blk")),
        P(("grp", "blk")),
    )
    return jax.shard_map(
        local, mesh=mesh, in_specs=placed, out_specs=P(("grp", "blk"), None), check_vma=False
    )
```

```python
import functools

import jax
import jax.numpy as jnp
from jax import lax
from jax.experimental import pallas as pl
from jax.experimental.pallas import tpu as pltpu
from jax.sharding import PartitionSpec as P

HEAD_DIM = 128
CL_GRP = 4
CL_SET = 2 * CL_GRP
RUN = 48
CODES = CL_SET * RUN
BLK = 128
FIXED = (4, 5, 6, 7)
FIXED_SHORT = (6,)
UNROLL = 32
TILE = 3
JOINT = 2
ALL = 64
FEW = 56
PACK = 8
UNPACK = 8
F32 = jnp.float32
BF16 = jnp.bfloat16
HIDDEN = -1e30


def chunk_rows(slots):
    return -(-(3 * slots + 8) // 16) * 16


def iota(shape, dim):
    return lax.broadcasted_iota(jnp.int32, shape, dim).astype(F32)


def column(row):
    return jnp.transpose(jnp.broadcast_to(row, (128, row.shape[1])))


def nt_dot(a, b):
    return lax.dot_general(a, b, (((1,), (1,)), ((), ())), preferred_element_type=F32)


def dot(a, b):
    return jnp.dot(a, b, preferred_element_type=F32)


def pack_kernel(slots, sets, parity_ref, cid_ref, pos_ref, q_ref, k_ref, v_ref, out_ref, slot_ref, place, meta):
    tokens = cid_ref.shape[1]

    @pl.when(pl.program_id(0) == 0)
    def _():
        cid = cid_ref[...]
        pos = pos_ref[...]
        own = jnp.bitwise_and(cid, CL_SET - 1)
        group = (cid - own).astype(F32) * (1.0 / CL_SET)
        key = cid.astype(F32) * tokens + iota((1, tokens), 1)
        keys = column(key)
        keys = jnp.concatenate([keys] * (tokens // 128), axis=1)
        below = keys < key
        rank = jnp.sum(jnp.where(below & (keys >= group * (CL_SET * tokens)), 1.0, 0.0), axis=0, keepdims=True)
        within = jnp.sum(jnp.where(below & (keys >= cid.astype(F32) * tokens), 1.0, 0.0), axis=0, keepdims=True)
        fits = rank < slots
        slot = jnp.where(fits, group * slots + rank, -1.0)
        slot_ref[...] = slot
        place[...] = jnp.where(iota((sets * slots, tokens), 0) == slot, 1.0, 0.0).astype(BF16)
        lane = jnp.where(fits, group * 128 + rank + 64 * parity_ref[0, 0].astype(F32), -1.0)
        spread = jnp.where(iota((sets * 128, tokens), 0) == lane, 1.0, 0.0).astype(BF16)
        short = jnp.where(jnp.max(rank, axis=1, keepdims=True) >= slots, 1.0, 0.0)
        low = jnp.bitwise_and(pos, 255)
        high = jnp.right_shift(pos, 8) + 1
        row = lax.broadcasted_iota(jnp.int32, (16, tokens), 0)
        facts = jnp.where(
            row == 0,
            high.astype(F32),
            jnp.where(row == 1, low.astype(F32), jnp.where(row == 2, own.astype(F32) + 1.0, jnp.where(row == 3, within, 0.0))),
        ).astype(BF16)
        meta[...] = nt_dot(facts, spread)
        meta[4:5, :] = jnp.broadcast_to(short, (1, sets * 128))

    gap = out_ref.shape[2] - 3 * slots - 8
    for h in range(0, out_ref.shape[1], 2):
        at = slice(h * HEAD_DIM, (h + 2) * HEAD_DIM)
        y = dot(place[...], jnp.concatenate([q_ref[:, at], k_ref[:, at], v_ref[:, at]], axis=1))
        for s in range(sets):
            part = y[s * slots : (s + 1) * slots]
            for u in range(2):
                pieces = [part[:, i * 128 : (i + 1) * 128] for i in (u, u + 2, u + 4)]
                if gap:
                    pieces.append(jnp.zeros((gap, 128), F32))
                pieces.append(meta[0:8, s * 128 : (s + 1) * 128])
                out_ref[s, h + u] = jnp.concatenate(pieces, axis=0).astype(BF16)


def attend_kernel(slots, x_ref, o_ref, short_ref, flat, xs, os, code, high, low, tab_v, tab, sem):
    sources, rows, _ = x_ref.shape
    blocks = sources // 4
    total_rows = xs.shape[0]
    whole_counts, unroll = (FIXED, UNROLL) if slots == FEW else (FIXED_SHORT, 2)
    os[...] = jnp.zeros(os.shape, BF16)
    ahead = 5 * sources // 16
    xs[0 : ahead * BLK, :] = jnp.zeros((ahead * BLK, xs.shape[1]), BF16)
    flat[...] = x_ref[:, rows - 16 : rows, :].astype(F32)[:, 8:16].reshape(flat.shape)

    def fact(i):
        return flat[pl.ds(i, sources, 8), :]

    high[...] = fact(0) * 256.0
    low[...] = fact(1)
    own = fact(2)
    within = fact(3)
    short_ref[...] = jnp.broadcast_to(jnp.max(fact(4), axis=0, keepdims=True), (8, 128))
    lane = iota((sources, 128), 1)
    r = lax.broadcasted_iota(jnp.int32, (128, CL_SET * 128), 0)
    s = lax.broadcasted_iota(jnp.int32, (128, CL_SET * 128), 1)
    to_each = jnp.where(r == jnp.right_shift(s, 7), 1.0, 0.0).astype(BF16)
    is_own = [jnp.where(own == c + 1, 1.0, 0.0) for c in range(CL_SET)]
    counts = nt_dot(jnp.concatenate(is_own, axis=1).astype(BF16), to_each).astype(BF16)
    r = lax.broadcasted_iota(jnp.int32, (sources, sources), 0)
    s = lax.broadcasted_iota(jnp.int32, (sources, sources), 1)
    first = jnp.bitwise_and(r, -4)
    masks = [s >= 0, s < r, s < first, s < first + 4]
    sums = dot(jnp.concatenate([jnp.where(m, 1.0, 0.0) for m in masks], axis=0).astype(BF16), counts)
    total, before, before_block, after_block = (sums[i * sources : (i + 1) * sources] for i in range(4))
    nblk = jnp.floor((total + (BLK - 1)) * (1.0 / BLK))
    start_blk = dot(nblk.astype(BF16), jnp.where((r < s) & (r < CL_SET), 1.0, 0.0).astype(BF16))
    skipped = jnp.floor(before_block * (1.0 / 16)) * 16
    shift = dot((before - skipped).astype(BF16), to_each)
    place = within
    for c in range(CL_SET):
        place = place + is_own[c] * shift[:, c * 128 : (c + 1) * 128]
    step = jnp.floor(place * (1.0 / RUN) + (0.5 / RUN))
    code[...] = jnp.where(own > 0.0, step * CODES + (own - 1.0) * RUN + (place - step * RUN) + 1.0, 0.0)
    passes = jnp.where(lane < CL_SET, jnp.floor((after_block - skipped + (RUN - 1)) * (1.0 / RUN)), 0.0)
    most = jnp.max(passes, axis=(0, 1), keepdims=True)
    table = jnp.where(lane < 2 * CL_SET, pltpu.roll(passes, CL_SET, 1), most)
    flat[0:sources] = jnp.where(lane < CL_SET, start_blk * BLK + skipped, table)
    tab_v[0:blocks] = flat[pl.ds(0, blocks, 4), :].astype(jnp.int32)
    tab_v[blocks : blocks + 8] = start_blk[0:8].astype(jnp.int32)
    tab_v[blocks + 8 :] = nblk[0:8].astype(jnp.int32)
    copy = pltpu.make_async_copy(tab_v, tab, sem)
    copy.start()
    copy.wait()
    most_passes = tab[0, 2 * CL_SET]

    def begin_of(c):
        return tab[blocks, c]

    def count_of(c):
        return tab[blocks + 8, c]

    def passes_of(b):
        return functools.reduce(jnp.maximum, [tab[b, CL_SET + c] for c in range(CL_SET)])

    used_blocks = begin_of(CL_SET - 1) + count_of(CL_SET - 1)

    def clear(i, _):
        at = pl.ds(pl.multiple_of(i * BLK, BLK), BLK)
        xs[at, :] = jnp.zeros((BLK, xs.shape[1]), BF16)
        return 0

    lax.fori_loop(ahead, jnp.minimum(used_blocks + 4, total_rows // BLK), clear, 0)

    def joined(ref, b):
        return jnp.concatenate(
            [
                ref[pl.ds(4 * b, 1), :] + ref[pl.ds(4 * b + 1, 1), :],
                ref[pl.ds(4 * b + 2, 1), :] + ref[pl.ds(4 * b + 3, 1), :],
            ],
            axis=1,
        )

    code_rows = iota((CODES, 256), 0)
    which = lax.broadcasted_iota(jnp.int32, (128, 256), 0)

    def compact(b, p):
        x4 = x_ref[pl.ds(4 * b, 4)].astype(F32)
        xcat = jnp.concatenate([x4[:, i * slots : i * slots + 64].reshape(256, 128) for i in range(3)], axis=1).astype(BF16)
        row = joined(code, b) - jnp.asarray(p * CODES + 1, F32)
        where_at = jnp.where(which == 0, joined(high, b), jnp.where(which == 1, joined(low, b), 0.0))
        xcat = jnp.concatenate([xcat, jnp.transpose(where_at).astype(BF16)], axis=1)
        select = jnp.where(code_rows == row, 1.0, 0.0).astype(BF16)
        y = dot(select, xcat).astype(BF16)
        ats = [pl.ds(pl.multiple_of(tab[b, c] + p * RUN, 16), RUN) for c in range(CL_SET)]
        new = [xs[at, :] + y[c * RUN : (c + 1) * RUN] for c, at in enumerate(ats)]
        for at, x in zip(ats, new):
            xs[at, :] = x

    def each_block(body):
        def some(i, _):
            for u in range(unroll):
                body(i * unroll + u, 0)

            @pl.when(most_passes > 1)
            def _():
                def rest(u, _):
                    b = i * unroll + u

                    def more(p, _):
                        body(b, p)
                        return 0

                    return lax.fori_loop(1, passes_of(b), more, 0)

                lax.fori_loop(0, unroll, rest, 0)

            return 0

        lax.fori_loop(0, blocks // unroll, some, 0)

    each_block(compact)

    scale = HEAD_DIM ** (-0.5) * 1.4426950408889634
    to_lanes = jnp.where(lax.broadcasted_iota(jnp.int32, (16, 128), 1) < 2, 1.0, 0.0).astype(BF16)
    to_all = jnp.where(lax.broadcasted_iota(jnp.int32, (128, 128), 0) < 2, 1.0, 0.0).astype(BF16)

    def key_places(at):
        kp = nt_dot(to_lanes, xs[at, 384:512])[0:1]
        return jnp.where(kp > 0.0, kp, 1e9)

    def hidden(scores, kp, qp):
        lanes = scores.shape[1] // 128
        return jnp.where(kp <= jnp.concatenate([qp] * lanes, axis=1), scores * scale, HIDDEN)

    def fixed(pair, count):
        for c in pair:
            begin, own_count = begin_of(c), count_of(c)
            kat = pl.ds(pl.multiple_of(begin * BLK, BLK), count * BLK)
            keys = xs[kat, 128:256]
            values = xs[kat, 256:384]
            mine = lax.broadcasted_iota(jnp.int32, (1, count * BLK), 1) < own_count * BLK
            kp = jnp.where(mine, key_places(kat), 1e9)
            for i in range(0, count, TILE):
                wide = min(TILE, count - i)
                at = pl.ds(pl.multiple_of((begin + i) * BLK, BLK), wide * BLK)
                scores = hidden(nt_dot(xs[at, 0:128], keys), kp, dot(xs[at, 384:512], to_all))
                weight = jnp.exp2(scores - jnp.max(scores, axis=1, keepdims=True))
                total = jnp.sum(weight, axis=1, keepdims=True)
                os[at, :] = (dot(weight.astype(BF16), values) / total).astype(BF16)

    def general(begin, count):
        def queries(i, _):
            at = pl.ds(pl.multiple_of((begin + i) * BLK, BLK), BLK)
            q = xs[at, 0:128]
            qp = dot(xs[at, 384:512], to_all)

            def keys(j, carried):
                top, total, summed = carried
                kat = pl.ds(pl.multiple_of((begin + j) * BLK, BLK), BLK)
                scores = hidden(nt_dot(q, xs[kat, 128:256]), key_places(kat), qp)
                fresh = jnp.maximum(top, jnp.max(scores, axis=1, keepdims=True))
                weight = jnp.exp2(scores - fresh)
                rescale = jnp.exp2(top - fresh)
                total = total * rescale + jnp.sum(weight, axis=1, keepdims=True)
                summed = summed * rescale + dot(weight.astype(BF16), xs[kat, 256:384])
                return fresh, total, summed

            init = (jnp.full((BLK, 1), HIDDEN, F32), jnp.zeros((BLK, 1), F32), jnp.zeros((BLK, 128), F32))
            _, total, summed = lax.fori_loop(0, count, keys, init)
            os[at, :] = (summed / total).astype(BF16)
            return 0

        lax.fori_loop(0, count, queries, 0)

    def clusters(k, _):
        pair = [JOINT * k + u for u in range(JOINT)]
        counts = [count_of(c) for c in pair]
        most = functools.reduce(jnp.maximum, counts)
        least = functools.reduce(jnp.minimum, counts)
        done = jnp.bool_(False)
        smaller = whole_counts[0] - 2
        for n in whole_counts:
            alike = (most > smaller) & (most <= n) & (least >= n - 2)
            pl.when(alike)(functools.partial(fixed, pair, n))
            done = done | alike
            smaller = n

        @pl.when(jnp.logical_not(done))
        def _():
            for c, n in zip(pair, counts):
                general(begin_of(c), n)

        return 0

    lax.fori_loop(0, CL_SET // JOINT, clusters, 0)

    code_lanes = iota((256, CODES), 1)

    def spread(b, p):
        col = column(joined(code, b) - jnp.asarray(p * CODES + 1, F32))
        col = jnp.concatenate([col] * (CODES // 128), axis=1)
        cat = jnp.concatenate(
            [os[pl.ds(pl.multiple_of(tab[b, c] + p * RUN, 16), RUN), :] for c in range(CL_SET)], axis=0
        )
        select = jnp.where(code_lanes == col, 1.0, 0.0).astype(BF16)
        new = dot(select, cat).reshape(4, 64, 128)[:, :slots]
        at = pl.ds(4 * b, 4)
        if isinstance(p, int):
            o_ref[at] = new.astype(BF16)
        else:
            o_ref[at] = (o_ref[at].astype(F32) + new).astype(BF16)

    each_block(spread)


def attend_call(slots, got):
    sources = got.shape[0]
    whole = pl.BlockSpec(memory_space=pltpu.VMEM)
    total_rows = sources * slots + (CL_SET + 4) * BLK
    return pl.pallas_call(
        functools.partial(attend_kernel, slots),
        in_specs=[whole],
        out_specs=[whole, whole],
        out_shape=[
            pltpu.VMEM((sources, slots, 128), BF16),
            jax.ShapeDtypeStruct((8, 128), F32),
        ],
        scratch_shapes=[
            pltpu.VMEM((sources * 8, 128), F32),
            pltpu.VMEM((total_rows, 4 * HEAD_DIM), BF16),
            pltpu.VMEM((total_rows, HEAD_DIM), BF16),
            pltpu.VMEM((sources, 128), F32),
            pltpu.VMEM((sources, 128), F32),
            pltpu.VMEM((sources, 128), F32),
            pltpu.VMEM((sources // 4 + 16, 128), jnp.int32),
            pltpu.SMEM((sources // 4 + 16, 128), jnp.int32),
            pltpu.SemaphoreType.DMA,
        ],
        compiler_params=pltpu.CompilerParams(vmem_limit_bytes=32 * 2**20),
        name="attend",
    )(pltpu.with_memory_space_constraint(got, pltpu.VMEM))


def unpack_kernel(slots, slot_ref, r_ref, out_ref, select):
    sets, heads = r_ref.shape[0], r_ref.shape[1]

    @pl.when(pl.program_id(0) == 0)
    def _():
        col = column(slot_ref[...])
        col = jnp.concatenate([col] * (-(-sets * slots // 128)), axis=1)[:, : sets * slots]
        select[...] = jnp.where(iota(select.shape, 1) == col, 1.0, 0.0).astype(BF16)

    for h in range(heads):
        x = r_ref[:, h].astype(F32).reshape(sets * slots, 128).astype(BF16)
        out_ref[:, h * 128 : (h + 1) * 128] = dot(select[...], x).astype(BF16)


def pack_call(slots, sets, parity, cid_row, pos_row, queries, keys, values):
    tokens, width = queries.shape
    heads = width // HEAD_DIM
    rows = chunk_rows(slots)
    some = pl.BlockSpec((tokens, PACK * HEAD_DIM), lambda h: (0, h))
    line = pl.BlockSpec((1, tokens), lambda h: (0, 0))
    return pl.pallas_call(
        functools.partial(pack_kernel, slots, sets),
        grid=(heads // PACK,),
        in_specs=[pl.BlockSpec(memory_space=pltpu.SMEM), line, line, some, some, some],
        out_specs=[pl.BlockSpec((sets, PACK, rows, 128), lambda h: (0, h, 0, 0)), line],
        out_shape=[
            jax.ShapeDtypeStruct((sets, heads, rows, 128), BF16),
            jax.ShapeDtypeStruct((1, tokens), F32),
        ],
        scratch_shapes=[pltpu.VMEM((sets * slots, tokens), BF16), pltpu.VMEM((16, sets * 128), F32)],
        compiler_params=pltpu.CompilerParams(vmem_limit_bytes=20 * 2**20),
        name="pack",
    )(parity, cid_row, pos_row, queries, keys, values)


def unpack_call(slots, slot, back):
    sets, heads = back.shape[:2]
    tokens = slot.shape[1]
    return pl.pallas_call(
        functools.partial(unpack_kernel, slots),
        grid=(heads // UNPACK,),
        in_specs=[
            pl.BlockSpec((1, tokens), lambda h: (0, 0)),
            pl.BlockSpec((sets, UNPACK, slots, 128), lambda h: (0, h, 0, 0)),
        ],
        out_specs=pl.BlockSpec((tokens, UNPACK * HEAD_DIM), lambda h: (0, h)),
        out_shape=pltpu.HBM((tokens, heads * HEAD_DIM), BF16),
        scratch_shapes=[pltpu.VMEM((tokens, sets * slots), BF16)],
        compiler_params=pltpu.CompilerParams(vmem_limit_bytes=16 * 2**20),
        name="unpack",
    )(slot, back)


def attention(slots, queries, keys, values, cid_row, pos_row, parity, fallback=None):
    heads = queries.shape[1] // HEAD_DIM
    sources = lax.axis_size("grp") * lax.axis_size("blk")
    sets = sources // heads
    sent, slot = pack_call(slots, sets, parity, cid_row, pos_row, queries, keys, values)
    got = lax.all_to_all(
        sent.reshape(sources, sent.shape[2], 128), ("grp", "blk"), split_axis=0, concat_axis=0, tiled=True
    )
    done, short = attend_call(slots, got)
    back = lax.all_to_all(done, ("grp", "blk"), split_axis=0, concat_axis=0, tiled=True)
    back = back.reshape(sets, heads, slots, 128)
    if fallback is None:
        return unpack_call(slots, slot, back)
    return lax.cond(short[0, 0] > 0.0, fallback, lambda: unpack_call(slots, slot, back))


def local(queries, keys, values, cluster_ids, positions):
    cid_row = cluster_ids.reshape(1, -1)
    pos_row = positions.reshape(1, -1)
    me = lax.axis_index("grp") * lax.axis_size("blk") + lax.axis_index("blk")
    parity = (me % 2).astype(jnp.int32).reshape(1, 1)
    args = (queries, keys, values, cid_row, pos_row, parity)
    return attention(FEW, *args, fallback=lambda: attention(ALL, *args))


def solution(mesh):
    placed = (
        P(("grp", "blk"), None),
        P(("grp", "blk"), None),
        P(("grp", "blk"), None),
        P(("grp", "blk")),
        P(("grp", "blk")),
    )
    return jax.shard_map(
        local, mesh=mesh, in_specs=placed, out_specs=P(("grp", "blk"), None), check_vma=False
    )
```
